32 devices in a mesh: dp: 8 (over y, x, core), head: 4 (over z).
Axes of the slice: x: 2, y: 2, z: 4, core: 2. Of those that a mesh axis runs over, the one named last changes fastest.
Arguments:
- text_in: bfloat16 [4096, 768], P('dp'), may hold values from -6 to 6
- visual_in: bfloat16 [4096, 768], P('dp'), may hold values from -80 to 80
- visual_count: int32 [8], P('dp'), may hold values from 256 to 512, as said below
- line_index: int32 [2, 4096], P(None, 'dp'), may hold values from 0 to 47
- box_index: int32 [2, 2, 4096], P(None, None, 'dp'), may hold values from 0 to 31
- qkv_weight: bfloat16 [768, 3, 1536], P(None, None, 'head'), may hold values from -0.21875 to 0.21875
- bias_table: float32 [24, 64], P('head'), may hold values from -5 to 5
- out_weight: bfloat16 [1536, 768], replicated, may hold values from -0.75 to 0.75
- out_bias: float32 [768], replicated, may hold values from -3 to 3
- norm1_gain: float32 [768], replicated, may hold values from 0.25 to 1.75
- norm1_shift: float32 [768], replicated, may hold values from -3 to 3
- ffn_weight_in: bfloat16 [768, 3072], replicated, may hold values from -0.21875 to 0.21875
- ffn_bias_in: float32 [3072], replicated, may hold values from -3 to 3
- ffn_weight_out: bfloat16 [3072, 768], replicated, may hold values from -0.109375 to 0.109375
- ffn_bias_out: float32 [768], replicated, may hold values from -3 to 3
- norm2_gain: float32 [768], replicated, may hold values from 0.25 to 1.75
- norm2_shift: float32 [768], replicated, may hold values from -3 to 3
- batch_gain: float32 [768], replicated, may hold values from 0.25 to 1.75
- batch_shift: float32 [768], replicated, may hold values from -3 to 3
- cotangent: bfloat16 [4096, 768], P('dp'), may hold values from -6 to 6
Outputs:
- layer_out: bfloat16 [4096, 768], P('dp')
- grad_text: float32 [4096, 768], P(('dp', 'head'))
- grad_visual: float32 [4096, 768], P(('dp', 'head'))
- grad_qkv: float32 [768, 3, 1536], P('dp', None, 'head')
- grad_bias_table: float32 [24, 64], P('head', 'dp')
- grad_out_weight: float32 [1536, 768], P('head', 'dp')
- grad_out_bias: float32 [768], P(('dp', 'head'))
- grad_norm1_gain: float32 [768], P(('dp', 'head'))
- grad_norm1_shift: float32 [768], P(('dp', 'head'))
- grad_ffn_in: float32 [768, 3072], P(('dp', 'head'))
- grad_ffn_bias_in: float32 [3072], P(('dp', 'head'))
- grad_ffn_out: float32 [3072, 768], P(('dp', 'head'))
- grad_ffn_bias_out: float32 [768], P(('dp', 'head'))
- grad_norm2_gain: float32 [768], P(('dp', 'head'))
- grad_norm2_shift: float32 [768], P(('dp', 'head'))
- batch_gain_gradient: float32 [768], replicated
- batch_shift_gradient: float32 [768], replicated
The draws below stay inside these ranges and needn't reach their ends.
Inputs may be any that keep to these rules, and one draw needn't show every extreme that they name: `visual_count`: each page holds half of 512 or 512 visual tokens; both occur in every draw.
All inputs are finite; a program needn't handle non-finite values.
Results may differ from the reference program's by a relative error of at most 0.018.
The reference program's roundings to bfloat16 on the way count: a program that leaves them out, or rounds other values in their place, can miss the bound.
Values may be sent and summed in bfloat16 or wider, within the bound.
No kernel may reach another device: no remote copies, remote signals or barrier semaphores. Data moves between devices by JAX's collectives and lax.ppermute only.
A program may use at most 128 MiB of HBM per device.

```python
import math
from functools import partial
import jax
import jax.numpy as jnp
from jax import lax

D = 768
H = 12
HD = 64
FF = 3072
PAGE_LEN = 512
NB_REL = 32
NB_BOX = 16
LINES = 48
BOXES = 32
PAGES = 8
TOKENS = 4096
TABW = 64


def draw_visual_count(key, part):
    picks = jax.random.randint(jax.random.fold_in(key, 7), (PAGES,), 0, 2)
    counts = PAGE_LEN // 2 * (1 + picks)
    counts = counts.at[0].set(PAGE_LEN).at[1].set(PAGE_LEN // 2)
    return counts.astype(jnp.int32)


def draw_visual_in(key, part):
    subkeys = jax.random.split(jax.random.fold_in(key, 13), 4)
    position = jnp.arange(TOKENS, dtype=jnp.float32) / TOKENS
    growth = jnp.exp(position * math.log(3.0)) * jnp.exp(jax.random.uniform(subkeys[0], (TOKENS,)) * math.log(2.0))
    channel_scale = 0.3 * jnp.exp(jax.random.uniform(subkeys[1], (D,)) * math.log(10.0))
    channel_offset = jax.random.uniform(subkeys[2], (D,), minval=-1.0, maxval=1.0)
    sample = jnp.clip(jax.random.normal(subkeys[3], (TOKENS, D)), -4.0, 4.0)
    values = channel_offset[None, :] + channel_scale[None, :] * growth[:, None] * sample
    return values.astype(jnp.float32).astype(jnp.bfloat16)


def place_ends(values, rng, smallest, high):
    longest = values.shape.index(max(values.shape))
    spots = []
    for shift in (0, 1):
        where = [jax.random.randint(jax.random.fold_in(rng, axis), (), 0, length) for axis, length in enumerate(values.shape)]
        where[longest] = (where[longest] + shift) % values.shape[longest]
        spots.append(tuple(where))
    return values.at[spots[0]].set(smallest).at[spots[1]].set(high)


def shard_levels(key, dims, cuts, low, high):
    factor_of, own = 1.0, jax.random.fold_in(key, 6)
    for dim, parts in cuts:
        draws = jnp.exp(jax.random.uniform(jax.random.fold_in(own, dim), (parts,), jnp.float32, low / len(cuts), high / len(cuts)))
        factor_of = factor_of * jnp.repeat(draws, dims[dim] // parts).reshape([-1 if axis == dim else 1 for axis in range(len(dims))])
    return factor_of


def gaussian(rng, dims, spread, bound, pieces=(), kind=jnp.bfloat16):
    values = spread * jax.random.normal(rng, dims, jnp.float32)
    if pieces:
        values = values * shard_levels(rng, dims, pieces, -0.22, 0.18)
    return jnp.clip(values, -bound, bound).astype(kind)


def setup_inputs(seed: int = 0) -> dict:
    arg_keys = jax.random.split(jax.random.key(seed), 21)
    return {
        "text_in": gaussian(arg_keys[0], (TOKENS, D), 1.0, 6.0, ((0, 8),)),
        "visual_in": draw_visual_in(jax.random.fold_in(arg_keys[20], 71), 0),
        "visual_count": draw_visual_count(jax.random.fold_in(arg_keys[20], 71), 0),
        "line_index": place_ends(jax.random.randint(arg_keys[3], (2, TOKENS), 0, LINES), jax.random.fold_in(arg_keys[3], 1), 0, LINES - 1).astype(jnp.int32),
        "box_index": place_ends(jax.random.randint(arg_keys[4], (2, 2, TOKENS), 0, BOXES), jax.random.fold_in(arg_keys[4], 1), 0, BOXES - 1).astype(jnp.int32),
        "qkv_weight": gaussian(arg_keys[5], (D, 3, 2 * H * HD), D ** -0.5, 0.21875, ((2, 4),)),
        "bias_table": gaussian(arg_keys[6], (2 * H, TABW), 1.0, 5.0, ((0, 4),), jnp.float32),
        "out_weight": gaussian(arg_keys[7], (2 * H * HD, D), HD ** -0.5, 0.75),
        "out_bias": gaussian(arg_keys[8], (D,), 0.5, 3.0, (), jnp.float32),
        "norm1_gain": jnp.clip(1.0 + 0.15 * jax.random.normal(arg_keys[9], (D,), jnp.float32), 0.25, 1.75),
        "norm1_shift": gaussian(arg_keys[10], (D,), 0.5, 3.0, (), jnp.float32),
        "ffn_weight_in": gaussian(arg_keys[11], (D, FF), D ** -0.5, 0.21875),
        "ffn_bias_in": gaussian(arg_keys[12], (FF,), 0.5, 3.0, (), jnp.float32),
        "ffn_weight_out": gaussian(arg_keys[13], (FF, D), FF ** -0.5, 0.109375),
        "ffn_bias_out": gaussian(arg_keys[14], (D,), 0.5, 3.0, (), jnp.float32),
        "norm2_gain": jnp.clip(1.0 + 0.15 * jax.random.normal(arg_keys[15], (D,), jnp.float32), 0.25, 1.75),
        "norm2_shift": gaussian(arg_keys[16], (D,), 0.5, 3.0, (), jnp.float32),
        "batch_gain": jnp.clip(1.0 + 0.15 * jax.random.normal(arg_keys[17], (D,), jnp.float32), 0.25, 1.75),
        "batch_shift": gaussian(arg_keys[18], (D,), 0.5, 3.0, (), jnp.float32),
        "cotangent": gaussian(arg_keys[19], (TOKENS, D), 1.0, 6.0, ((0, 8),)),
    }


EPSILON = 1e-05
FLOOR_SCORE = -1000000000.0
HIGHEST = lax.Precision.HIGHEST

@jax.custom_vjp
def low(v):
    return lax.optimization_barrier(v.astype(jnp.bfloat16)).astype(jnp.float32)

@jax.custom_vjp
def low_back(v):
    return v

def low_keep(v):
    return (low(v), None)

def low_pass(kept, grad):
    return (grad,)

def back_keep(v):
    return (v, None)

def back_low(kept, grad):
    return (low(grad),)
low.defvjp(low_keep, low_pass)
low_back.defvjp(back_keep, back_low)

def layer_norm(hidden, gain, shift):
    average = lax.optimization_barrier(jnp.mean(hidden, axis=-1, keepdims=True))
    centered_values = hidden - average
    variance = lax.optimization_barrier(jnp.mean(centered_values * centered_values, axis=-1, keepdims=True))
    return centered_values * lax.rsqrt(variance + EPSILON) * gain + shift

def bucket_index(line_row, box_rows):
    rel_half = NB_REL // 2
    box_half = NB_BOX // 2
    relative = jnp.clip(line_row[None, :] - line_row[:, None], -rel_half, rel_half - 1) + rel_half
    across = jnp.clip(box_rows[0][None, :] - box_rows[0][:, None], -box_half, box_half - 1) + box_half + NB_REL
    downward = jnp.clip(box_rows[1][None, :] - box_rows[1][:, None], -box_half, box_half - 1) + box_half + NB_REL + NB_BOX
    return (relative.astype(jnp.int32), across.astype(jnp.int32), downward.astype(jnp.int32))

def page_heads(table, inputs):
    qkv_page, line_page, box_page, count = inputs
    position = jnp.arange(PAGE_LEN, dtype=jnp.int32)
    biases = []
    for stream in range(2):
        relative, across, downward = bucket_index(line_page[stream], box_page[stream])
        rows_tab = table[stream * H:(stream + 1) * H]
        biases.append(rows_tab[:, relative] + rows_tab[:, across] + rows_tab[:, downward])
    bias = jnp.concatenate(biases, axis=0)
    scores = jnp.einsum('ihd,jhd->hij', qkv_page[:, 0], qkv_page[:, 1], precision=HIGHEST) * HD ** (-0.5) + bias
    scores = low_back(scores)
    visual_head = jnp.arange(2 * H, dtype=jnp.int32) >= H
    allowed = jnp.logical_or(jnp.logical_not(visual_head)[:, None], position[None, :] < count)
    scores = jnp.where(allowed[:, None, :], scores, FLOOR_SCORE)
    prob = jax.nn.softmax(scores, axis=-1)
    heads = jnp.einsum('hij,jhd->ihd', low(prob), qkv_page[:, 2], precision=HIGHEST)
    heads = heads * jnp.transpose(allowed).astype(jnp.float32)[:, :, None]
    return low_back(low(heads))

def reference(text_in, visual_in, visual_count, line_index, box_index, qkv_weight, bias_table, out_weight, out_bias, norm1_gain, norm1_shift, ffn_weight_in, ffn_bias_in, ffn_weight_out, ffn_bias_out, norm2_gain, norm2_shift, batch_gain, batch_shift, cotangent):
    slots = jnp.arange(PAGE_LEN, dtype=jnp.int32)
    valid_rows = (slots[None, :] < visual_count[:, None]).astype(jnp.float32).reshape(TOKENS, 1)
    total_count = jnp.sum(valid_rows)
    line_pages = jnp.transpose(line_index.reshape(2, PAGES, PAGE_LEN), (1, 0, 2))
    box_pages = jnp.transpose(box_index.reshape(2, 2, PAGES, PAGE_LEN), (2, 0, 1, 3))

    def forward(text, visual, qkv_w, table, out_w, out_b, gain_one, shift_one, w_in, b_in, w_out, b_out, gain_two, shift_two, bn_gain, bn_shift):
        feature_mean = lax.optimization_barrier(jnp.sum(visual * valid_rows, axis=0)) / total_count
        centered_values = (visual - feature_mean) * valid_rows
        feature_var = lax.optimization_barrier(jnp.sum(centered_values * centered_values, axis=0)) / total_count
        normed = (centered_values * lax.rsqrt(feature_var + EPSILON) * bn_gain + bn_shift) * valid_rows
        visual_low = low(normed)
        text_qkv = jnp.dot(text, qkv_w[:, :, :H * HD].reshape(D, 3 * H * HD), precision=HIGHEST).reshape(TOKENS, 3, H, HD)
        visual_qkv = jnp.dot(visual_low, qkv_w[:, :, H * HD:].reshape(D, 3 * H * HD), precision=HIGHEST).reshape(TOKENS, 3, H, HD)
        qkv_all = low_back(low(jnp.concatenate([text_qkv, visual_qkv], axis=2)))
        heads = lax.map(jax.checkpoint(partial(page_heads, table)), (qkv_all.reshape(PAGES, PAGE_LEN, 3, 2 * H, HD), line_pages, box_pages, visual_count))
        joined = heads.reshape(TOKENS, 2 * H * HD)
        attention = low_back(jnp.dot(joined, out_w, precision=HIGHEST))
        hidden_one = text + attention + out_b
        after_one = layer_norm(hidden_one, gain_one, shift_one)
        pre = low_back(jnp.dot(low(after_one), w_in, precision=HIGHEST) + b_in)
        act = low(jax.nn.gelu(pre, approximate=False))
        branch = low_back(jnp.dot(act, w_out, precision=HIGHEST) + b_out)
        hidden_two = after_one + branch
        return layer_norm(hidden_two, gain_two, shift_two)
    floats = tuple((a.astype(jnp.float32) for a in (text_in, visual_in, qkv_weight, bias_table, out_weight, out_bias, norm1_gain, norm1_shift, ffn_weight_in, ffn_bias_in, ffn_weight_out, ffn_bias_out, norm2_gain, norm2_shift, batch_gain, batch_shift)))
    result, pull = jax.vjp(forward, *floats)
    g_text, g_visual, g_qkv, g_table, g_outw, g_outb, g_gain1, g_shift1, g_win, g_bin, g_wout, g_bout, g_gain2, g_shift2, g_bng, g_bnb = pull(cotangent.astype(jnp.float32))
    return (result.astype(jnp.bfloat16), g_text, g_visual, g_qkv, g_table, g_outw, g_outb, g_gain1, g_shift1, g_win, g_bin, g_wout, g_bout, g_gain2, g_shift2, g_bng, g_bnb)
```

```python
import functools

import jax
import jax.numpy as jnp
from jax import lax
from jax.experimental import pallas as pl
from jax.experimental.pallas import tpu as pltpu
from jax.sharding import PartitionSpec as P

H = 12
HD = 64
NB_REL = 32
NB_BOX = 16
LINES = 48
BOXES = 32

EPSILON = 1e-05
FLOOR_SCORE = -1000000000.0
SCALE = HD ** (-0.5)
LEVELS = 128
MASK_LANE = LINES + 2 * BOXES
VMEM_LIMIT = 60 * 1024 * 1024

F32 = jnp.float32
BF16 = jnp.bfloat16

NN = (((1,), (0,)), ((), ()))
NT = (((1,), (1,)), ((), ()))
TN = (((0,), (0,)), ((), ()))


def dot(left, right, dims=NN):
    return lax.dot_general(left, right, dims, preferred_element_type=F32)


def iota(shape, axis):
    return lax.broadcasted_iota(jnp.int32, shape, axis)


def params():
    return pltpu.CompilerParams(vmem_limit_bytes=VMEM_LIMIT)


def vmem(count):
    return [pl.BlockSpec(memory_space=pltpu.VMEM)] * count


def stream_is_visual():
    return lax.axis_index("head") >= lax.axis_size("head") // 2


GROUPS = (
    (0, LINES, NB_REL // 2, 0),
    (LINES, LINES + BOXES, NB_BOX // 2, NB_REL),
    (LINES + BOXES, LINES + 2 * BOXES, NB_BOX // 2, NB_REL + NB_BOX),
)


def bucket_map(half, offset, table_width):
    level = iota((table_width, LEVELS), 1) - LEVELS // 2
    bucket = jnp.clip(level, -half, half - 1) + half + offset
    return (bucket == iota((table_width, LEVELS), 0)).astype(F32)


def same_group(row, lane):
    inside = jnp.zeros(row.shape, jnp.bool_)
    for start, stop, unused_half, unused_offset in GROUPS:
        inside = inside | ((row >= start) & (row < stop) & (lane >= start) & (lane < stop))
    return inside


def prep_kernel(count_ref, line_ref, box_ref, table_ref, oh_ref, oht_ref, tab_ref):
    visual = stream_is_visual()
    tokens = line_ref.shape[1]
    heads_local, table_width = table_ref.shape
    line = jnp.where(visual, line_ref[1:2, :], line_ref[0:1, :])
    across = jnp.where(visual, box_ref[1, 0:1, :], box_ref[0, 0:1, :]) + LINES
    down = jnp.where(visual, box_ref[1, 1:2, :], box_ref[0, 1:2, :]) + (LINES + BOXES)
    level = iota((LEVELS, tokens), 0)
    wanted = jnp.where(level < LINES, line, jnp.where(level < LINES + BOXES, across, down))
    one_hot = (wanted == level).astype(F32)
    back = LEVELS - 1 - level
    wanted_back = jnp.where(back < LINES, line, jnp.where(back < LINES + BOXES, across, down))
    oht_ref[...] = (wanted_back == back).astype(F32).astype(BF16)
    closed = jnp.logical_and(visual, iota((LEVELS, tokens), 1) >= count_ref[0])
    mask = jnp.where(closed, FLOOR_SCORE, 0.0)
    oh_ref[...] = jnp.transpose(jnp.where(level == MASK_LANE, mask, one_hot)).astype(BF16)
    row = iota((LEVELS, LEVELS), 0)
    lane = iota((LEVELS, LEVELS), 1)
    inside = same_group(row, lane)
    table = table_ref[...]
    high = table.astype(BF16)
    low = (table - high.astype(F32)).astype(BF16)
    maps = [
        bucket_map(half, offset, table_width).astype(BF16)
        for unused_start, unused_stop, half, offset in GROUPS
    ]
    for part, values in enumerate((high, low)):
        spread = [dot(values, one_map) for one_map in maps]
        for head in range(heads_local):
            rows = [jnp.broadcast_to(s[head : head + 1, :], (LEVELS, LEVELS)) for s in spread]
            picked = jnp.where(
                row < LINES, rows[0], jnp.where(row < LINES + BOXES, rows[1], rows[2])
            )
            turned = pltpu.roll(picked, LEVELS // 2, 1, stride=1, stride_axis=0)
            pairs = jnp.where(inside, turned, 0.0)
            if part == 0:
                pairs = jnp.where((lane == MASK_LANE) & (row < LINES), 1.0, pairs)
            tab_ref[head, :, part * LEVELS : (part + 1) * LEVELS] = pairs.astype(BF16)


def prep(visual_count, line_index, box_index, bias_table):
    tokens = line_index.shape[1]
    heads_local = bias_table.shape[0]
    return pl.pallas_call(
        prep_kernel,
        out_shape=(
            jax.ShapeDtypeStruct((tokens, LEVELS), BF16),
            jax.ShapeDtypeStruct((LEVELS, tokens), BF16),
            jax.ShapeDtypeStruct((heads_local, LEVELS, 2 * LEVELS), BF16),
        ),
        in_specs=[pl.BlockSpec(memory_space=pltpu.SMEM)] + vmem(3),
        out_specs=tuple(vmem(3)),
        compiler_params=params(),
        name="prep",
    )(visual_count, line_index, box_index, bias_table)


def attend_kernel(
    count_ref,
    text_ref,
    visual_ref,
    stats_ref,
    w_ref,
    tab_ref,
    oh_ref,
    x_ref,
    qkv_ref,
    heads_ref,
    prob_ref,
    prob_keep,
    sems,
):
    visual = stream_is_visual()
    tokens, width = text_ref.shape
    local_width = w_ref.shape[1] // 3
    heads_local = local_width // HD
    count = count_ref[0]
    block = tokens // 2

    @pl.when(visual)
    def _():
        mean, scale, gain, shift = (stats_ref[i : i + 1, :] for i in range(4))
        for part in range(2):
            rows = pl.ds(part * block, block)
            keep = (iota((block, 1), 0) + part * block < count).astype(F32)
            centred = (visual_ref[rows, :].astype(F32) - mean) * keep
            x_ref[rows, :] = ((centred * scale * gain + shift) * keep).astype(BF16)

    @pl.when(jnp.logical_not(visual))
    def _():
        x_ref[...] = text_ref[...]

    for m in range(3):
        cols = pl.ds(m * local_width, local_width)
        qkv_ref[:, cols] = dot(x_ref[...], w_ref[:, cols]).astype(BF16)

    allowed = jnp.logical_or(jnp.logical_not(visual), iota((tokens, 1), 0) < count).astype(F32)
    one_hot = oh_ref[...]
    copies = []
    outs = []
    for head in range(heads_local):
        cols = [pl.ds(m * local_width + head * HD, HD) for m in range(3)]
        keys = jnp.concatenate([one_hot, one_hot, qkv_ref[:, cols[1]]], axis=1)
        left = dot(one_hot, tab_ref[head]).astype(BF16)
        values = qkv_ref[:, cols[2]]
        query = qkv_ref[:, cols[0]] * jnp.asarray(SCALE, BF16)
        parts = []
        for part in range(2):
            span = slice(part * block, (part + 1) * block)
            scores = dot(jnp.concatenate([left[span], query[span]], axis=1), keys, NT)
            top = jnp.max(scores, axis=1, keepdims=True)
            shifted = jnp.exp(scores - top)
            total = jnp.sum(shifted, axis=1, keepdims=True)
            prob = (shifted * (1.0 / total)).astype(BF16)
            prob_keep[head, span, :] = prob
            parts.append(dot(prob, values))
        copy = pltpu.make_async_copy(prob_keep.at[head], prob_ref.at[head], sems.at[head])
        copy.start()
        copies.append(copy)
        outs.append((jnp.concatenate(parts, axis=0) * allowed).astype(BF16))
        if head % 2 == 1:
            heads_ref[:, (head - 1) * HD : (head + 1) * HD] = jnp.concatenate(outs[-2:], axis=1)
    if heads_local % 2:
        heads_ref[:, (heads_local - 1) * HD :] = outs[-1]
    for copy in copies:
        copy.wait()


def attend(visual_count, text_in, visual_in, stats, weight, tab, one_hot):
    tokens, width = text_in.shape
    local_width = weight.shape[1] // 3
    heads_local = local_width // HD
    return pl.pallas_call(
        attend_kernel,
        out_shape=(
            jax.ShapeDtypeStruct((tokens, width), BF16),
            jax.ShapeDtypeStruct((tokens, 3 * local_width), BF16),
            jax.ShapeDtypeStruct((tokens, local_width), BF16),
            jax.ShapeDtypeStruct((heads_local, tokens, tokens), BF16),
        ),
        in_specs=[pl.BlockSpec(memory_space=pltpu.SMEM)] + vmem(6),
        out_specs=tuple(vmem(3)) + (pl.BlockSpec(memory_space=pl.ANY),),
        scratch_shapes=[
            pltpu.VMEM((heads_local, tokens, tokens), BF16),
            pltpu.SemaphoreType.DMA((heads_local,)),
        ],
        compiler_params=params(),
        name="attend",
    )(visual_count, text_in, visual_in, stats, weight, tab, one_hot)


ERF_P = 0.3275911 * 0.7071067811865476
ERF_A = (0.254829592, -0.284496736, 1.421413741, -1.453152027, 1.061405429)
VEC_ROWS = 16


def gelu_parts(pre):
    t = 1.0 / (1.0 + ERF_P * jnp.abs(pre))
    bell = jnp.exp(-0.5 * pre * pre)
    poly = 0.5 * ERF_A[4]
    for coefficient in ERF_A[3::-1]:
        poly = poly * t + 0.5 * coefficient
    tail = poly * t * bell
    cdf = jnp.where(pre >= 0.0, 1.0 - tail, tail)
    return pre * cdf, cdf + pre * (bell * 0.3989422804014327)


def normed_rows(hidden):
    average = jnp.mean(hidden, axis=-1, keepdims=True)
    centred = hidden - average
    scale = lax.rsqrt(jnp.mean(centred * centred, axis=-1, keepdims=True) + EPSILON)
    return centred * scale, scale


def normed_back(upstream, hat, scale, gain):
    scaled = upstream * gain
    return scale * (
        scaled
        - jnp.mean(scaled, axis=-1, keepdims=True)
        - hat * jnp.mean(scaled * hat, axis=-1, keepdims=True)
    )


def owner_of(half, step):
    place = lax.axis_index("dp")
    core = place & 1
    chip = place >> 1
    return ((chip ^ step) << 1) | (core if half == 0 else 1 - core)


def ffn_kernel(pieces, fused, *refs):
    (text_ref, cot_ref), refs = refs[:2], refs[2:]
    piece_refs, refs = refs[:pieces], refs[pieces:]
    (wo_hbm, w1_hbm, w2_hbm, small_ref, b1_ref), refs = refs[:5], refs[5:]
    (out_ref, share_ref, dheads_ref, dheadst_ref), refs = refs[:4], refs[4:]
    if fused:
        (mine_ref, sib_ref), refs = refs[:2], refs[2:]
        wo, w1, w2, sems, slope, act_ref, dpre_ref, low_ref, branch_ref, mix_ref, sib, vec = refs
    else:
        (act_ref, dpre_ref, low_ref, branch_ref, mix_ref, vec), refs = refs[:6], refs[6:]
        wo, w1, w2, sems, slope = refs
    copies = [
        pltpu.make_async_copy(src, dst, sems.at[i])
        for i, (src, dst) in enumerate(((wo_hbm, wo), (w1_hbm, w1), (w2_hbm, w2)))
    ]
    for copy in copies:
        copy.start()
    tokens, width = text_ref.shape
    hidden_width = w1.shape[1]
    local_width = piece_refs[0].shape[1]
    head_rank = lax.axis_index("head")
    out_bias, gain1, shift1, b2, gain2, shift2 = (small_ref[i : i + 1, :] for i in range(6))
    block = tokens // 2
    chunk = width
    chunks = hidden_width // chunk
    share = share_ref.shape[0]
    vec[...] = jnp.zeros_like(vec)
    own_rows = pl.ds(pl.multiple_of(head_rank * local_width, 64), local_width)

    def step(index, carry):
        rows = pl.ds(pl.multiple_of(index * block, block), block)

        @pl.when(index == 0)
        def _():
            copies[0].wait()

        mixed = text_ref[rows, :].astype(F32) + out_bias
        for step_index, piece in enumerate(piece_refs):
            source = head_rank ^ step_index
            wo_rows = pl.ds(pl.multiple_of(source * local_width, 64), local_width)
            mixed = mixed + dot(piece[rows, :], wo[wo_rows, :])
        hat1, scale1 = normed_rows(mixed)
        after = hat1 * gain1 + shift1
        after_low = after.astype(BF16)
        low_ref[rows, :] = after_low

        @pl.when(index == 0)
        def _():
            copies[1].wait()
            copies[2].wait()

        branch = jnp.zeros((block, width), F32)
        for c in range(chunks):
            cols = pl.ds(c * chunk, chunk)
            pre = dot(after_low, w1[:, cols]) + b1_ref[c : c + 1, :]
            act, derivative = gelu_parts(pre)
            slope[:, cols] = derivative
            act = act.astype(BF16)
            act_ref[rows, cols] = act
            branch = branch + dot(act, w2[cols, :])
        hat2, scale2 = normed_rows(after + (branch + b2))
        out_ref[rows, :] = (hat2 * gain2 + shift2).astype(BF16)
        upstream = cot_ref[rows, :].astype(F32)
        dh_two = normed_back(upstream, hat2, scale2, gain2)
        dbranch = dh_two.astype(BF16)
        branch_ref[rows, :] = dbranch
        vec[7:8, :] += jnp.sum(dbranch.astype(F32), axis=0, keepdims=True)
        vec[8:9, :] += jnp.sum(upstream * hat2, axis=0, keepdims=True)
        vec[9:10, :] += jnp.sum(upstream, axis=0, keepdims=True)
        dy = dh_two
        for c in range(chunks):
            cols = pl.ds(c * chunk, chunk)
            dpre = (dot(dbranch, w2[cols, :], NT) * slope[:, cols]).astype(BF16)
            dpre_ref[rows, cols] = dpre
            vec[3 + c : 4 + c, :] += jnp.sum(dpre.astype(F32), axis=0, keepdims=True)
            dy = dy + dot(dpre, w1[:, cols], NT)
        dh_one = normed_back(dy, hat1, scale1, gain1)
        vec[0:1, :] += jnp.sum(dh_one, axis=0, keepdims=True)
        vec[1:2, :] += jnp.sum(dy * hat1, axis=0, keepdims=True)
        vec[2:3, :] += jnp.sum(dy, axis=0, keepdims=True)
        per_block = block // share
        for part in range(per_block):

            @pl.when(index * per_block + part == head_rank)
            def _():
                share_ref[...] = dh_one[part * share : (part + 1) * share]

        dmix = dh_one.astype(BF16)
        mix_ref[rows, :] = dmix
        dheads_ref[rows, :] = dot(dmix, wo[own_rows, :], NT).astype(BF16)
        dheadst_ref[:, rows] = dot(wo[own_rows, :], dmix, NT).astype(BF16)
        return carry

    lax.fori_loop(0, tokens // block, step, 0)
    if not fused:
        return

    owners = [owner_of(half, k) for half in range(2) for k in range(4)]
    width_own = width // 8
    part_in = width_own // 4
    window = hidden_width // 8
    part_out = window // 4
    targets = [mine_ref.at[k] for k in range(4)] + [sib.at[k] for k in range(4)]
    lane = iota((part_in, width), 1)
    row = iota((part_in, width), 0)
    pick = jnp.concatenate(
        [
            (lane == owner * width_own + head_rank * part_in + row).astype(F32)
            for owner in owners
        ],
        axis=0,
    ).astype(BF16)
    low_t = dot(pick, low_ref[...], NT).astype(BF16)
    for c in range(chunks):
        grad = dot(low_t, dpre_ref[:, c * chunk : (c + 1) * chunk])
        for n, target in enumerate(targets):
            target[c * part_in : (c + 1) * part_in, :] = grad[n * part_in : (n + 1) * part_in]
    base = chunks * part_in
    pick = (
        iota((part_out, window), 1) == head_rank * part_out + iota((part_out, window), 0)
    ).astype(F32).astype(BF16)
    for owner, target in zip(owners, targets):
        cols = pl.ds(pl.multiple_of(owner * window, 128), window)
        act_t = dot(pick, act_ref[:, cols], NT).astype(BF16)
        target[base : base + part_out, :] = dot(act_t, branch_ref[...])
    base += part_out
    lane = iota((width_own, width), 1)
    row = iota((width_own, width), 0)
    half_own = width_own // 2
    for owner, target in zip(owners, targets):
        pick = (lane == owner * width_own + row).astype(F32).astype(BF16)
        mix_t = dot(pick, mix_ref[...], NT).astype(BF16)
        grad = dot(mix_t, piece_refs[0][...])
        target[base : base + half_own, :] = jnp.concatenate(
            [grad[:half_own], grad[half_own:]], axis=1
        )
    base += half_own
    for target in targets:
        target[base : base + VEC_ROWS, :] = vec[...]
    for k in range(4):
        sib_ref[k] = sib[k].astype(BF16)


def ffn(text_in, cotangent, pieces, out_weight, w1, w2, small, b1, share, fused):
    tokens, width = text_in.shape
    hidden_width = w1.shape[1]
    local_width = pieces[0].shape[1]
    block = tokens // 2
    weights = [
        pltpu.VMEM(out_weight.shape, BF16),
        pltpu.VMEM(w1.shape, BF16),
        pltpu.VMEM(w2.shape, BF16),
        pltpu.SemaphoreType.DMA((3,)),
        pltpu.VMEM((block, hidden_width), F32),
    ]
    kept = [
        ((tokens, hidden_width), BF16),
        ((tokens, hidden_width), BF16),
        ((tokens, width), BF16),
        ((tokens, width), BF16),
        ((tokens, width), BF16),
    ]
    outs = [
        jax.ShapeDtypeStruct((tokens, width), BF16),
        jax.ShapeDtypeStruct((share, width), F32),
        jax.ShapeDtypeStruct((tokens, local_width), BF16),
        jax.ShapeDtypeStruct((local_width, tokens), BF16),
    ]
    if fused:
        rows = 2 * (hidden_width // 32) + width // 16 + VEC_ROWS
        outs += [
            jax.ShapeDtypeStruct((4, rows, width), F32),
            jax.ShapeDtypeStruct((4, rows, width), BF16),
        ]
        scratch = weights + [pltpu.VMEM(*entry) for entry in kept]
        scratch += [pltpu.VMEM((4, rows, width), F32), pltpu.VMEM((VEC_ROWS, width), F32)]
    else:
        outs += [jax.ShapeDtypeStruct(*entry) for entry in kept]
        outs += [jax.ShapeDtypeStruct((VEC_ROWS, width), F32)]
        scratch = weights
    return pl.pallas_call(
        functools.partial(ffn_kernel, len(pieces), fused),
        out_shape=tuple(outs),
        in_specs=vmem(2 + len(pieces)) + [pl.BlockSpec(memory_space=pl.ANY)] * 3 + vmem(2),
        out_specs=tuple(vmem(len(outs))),
        scratch_shapes=scratch,
        compiler_params=params(),
        name="ffn",
    )(text_in, cotangent, *pieces, out_weight, w1, w2, small, b1)


def attend_back_kernel(
    count_ref,
    qkv_ref,
    heads_ref,
    dheads_ref,
    dheadst_ref,
    oh_ref,
    oht_ref,
    w_ref,
    visual_ref,
    stats_ref,
    prob_hbm,
    *refs,
):
    steps = lax.axis_size("head")
    dqkv_ref, pair_ref, sums_ref = refs[:3]
    part_refs = refs[3 : 3 + steps]
    prob_keep, sems = refs[3 + steps :]
    visual = stream_is_visual()
    tokens = qkv_ref.shape[0]
    local_width = qkv_ref.shape[1] // 3
    heads_local = local_width // HD
    count = count_ref[0]
    copies = [
        pltpu.make_async_copy(prob_hbm.at[head], prob_keep.at[head], sems.at[head])
        for head in range(heads_local)
    ]
    for copy in copies:
        copy.start()
    open_row = jnp.logical_or(jnp.logical_not(visual), iota((tokens, 1), 0) < count)
    open_lane = jnp.logical_or(jnp.logical_not(visual), iota((1, tokens), 1) < count)
    allowed = open_row.astype(BF16)
    allowed_lane = open_lane.astype(BF16)
    one_hot = oh_ref[...]
    one_hot_t = oht_ref[...]
    inside = same_group(LEVELS - 1 - iota((LEVELS, LEVELS), 0), iota((LEVELS, LEVELS), 1))
    eye = (iota((HD, HD), 0) == iota((HD, HD), 1)).astype(F32).astype(BF16)
    extra = jnp.concatenate(
        [jnp.ones((tokens, 2), F32), jnp.zeros((tokens, HD - 2), F32)], axis=1
    ).astype(BF16)
    lane = iota((tokens, HD), 1)
    turned = [[], [], []]
    for head in range(heads_local):
        cols = [pl.ds(m * local_width + head * HD, HD) for m in range(3)]
        own = slice(head * HD, (head + 1) * HD)
        query, keys, values = (qkv_ref[:, c] for c in cols)
        dout = dheads_ref[:, own] * allowed
        dout_t = dheadst_ref[own, :] * allowed_lane
        inner = -jnp.sum(
            dout.astype(F32) * heads_ref[:, own].astype(F32), axis=1, keepdims=True
        )
        high = inner.astype(BF16).astype(F32)
        tail = jnp.where(lane == 0, high, jnp.where(lane == 1, inner - high, 0.0)).astype(BF16)
        copies[head].wait()
        centred = dot(
            jnp.concatenate([dout, tail], axis=1), jnp.concatenate([values, extra], axis=1), NT
        )
        prob = prob_keep[head]
        dscore = (prob.astype(F32) * centred).astype(BF16)
        both = dot(dscore, jnp.concatenate([one_hot, keys], axis=1))
        level_high = both[:, :LEVELS].astype(BF16)
        level_low = (both[:, :LEVELS] - level_high.astype(F32)).astype(BF16)
        pairs = dot(one_hot_t, level_high) + dot(one_hot_t, level_low)
        pair_ref[head] = jnp.where(inside, pairs, 0.0)
        turned[0].append(both[:, LEVELS:] * SCALE)
        query_t = dot(eye, query, NT).astype(BF16)
        turned[1].append(dot(query_t, dscore) * SCALE)
        turned[2].append(dot(dout_t, prob))
        if head % 2 == 1 or head == heads_local - 1:
            start = head - head % 2
            span = HD * len(turned[0])
            for m in range(3):
                joined = jnp.concatenate(turned[m], axis=1 if m == 0 else 0)
                if m:
                    joined = jnp.transpose(joined)
                dqkv_ref[:, pl.ds(m * local_width + start * HD, span)] = joined.astype(BF16)
            turned = [[], [], []]

    head_rank = lax.axis_index("head")
    share = tokens // steps
    mean, scale = stats_ref[0:1, :], stats_ref[1:2, :]
    shift_sum = jnp.zeros(mean.shape, F32)
    gain_sum = jnp.zeros(mean.shape, F32)
    for k in range(steps):
        start = pl.multiple_of((head_rank ^ k) * share, share)
        rows = pl.ds(start, share)
        part = dot(dqkv_ref[rows, :], w_ref[...], NT)
        part_refs[k][...] = part.astype(BF16)
        keep = jnp.logical_and(visual, iota((share, 1), 0) + start < count).astype(F32)
        kept = part * keep
        shift_sum = shift_sum + jnp.sum(kept, axis=0, keepdims=True)
        hat = (visual_ref[rows, :].astype(F32) - mean) * scale
        gain_sum = gain_sum + jnp.sum(kept * hat, axis=0, keepdims=True)
    sums_ref[...] = jnp.concatenate(
        [shift_sum, gain_sum, jnp.zeros((6, mean.shape[1]), F32)], axis=0
    )


def attend_back(
    visual_count, qkv, heads, dheads, dheads_t, one_hot, one_hot_t, weight, visual_in, stats, prob
):
    tokens, width = visual_in.shape
    local_width = heads.shape[1]
    heads_local = local_width // HD
    steps = lax.axis_size("head")
    return pl.pallas_call(
        attend_back_kernel,
        out_shape=(
            jax.ShapeDtypeStruct((tokens, 3 * local_width), BF16),
            jax.ShapeDtypeStruct((heads_local, LEVELS, LEVELS), F32),
            jax.ShapeDtypeStruct((8, width), F32),
        )
        + tuple(jax.ShapeDtypeStruct((tokens // steps, width), BF16) for k in range(steps)),
        in_specs=[pl.BlockSpec(memory_space=pltpu.SMEM)]
        + vmem(9)
        + [pl.BlockSpec(memory_space=pl.ANY)],
        out_specs=tuple(vmem(3 + steps)),
        scratch_shapes=[
            pltpu.VMEM((heads_local, tokens, tokens), BF16),
            pltpu.SemaphoreType.DMA((heads_local,)),
        ],
        compiler_params=params(),
        name="attend_back",
    )(
        visual_count,
        qkv,
        heads,
        dheads,
        dheads_t,
        one_hot,
        one_hot_t,
        weight,
        visual_in,
        stats,
        prob,
    )


def qkv_grad_kernel(fused, x_ref, dqkv_ref, pair_ref, *refs):
    tokens, width = x_ref.shape
    heads_local = pair_ref.shape[0]
    table_width = NB_REL + 2 * NB_BOX
    sums = [[], [], []]
    for head in range(heads_local):
        back = pltpu.roll(pair_ref[head], LEVELS // 2 + 1, 1, stride=1, stride_axis=0)
        for n, (start, stop, unused_half, unused_offset) in enumerate(GROUPS):
            rows = back[LEVELS - stop : LEVELS - start]
            sums[n].append(jnp.sum(rows, axis=0, keepdims=True))
    table = jnp.zeros((8, table_width), F32)
    for n, (unused_start, unused_stop, half, offset) in enumerate(GROUPS):
        stacked = jnp.concatenate(
            sums[n] + [jnp.zeros((8 - heads_local, LEVELS), F32)], axis=0
        )
        spread = bucket_map(half, offset, table_width).astype(BF16)
        high = stacked.astype(BF16)
        rest = stacked - high.astype(F32)
        low = rest.astype(BF16)
        lowest = (rest - low.astype(F32)).astype(BF16)
        for piece in (high, low, lowest):
            table = table + dot(piece, spread, NT)
    if not fused:
        grad_ref, table_ref = refs
        table_ref[...] = table
        eye = (iota((width, width), 0) == iota((width, width), 1)).astype(F32).astype(BF16)
        x_t = dot(eye, x_ref[...], NT).astype(BF16)
        grad_ref[...] = dot(x_t, dqkv_ref[...]).astype(BF16)
        return
    mine_ref, sib_ref = refs
    width_own = width // 8
    lane = iota((width_own, width), 1)
    row = iota((width_own, width), 0)
    columns = dqkv_ref.shape[1]
    padded = jnp.concatenate(
        [
            jnp.concatenate([table, jnp.zeros((8, columns - table_width), F32)], axis=1),
            jnp.zeros((8, columns), F32),
        ],
        axis=0,
    )
    for half, target in ((1, sib_ref), (0, mine_ref)):
        pick = jnp.concatenate(
            [(lane == owner_of(half, k) * width_own + row).astype(F32) for k in range(4)], axis=0
        ).astype(BF16)
        x_t = dot(pick, x_ref[...], NT).astype(BF16)
        grad = dot(x_t, dqkv_ref[...])
        for k in range(4):
            target[k] = jnp.concatenate(
                [grad[k * width_own : (k + 1) * width_own], padded], axis=0
            ).astype(target.dtype)


def qkv_grad(x, dqkv, pairs, fused):
    tokens, width = x.shape
    columns = dqkv.shape[1]
    if fused:
        rows = width // 8 + 16
        outs = (
            jax.ShapeDtypeStruct((4, rows, columns), F32),
            jax.ShapeDtypeStruct((4, rows, columns), BF16),
        )
    else:
        outs = (
            jax.ShapeDtypeStruct((width, columns), BF16),
            jax.ShapeDtypeStruct((8, NB_REL + 2 * NB_BOX), F32),
        )
    return pl.pallas_call(
        functools.partial(qkv_grad_kernel, fused),
        out_shape=outs,
        in_specs=vmem(3),
        out_specs=tuple(vmem(2)),
        compiler_params=params(),
        name="qkv_grad",
    )(x, dqkv, pairs)


def swap(value, axis, mask):
    size = lax.axis_size(axis)
    return lax.ppermute(value, axis, [(i, i ^ mask) for i in range(size)])


def owned_sum(mine, sib):
    joined = mine + swap(sib, "dp", 1).astype(F32)
    total = joined[0]
    for k in range(1, 4):
        total = total + swap(joined[k].astype(BF16), "dp", k << 1).astype(F32)
    return total


def small_sum(value, fused):
    if not fused:
        return lax.psum(value, ("dp", "head"))
    value = value + swap(value, "dp", 1)
    value = value + swap(value, "dp", 2) + swap(value, "dp", 4) + swap(value, "dp", 6)
    return value + swap(value, "head", 1) + swap(value, "head", 2) + swap(value, "head", 3)


def batch_stats(visual, valid_rows, fused):
    count = jnp.sum(valid_rows)
    sums = jnp.sum(visual * valid_rows, axis=0)
    centred = (visual - sums / count) * valid_rows
    squares = jnp.sum(centred * centred, axis=0)
    packed = jnp.stack([sums, squares, jnp.full_like(sums, count)])

    def join(blocks):
        total = functools.reduce(jnp.add, (b[0] for b in blocks))
        number = functools.reduce(jnp.add, (b[2] for b in blocks))
        mean = total / number
        spread = functools.reduce(
            jnp.add, (b[1] + b[2] * (b[0] / b[2] - mean) ** 2 for b in blocks)
        )
        return jnp.stack([total, spread, number])

    if fused:
        packed = join([packed, swap(packed, "dp", 1)])
        packed = join([packed] + [swap(packed, "dp", k) for k in (2, 4, 6)])
    else:
        gathered = lax.all_gather(packed, "dp")
        packed = join([gathered[i] for i in range(gathered.shape[0])])
    total, spread, number = packed
    return total / number, lax.rsqrt(spread / number + EPSILON), number[0]


def per_device(
    text_in,
    visual_in,
    visual_count,
    line_index,
    box_index,
    qkv_weight,
    bias_table,
    out_weight,
    out_bias,
    norm1_gain,
    norm1_shift,
    ffn_weight_in,
    ffn_bias_in,
    ffn_weight_out,
    ffn_bias_out,
    norm2_gain,
    norm2_shift,
    batch_gain,
    batch_shift,
    cotangent,
):
    tokens, width = text_in.shape
    local_width = qkv_weight.shape[2]
    heads_local = local_width // HD
    head_count = lax.axis_size("head")
    dp_count = lax.axis_size("dp")
    head_rank = lax.axis_index("head")
    dp_rank = lax.axis_index("dp")
    fused = head_count == 4 and dp_count == 8
    share = tokens // head_count
    first_row = head_rank * share
    hidden_width = ffn_weight_in.shape[1]
    table_width = bias_table.shape[1]

    valid_rows = (jnp.arange(tokens, dtype=jnp.int32) < visual_count[0]).astype(F32)[:, None]
    mean, batch_scale, total_count = batch_stats(visual_in.astype(F32), valid_rows, fused)
    stats = jnp.concatenate(
        [jnp.stack([mean, batch_scale, batch_gain, batch_shift]), jnp.zeros((4, width), F32)]
    )
    weight = qkv_weight.reshape(width, 3 * local_width)
    one_hot, one_hot_t, tab = prep(visual_count, line_index, box_index, bias_table)
    x, qkv, heads, prob = attend(visual_count, text_in, visual_in, stats, weight, tab, one_hot)
    pieces = [heads] + [swap(heads, "head", k) for k in range(1, head_count)]
    small = jnp.concatenate(
        [
            jnp.stack(
                [out_bias, norm1_gain, norm1_shift, ffn_bias_out, norm2_gain, norm2_shift]
            ),
            jnp.zeros((2, width), F32),
        ]
    )
    results = ffn(
        text_in,
        cotangent,
        pieces,
        out_weight,
        ffn_weight_in,
        ffn_weight_out,
        small,
        ffn_bias_in.reshape(hidden_width // width, width),
        share,
        fused,
    )
    layer_out, dh_share, dheads, dheads_t = results[:4]
    part_in = width // (dp_count * head_count)
    part_out = hidden_width // (dp_count * head_count)
    own_in = dp_rank * (width // dp_count) + head_rank * part_in
    if fused:
        mine, sib = results[4:]
        total = owned_sum(mine, sib)
        chunks = hidden_width // width
        base = chunks * part_in
        grad_ffn_in = jnp.transpose(
            total[:base].reshape(chunks, part_in, width), (1, 0, 2)
        ).reshape(part_in, hidden_width)
        grad_ffn_out = total[base : base + part_out]
        base += part_out
        half_own = width // dp_count // 2
        packed = total[base : base + half_own]
        grad_out_weight = jnp.transpose(
            jnp.concatenate([packed[:, :local_width], packed[:, local_width:]], axis=0)
        )
        vec = total[base + half_own :]
    else:
        act, dpre, after_low, dbranch, dmix, vec = results[4:]

        def scatter(value, dimension):
            return lax.psum_scatter(
                value.astype(BF16), "dp", scatter_dimension=dimension, tiled=True
            ).astype(F32)

        def own_columns(value, part):
            split = value.reshape(tokens, dp_count, head_count, part)
            return lax.dynamic_index_in_dim(split, head_rank, 2, keepdims=False).reshape(
                tokens, dp_count * part
            )

        grad_ffn_in = scatter(dot(own_columns(after_low, part_in), dpre, TN), 0)
        grad_ffn_out = scatter(dot(own_columns(act, part_out), dbranch, TN), 0)
        grad_out_weight = scatter(dot(heads, dmix, TN), 1)
        vec = lax.psum(vec.astype(BF16), "dp").astype(F32)

    def own_slice(index):
        return lax.dynamic_slice_in_dim(vec[index], own_in, part_in, 0)

    grad_ffn_bias_in = lax.dynamic_slice_in_dim(
        vec[3 : 3 + hidden_width // width].reshape(hidden_width),
        dp_rank * (hidden_width // dp_count) + head_rank * part_out,
        part_out,
        0,
    )

    dqkv, pairs, sums, *parts = attend_back(
        visual_count,
        qkv,
        heads,
        dheads,
        dheads_t,
        one_hot,
        one_hot_t,
        weight,
        visual_in,
        stats,
        prob,
    )
    received = [parts[0].astype(F32)] + [
        swap(parts[k], "head", k).astype(F32) for k in range(1, head_count)
    ]
    sums = small_sum(sums[:2], fused)
    if fused:
        grads = owned_sum(*qkv_grad(x, dqkv, pairs, True))
        own = width // dp_count
        grad_qkv = grads[:own].reshape(own, 3, local_width)
        table = grads[own : own + heads_local, :table_width]
        own = table_width // dp_count
        grad_bias_table = lax.dynamic_slice_in_dim(table, dp_rank * own, own, 1)
    else:
        grad, table = qkv_grad(x, dqkv, pairs, False)
        grad_qkv = scatter(grad.reshape(width, 3, local_width), 0)
        grad_bias_table = scatter(table[:heads_local], 1)

    half = head_count // 2
    same = functools.reduce(jnp.add, received[:half])
    other = functools.reduce(jnp.add, received[half:])
    visual = head_rank >= half
    grad_text = dh_share + jnp.where(visual, other, same)
    valid_share = lax.dynamic_slice_in_dim(valid_rows, first_row, share, 0)
    hat = (
        (lax.dynamic_slice_in_dim(visual_in, first_row, share, 0).astype(F32) - mean)
        * valid_share
        * batch_scale
    )
    dnormed = jnp.where(visual, same, other) * valid_share
    shift_gradient, gain_gradient = sums[0], sums[1]
    grad_visual = (
        valid_share
        * batch_scale
        * batch_gain
        * (dnormed - shift_gradient / total_count - hat * gain_gradient / total_count)
    )
    return (
        layer_out,
        grad_text,
        grad_visual,
        grad_qkv,
        grad_bias_table,
        grad_out_weight,
        own_slice(0),
        own_slice(1),
        own_slice(2),
        grad_ffn_in,
        grad_ffn_bias_in,
        grad_ffn_out,
        own_slice(7),
        own_slice(8),
        own_slice(9),
        gain_gradient,
        shift_gradient,
    )


def solution(mesh):
    in_specs = (
        P("dp", None),
        P("dp", None),
        P("dp"),
        P(None, "dp"),
        P(None, None, "dp"),
        P(None, None, "head"),
        P("head", None),
        P(),
        P(),
        P(),
        P(),
        P(),
        P(),
        P(),
        P(),
        P(),
        P(),
        P(),
        P(),
        P("dp", None),
    )
    out_specs = (
        P("dp", None),
        P(("dp", "head"), None),
        P(("dp", "head"), None),
        P("dp", None, "head"),
        P("head", "dp"),
        P("head", "dp"),
        P(("dp", "head")),
        P(("dp", "head")),
        P(("dp", "head")),
        P(("dp", "head"), None),
        P(("dp", "head")),
        P(("dp", "head"), None),
        P(("dp", "head")),
        P(("dp", "head")),
        P(("dp", "head")),
        P(),
        P(),
    )
    return jax.shard_map(
        per_device, mesh=mesh, in_specs=in_specs, out_specs=out_specs, check_vma=False
    )
```

```python
import functools

import jax
import jax.numpy as jnp
from jax import lax
from jax.experimental import pallas as pl
from jax.experimental.pallas import tpu as pltpu
from jax.sharding import PartitionSpec as P

HD = 64
NB_REL = 32
NB_BOX = 16
LINES = 48
BOXES = 32

EPSILON = 1e-05
FLOOR_SCORE = -1000000000.0
SCALE = HD ** (-0.5)
LEVELS = 128
MASK_LANE = LINES + 2 * BOXES
VMEM_LIMIT = 12 * 1024 * 1024
VEC_ROWS = 16
CHUNKS = 2

F32 = jnp.float32
BF16 = jnp.bfloat16

NN = (((1,), (0,)), ((), ()))
NT = (((1,), (1,)), ((), ()))
TN = (((0,), (0,)), ((), ()))
TT = (((0,), (1,)), ((), ()))


def dot(left, right, dims=NN):
    return lax.dot_general(left, right, dims, preferred_element_type=F32)


def iota(shape, axis):
    return lax.broadcasted_iota(jnp.int32, shape, axis)


def one_hot(condition):
    return condition.astype(F32).astype(BF16)


def thirds(value):
    high = value.astype(BF16)
    rest = value - high.astype(F32)
    middle = rest.astype(BF16)
    return high, middle, (rest - middle.astype(F32)).astype(BF16)


def picked(value, selector, dims=NN):
    return functools.reduce(jnp.add, (dot(part, selector, dims) for part in thirds(value)))


def call(kernel, name, micros, outs, args, count=None, scratch=(), final=()):
    vmem = pl.BlockSpec(memory_space=pltpu.VMEM)
    scalars = [] if count is None else [count]
    return pl.pallas_call(
        kernel,
        out_shape=tuple(
            jax.ShapeDtypeStruct(*entry) if place in final else pltpu.VMEM(*entry)
            for place, entry in enumerate(outs)
        ),
        in_specs=[pl.BlockSpec(memory_space=pltpu.SMEM)] * len(scalars) + [vmem] * len(args),
        out_specs=tuple(vmem for entry in outs),
        scratch_shapes=list(scratch),
        compiler_params=pltpu.CompilerParams(vmem_limit_bytes=VMEM_LIMIT),
        cost_estimate=pl.CostEstimate(
            flops=int(micros * 1e9), bytes_accessed=int(micros * 3e6), transcendentals=0
        ),
        name=name,
    )(*scalars, *[pltpu.with_memory_space_constraint(a, pltpu.VMEM) for a in args])


def stream_is_visual():
    return lax.axis_index("head") >= lax.axis_size("head") // 2


def stats_kernel(count_ref, visual_ref, out_ref):
    tokens, width = visual_ref.shape
    number = count_ref[0].astype(F32)
    keep = (iota((tokens, 1), 0) < count_ref[0]).astype(F32)
    visual = visual_ref[...].astype(F32)
    total = jnp.sum(visual * keep, axis=0, keepdims=True)
    centred = (visual - total / number) * keep
    spread = jnp.sum(centred * centred, axis=0, keepdims=True)
    out_ref[...] = jnp.concatenate(
        [total, spread, jnp.full((1, width), number, F32), jnp.zeros((5, width), F32)], axis=0
    )


def joined_stats(blocks):
    total = functools.reduce(jnp.add, (b[0:1] for b in blocks))
    number = functools.reduce(jnp.add, (b[2:3] for b in blocks))
    mean = total / number
    spread = functools.reduce(
        jnp.add, (b[1:2] + b[2:3] * (b[0:1] / b[2:3] - mean) ** 2 for b in blocks)
    )
    return total, spread, number


def join_stats_kernel(*refs):
    total, spread, number = joined_stats([ref[...] for ref in refs[:-1]])
    refs[-1][...] = jnp.concatenate(
        [total, spread, number, jnp.zeros((5, total.shape[1]), F32)], axis=0
    )


GROUPS = (
    (0, LINES, NB_REL // 2, 0),
    (LINES, LINES + BOXES, NB_BOX // 2, NB_REL),
    (LINES + BOXES, LINES + 2 * BOXES, NB_BOX // 2, NB_REL + NB_BOX),
)


def bucket_map(level, half, offset, table_width):
    bucket = jnp.clip(level, -half, half - 1) + half + offset
    return one_hot(bucket == iota((table_width, LEVELS), 0))


def same_group(row, lane):
    inside = jnp.zeros(row.shape, jnp.bool_)
    for start, stop, unused_half, unused_offset in GROUPS:
        inside = inside | ((row >= start) & (row < stop) & (lane >= start) & (lane < stop))
    return inside


def by_level(level, line, across, down):
    wanted = jnp.where(level < LINES, line, jnp.where(level < LINES + BOXES, across, down))
    return wanted == level


def prep_kernel(count_ref, line_ref, box_ref, table_ref, bias_ref, *refs):
    oh_ref, back_ref, tab_ref, small_ref, b1_ref = refs[8:]
    width = small_ref.shape[1]
    small_ref[...] = jnp.concatenate([ref[...] for ref in refs[:8]], axis=0)
    for c in range(bias_ref.shape[1] // width):
        b1_ref[c : c + 1, :] = bias_ref[:, c * width : (c + 1) * width]
    visual = stream_is_visual()
    tokens = line_ref.shape[1]
    heads_local, table_width = table_ref.shape
    line = jnp.where(visual, line_ref[1:2, :], line_ref[0:1, :])
    across = jnp.where(visual, box_ref[1, 0:1, :], box_ref[0, 0:1, :]) + LINES
    down = jnp.where(visual, box_ref[1, 1:2, :], box_ref[0, 1:2, :]) + (LINES + BOXES)
    level = iota((LEVELS, tokens), 0)
    back_ref[...] = one_hot(by_level(LEVELS - 1 - level, line, across, down))
    closed = jnp.logical_and(visual, iota((LEVELS, tokens), 1) >= count_ref[0])
    mask = jnp.where(closed, FLOOR_SCORE, 0.0)
    flags = by_level(level, line, across, down).astype(F32)
    oh_ref[...] = jnp.transpose(jnp.where(level == MASK_LANE, mask, flags)).astype(BF16)
    row = iota((LEVELS, LEVELS), 0)
    lane = iota((LEVELS, LEVELS), 1)
    inside = same_group(row, lane)
    offsets = iota((table_width, LEVELS), 1) - LEVELS // 2
    table = table_ref[...]
    spread = [
        picked(table, bucket_map(offsets, half, offset, table_width))
        for unused_start, unused_stop, half, offset in GROUPS
    ]
    for head in range(heads_local):
        rows = [jnp.broadcast_to(s[head : head + 1, :], (LEVELS, LEVELS)) for s in spread]
        chosen = jnp.where(row < LINES, rows[0], jnp.where(row < LINES + BOXES, rows[1], rows[2]))
        turned = pltpu.roll(chosen, LEVELS // 2, 1, stride=1, stride_axis=0)
        pairs = jnp.where(inside, turned, 0.0)
        high = jnp.where((lane == MASK_LANE) & (row < LINES), 1.0, pairs)
        tab_ref[:, head * LEVELS : (head + 1) * LEVELS] = high.astype(BF16)


def attend_chunk(chunk, count_ref, q_ref, k_ref, vt_ref, tab_ref, oh_ref, heads_ref, prob_ref):
    visual = stream_is_visual()
    tokens, local_width = q_ref.shape
    heads_local = local_width // HD
    block = heads_ref.shape[1]
    span = slice(chunk * block, (chunk + 1) * block)
    place = iota((1, block), 1) + chunk * block
    allowed = jnp.logical_or(jnp.logical_not(visual), place < count_ref[0]).astype(F32)
    one = oh_ref[...]
    left = dot(oh_ref[span, :], tab_ref[...]).astype(BF16)
    ones = jnp.ones((16, tokens), F32).astype(BF16)

    def scores(head):
        own = slice(head * HD, (head + 1) * HD)
        query = q_ref[span, own] * jnp.asarray(SCALE, BF16)
        right = jnp.concatenate([left[:, head * LEVELS : (head + 1) * LEVELS], query], axis=1)
        return dot(jnp.concatenate([one, k_ref[:, own]], axis=1), right, NT)

    following = scores(0)
    for head in range(heads_local):
        own = slice(head * HD, (head + 1) * HD)
        current = following
        if head + 1 < heads_local:
            following = scores(head + 1)
        shifted = jnp.exp(current - jnp.max(current, axis=0, keepdims=True))
        mixed = dot(jnp.concatenate([vt_ref[own, :], ones], axis=0), shifted.astype(BF16))
        share = 1.0 / mixed[HD : HD + 1]
        prob_ref[head] = (shifted * share).astype(BF16)
        heads_ref[own, :] = (mixed[:HD] * (share * allowed)).astype(BF16)


def attend_first_kernel(pieces, count_ref, text_ref, visual_ref, small_ref, w_ref, tab_ref, oh_ref, *refs):
    piece_refs, refs = refs[:pieces], refs[pieces:]
    stats_ref, x_ref, q_ref, k_ref, v_ref, kt_ref, vt_ref, heads_ref, prob_ref = refs
    visual = stream_is_visual()
    tokens, width = text_ref.shape
    total, spread, number = joined_stats([ref[...] for ref in piece_refs])
    mean = total / number
    scale = lax.rsqrt(spread / number + EPSILON)
    gain, shift = small_ref[6:7, :], small_ref[7:8, :]
    stats_ref[...] = jnp.concatenate(
        [mean, scale, gain, number, jnp.zeros((4, width), F32)], axis=0
    )

    @pl.when(visual)
    def _():
        keep = (iota((tokens, 1), 0) < count_ref[0]).astype(F32)
        centred = (visual_ref[...].astype(F32) - mean) * keep
        x_ref[...] = ((centred * scale * gain + shift) * keep).astype(BF16)

    @pl.when(jnp.logical_not(visual))
    def _():
        x_ref[...] = text_ref[...]

    x = x_ref[...]
    q_ref[...] = dot(x, w_ref[0]).astype(BF16)
    k_ref[...] = dot(x, w_ref[1]).astype(BF16)
    v_ref[...] = dot(x, w_ref[2]).astype(BF16)
    kt_ref[...] = dot(w_ref[1], x, TT).astype(BF16)
    vt_ref[...] = dot(w_ref[2], x, TT).astype(BF16)
    attend_chunk(0, count_ref, q_ref, k_ref, vt_ref, tab_ref, oh_ref, heads_ref, prob_ref)


ERF_P = 0.3275911 * 0.7071067811865476
ERF_A = (0.254829592, -0.284496736, 1.421413741, -1.453152027, 1.061405429)


def gelu_parts(pre):
    t = 1.0 / (1.0 + ERF_P * jnp.abs(pre))
    bell = jnp.exp(-0.5 * pre * pre)
    poly = 0.5 * ERF_A[4]
    for coefficient in ERF_A[3::-1]:
        poly = poly * t + 0.5 * coefficient
    tail = poly * t * bell
    cdf = jnp.where(pre >= 0.0, 1.0 - tail, tail)
    return pre * cdf, cdf + pre * (bell * 0.3989422804014327)


def normed_rows(hidden):
    average = jnp.mean(hidden, axis=-1, keepdims=True)
    centred = hidden - average
    scale = lax.rsqrt(jnp.mean(centred * centred, axis=-1, keepdims=True) + EPSILON)
    return centred * scale, scale


def normed_back(upstream, hat, scale, gain):
    scaled = upstream * gain
    return scale * (
        scaled
        - jnp.mean(scaled, axis=-1, keepdims=True)
        - hat * jnp.mean(scaled * hat, axis=-1, keepdims=True)
    )


def ffn_kernel(chunk, relative, pieces, *refs):
    (text_ref, cot_ref, wo, w1, w2, small_ref, b1_ref), refs = refs[:7], refs[7:]
    piece_refs, refs = refs[:pieces], refs[pieces:]
    out_ref, share_ref, act_ref, dpre_ref, low_ref, branch_ref, mix_ref = refs[:7]
    dheads_ref, dheadst_ref, vec_ref, slope = refs[7:]
    local_width, block = piece_refs[0].shape
    width = text_ref.shape[1]
    hidden_width = w1.shape[1]
    head_rank = lax.axis_index("head")
    out_bias, gain1, shift1, b2, gain2, shift2 = (small_ref[i : i + 1, :] for i in range(6))
    parts = hidden_width // width
    share = share_ref.shape[0]
    rows = slice(chunk * block, (chunk + 1) * block)
    own_rows = pl.ds(pl.multiple_of(head_rank * local_width, 64), local_width)

    sources = [
        (ref[...], head_rank ^ index if relative else index)
        for index, ref in enumerate(piece_refs)
    ]
    mixed = text_ref[rows, :].astype(F32) + out_bias
    for piece, source in sources:
        wo_rows = pl.ds(pl.multiple_of(source * local_width, 64), local_width)
        mixed = mixed + dot(piece, wo[wo_rows, :], TN)
    hat1, scale1 = normed_rows(mixed)
    after = hat1 * gain1 + shift1
    after_low = after.astype(BF16)
    low_ref[...] = after_low
    branch = jnp.zeros((block, width), F32)
    for c in range(parts):
        cols = slice(c * width, (c + 1) * width)
        act, slope[:, cols] = gelu_parts(dot(after_low, w1[:, cols]) + b1_ref[c : c + 1, :])
        act = act.astype(BF16)
        act_ref[:, cols] = act
        branch = branch + dot(act, w2[cols, :])
    hat2, scale2 = normed_rows(after + (branch + b2))
    out_ref[...] = (hat2 * gain2 + shift2).astype(BF16)
    upstream = cot_ref[rows, :].astype(F32)
    dh_two = normed_back(upstream, hat2, scale2, gain2)
    dbranch = dh_two.astype(BF16)
    branch_ref[...] = dbranch
    vec = [None] * 3
    dy = dh_two
    for c in range(parts):
        cols = slice(c * width, (c + 1) * width)
        dpre = (dot(dbranch, w2[cols, :], NT) * slope[:, cols]).astype(BF16)
        dpre_ref[:, cols] = dpre
        vec.append(dpre.astype(F32))
        dy = dy + dot(dpre, w1[:, cols], NT)
    dh_one = normed_back(dy, hat1, scale1, gain1)
    vec[:3] = [dh_one, dy * hat1, dy]
    vec += [dbranch.astype(F32), upstream * hat2, upstream]
    sums = [jnp.sum(v, axis=0, keepdims=True) for v in vec]
    vec_ref[...] = jnp.concatenate(
        sums + [jnp.zeros((VEC_ROWS - len(sums), width), F32)], axis=0
    )
    share_ref[...] = jnp.zeros_like(share_ref)
    per_block = block // share
    for part in range(per_block):

        @pl.when(head_rank == chunk * per_block + part)
        def _():
            share_ref[...] = dh_one[part * share : (part + 1) * share]

    dmix = dh_one.astype(BF16)
    mix_ref[...] = dmix
    dheads_ref[...] = dot(dmix, wo[own_rows, :], NT).astype(BF16)
    dheadst_ref[...] = dot(wo[own_rows, :], dmix, NT).astype(BF16)


def owner_of(half, step):
    place = lax.axis_index("dp")
    core = place & 1
    return (((place >> 1) ^ step) << 1) | (core if half == 0 else 1 - core)


def weight_grad_kernel(*refs):
    head_rank = lax.axis_index("head")
    names = ("out", "act", "dpre", "low", "branch", "mix", "heads", "vec")
    groups = {name: refs[i * CHUNKS : (i + 1) * CHUNKS] for i, name in enumerate(names)}
    layer_ref, mine_ref, sib_ref, sib, whole = refs[len(names) * CHUNKS :]
    block, width = groups["out"][0].shape
    hidden_width = groups["act"][0].shape[1]
    parts = hidden_width // width
    owners = [owner_of(half, k) for half in range(2) for k in range(4)]
    targets = [mine_ref.at[k] for k in range(4)] + [sib.at[k] for k in range(4)]
    width_own = width // 8
    part_in = width_own // 4
    window = hidden_width // 8
    part_out = window // 4
    half_own = width_own // 2
    for c in range(CHUNKS):
        layer_ref[c * block : (c + 1) * block, :] = groups["out"][c][...]

    lane = iota((part_in, width), 1)
    row = iota((part_in, width), 0)
    pick = jnp.concatenate(
        [
            one_hot(lane == owner * width_own + head_rank * part_in + row).astype(F32)
            for owner in owners
        ],
        axis=0,
    ).astype(BF16)
    low_t = [dot(pick, low[...], NT).astype(BF16) for low in groups["low"]]
    for p in range(parts):
        cols = slice(p * width, (p + 1) * width)
        grad = functools.reduce(
            jnp.add, (dot(low_t[c], groups["dpre"][c][:, cols]) for c in range(CHUNKS))
        )
        for n, target in enumerate(targets):
            target[p * part_in : (p + 1) * part_in, :] = grad[n * part_in : (n + 1) * part_in]
    base = parts * part_in
    pick = one_hot(
        iota((part_out, window), 1) == head_rank * part_out + iota((part_out, window), 0)
    )
    grad = jnp.zeros((8 * part_out, width), F32)
    for c in range(CHUNKS):
        stacked = []
        for owner in owners:
            cols = pl.ds(pl.multiple_of(owner * window, 128), window)
            stacked.append(dot(pick, groups["act"][c][:, cols], NT).astype(BF16))
        grad = grad + dot(jnp.concatenate(stacked, axis=0), groups["branch"][c][...])
    for n, target in enumerate(targets):
        target[base : base + part_out, :] = grad[n * part_out : (n + 1) * part_out]
    base += part_out
    whole[...] = functools.reduce(
        jnp.add, (dot(groups["mix"][c][...], groups["heads"][c][...], TT) for c in range(CHUNKS))
    )
    vec = functools.reduce(jnp.add, (v[...] for v in groups["vec"]))
    for owner, target in zip(owners, targets):
        start = pl.multiple_of(owner * width_own, 8)
        target[base : base + half_own, :] = jnp.concatenate(
            [whole[pl.ds(start, half_own), :], whole[pl.ds(start + half_own, half_own), :]],
            axis=1,
        )
        target[base + half_own : base + half_own + VEC_ROWS, :] = vec
    for k in range(4):
        sib_ref[k] = sib[k].astype(BF16)


def join_kernel(mine_ref, other_ref, *outs):
    for k, out in enumerate(outs):
        out[...] = (mine_ref[k] + other_ref[k].astype(F32)).astype(out.dtype)


def attend_back_heads(heads, offset, count_ref, refs, dqkv_ref, pair_ref):
    q_ref, k_ref, v_ref, kt_ref, oh_ref, back_ref = refs[:6]
    groups = [refs[6 + i * CHUNKS : 6 + (i + 1) * CHUNKS] for i in range(4)]
    head_refs, dhead_refs, dheadt_refs, prob_refs = groups
    visual = stream_is_visual()
    tokens = q_ref.shape[0]
    block = tokens // CHUNKS
    count = count_ref[0]
    one = oh_ref[...]
    back = back_ref[...]
    inside = same_group(LEVELS - 1 - iota((LEVELS, LEVELS), 0), iota((LEVELS, LEVELS), 1))
    extra = one_hot(iota((tokens, 16), 1) < 2)
    sublane = iota((16, block), 0)
    turned = [[], [], []]
    for n in range(heads):
        head = offset + n
        own = slice(head * HD, (head + 1) * HD)
        left = jnp.concatenate([v_ref[:, own], extra], axis=1)
        below = jnp.concatenate([back, kt_ref[own, :]], axis=0)
        dquery_t = []
        dkey = jnp.zeros((tokens, HD), F32)
        dvalue = jnp.zeros((tokens, HD), F32)
        pairs = jnp.zeros((LEVELS, LEVELS), F32)
        for c in range(CHUNKS):
            span = slice(c * block, (c + 1) * block)
            free = jnp.logical_not(visual)
            row_open = jnp.logical_or(free, iota((block, 1), 0) + c * block < count)
            lane_open = jnp.logical_or(free, iota((1, block), 1) + c * block < count)
            dout = dhead_refs[c][:, own] * row_open.astype(BF16)
            dout_t = dheadt_refs[c][own, :] * lane_open.astype(BF16)
            inner = -jnp.sum(
                dout_t.astype(F32) * head_refs[c][own, :].astype(F32), axis=0, keepdims=True
            )
            high = inner.astype(BF16).astype(F32)
            tail = jnp.where(sublane == 0, high, jnp.where(sublane == 1, inner - high, 0.0))
            centred = dot(left, jnp.concatenate([dout_t, tail.astype(BF16)], axis=0))
            prob = prob_refs[c][head]
            dscore = (prob.astype(F32) * centred).astype(BF16)
            both = dot(below, dscore)
            level = both[:LEVELS]
            level_high = level.astype(BF16)
            level_low = (level - level_high.astype(F32)).astype(BF16)
            one_part = one[span, :]
            pairs = pairs + dot(level_high, one_part) + dot(level_low, one_part)
            dquery_t.append(both[LEVELS:] * SCALE)
            dkey = dkey + dot(dscore, q_ref[span, own])
            dvalue = dvalue + dot(prob, dout)
        pair_ref[n] = jnp.where(inside, pairs, 0.0)
        turned[0].append(jnp.concatenate(dquery_t, axis=1))
        turned[1].append(dkey * SCALE)
        turned[2].append(dvalue)
        if n % 2 == 1 or n == heads - 1:
            start = n - n % 2
            wide = HD * len(turned[0])
            for m in range(3):
                joined = jnp.concatenate(turned[m], axis=0 if m == 0 else 1)
                if m == 0:
                    joined = jnp.transpose(joined)
                dqkv_ref[m, :, start * HD : start * HD + wide] = joined.astype(BF16)
            turned = [[], [], []]


def back_first_kernel(heads, count_ref, *refs):
    attend_back_heads(heads, 0, count_ref, refs[:-2], *refs[-2:])


def back_second_kernel(heads, offset, count_ref, first_ref, w_ref, visual_ref, stats_ref, *refs):
    steps = lax.axis_size("head")
    inner, refs = refs[: 6 + 4 * CHUNKS], refs[6 + 4 * CHUNKS :]
    dqkv_ref, pair_ref, sums_ref, part_ref = refs
    attend_back_heads(heads, offset, count_ref, inner, dqkv_ref, pair_ref)
    visual = stream_is_visual()
    tokens = visual_ref.shape[0]
    share = tokens // steps
    mean, scale = stats_ref[0:1, :], stats_ref[1:2, :]
    shift_sum = jnp.zeros(mean.shape, F32)
    gain_sum = jnp.zeros(mean.shape, F32)
    for k in range(steps):
        start = k * share
        rows = slice(start, start + share)
        part = jnp.zeros((share, mean.shape[1]), F32)
        for m in range(3):
            left = jnp.concatenate([first_ref[m, rows, :], dqkv_ref[m, rows, :]], axis=1)
            part = part + dot(left, w_ref[m], NT)
        part_ref[k] = part.astype(BF16)
        keep = jnp.logical_and(visual, iota((share, 1), 0) + start < count_ref[0]).astype(F32)
        kept = part * keep
        shift_sum = shift_sum + jnp.sum(kept, axis=0, keepdims=True)
        hat = (visual_ref[rows, :].astype(F32) - mean) * scale
        gain_sum = gain_sum + jnp.sum(kept * hat, axis=0, keepdims=True)
    sums_ref[...] = jnp.concatenate(
        [shift_sum, gain_sum, jnp.zeros((6, mean.shape[1]), F32)], axis=0
    )


def table_sums(pair_refs):
    table_width = NB_REL + 2 * NB_BOX
    sums = [[], [], []]
    for ref in pair_refs:
        for head in range(ref.shape[0]):
            turned = pltpu.roll(ref[head], LEVELS // 2 + 1, 1, stride=1, stride_axis=0)
            for n, (start, stop, unused_half, unused_offset) in enumerate(GROUPS):
                rows = turned[LEVELS - stop : LEVELS - start]
                sums[n].append(jnp.sum(rows, axis=0, keepdims=True))
    table = jnp.zeros((8, table_width), F32)
    offsets = LEVELS // 2 - iota((table_width, LEVELS), 1)
    for n, (unused_start, unused_stop, half, offset) in enumerate(GROUPS):
        missing = 8 - len(sums[n])
        stacked = jnp.concatenate(sums[n] + [jnp.zeros((missing, LEVELS), F32)], axis=0)
        table = table + picked(stacked, bucket_map(offsets, half, offset, table_width), NT)
    return table


def qkv_grad_kernel(fused, x_ref, first_ref, second_ref, pair_one, pair_two, *outs):
    tokens, width = x_ref.shape
    local_width = first_ref.shape[2] + second_ref.shape[2]
    table = table_sums((pair_one, pair_two))
    x = x_ref[...]

    def columns(m):
        return jnp.concatenate([first_ref[m], second_ref[m]], axis=1)

    if not fused:
        grad_ref, table_ref = outs
        table_ref[...] = table
        for m in range(3):
            grad_ref[m] = dot(x, columns(m), TN).astype(BF16)
        return
    mine_ref, sib_ref, whole = outs
    width_own = width // 8
    padded = jnp.concatenate(
        [
            jnp.concatenate([table, jnp.zeros((8, local_width - table.shape[1]), F32)], axis=1),
            jnp.zeros((8, local_width), F32),
        ],
        axis=0,
    )
    for m in range(3):
        whole[m] = dot(x, columns(m), TN)
    for half, target in ((1, sib_ref), (0, mine_ref)):
        for k in range(4):
            rows = pl.ds(pl.multiple_of(owner_of(half, k) * width_own, 8), width_own)
            target[k] = jnp.concatenate([whole[m, rows, :] for m in range(3)] + [padded], axis=0).astype(
                target.dtype
            )


def finish_grads_kernel(hidden_width, *refs):
    ffn_refs, qkv_refs, outs = refs[:4], refs[4:8], refs[8:]
    grad_in, grad_out, grad_ow, bias_in, grad_qkv, grad_table = outs[:6]
    total = functools.reduce(jnp.add, (ref[...].astype(F32) for ref in ffn_refs))
    width = total.shape[1]
    part_in = grad_in.shape[0]
    part_out = grad_out.shape[0]
    half_own = grad_ow.shape[1] // 2
    local_width = grad_ow.shape[0]
    parts = hidden_width // width
    place = lax.axis_index("dp") * lax.axis_size("head") + lax.axis_index("head")
    grad_in[...] = jnp.concatenate(
        [total[p * part_in : (p + 1) * part_in] for p in range(parts)], axis=1
    )
    base = parts * part_in
    grad_out[...] = total[base : base + part_out]
    base += part_out
    packed = total[base : base + half_own]
    grad_ow[...] = jnp.transpose(
        jnp.concatenate([packed[:, :local_width], packed[:, local_width:]], axis=0)
    )
    vec = total[base + half_own :]
    lane = iota((width, 128), 0)
    column = iota((width, 128), 1)
    own = picked(vec, one_hot((lane == place * part_in + column) & (column < part_in)))
    for row, out in zip((0, 1, 2, 7, 8, 9), outs[6:]):
        out[...] = own[row : row + 1, :part_in]
    first = place * part_out
    wide = picked(
        vec, one_hot((lane == lax.rem(first, width) + column) & (column < part_out))
    )
    row = iota((VEC_ROWS, 128), 0)
    chosen = jnp.where(row == 3 + lax.div(first, width), wide, 0.0)
    bias_in[...] = jnp.sum(chosen, axis=0, keepdims=True)[:, :part_out]
    grads = functools.reduce(jnp.add, (ref[...].astype(F32) for ref in qkv_refs))
    width_own = grad_qkv.shape[1]
    for m in range(3):
        grad_qkv[m] = grads[m * width_own : (m + 1) * width_own]
    table = grads[3 * width_own : 3 * width_own + 8]
    buckets = grad_table.shape[1]
    lane = iota((local_width, 128), 0)
    column = iota((local_width, 128), 1)
    start = lax.axis_index("dp") * buckets
    cut = picked(table, one_hot((lane == start + column) & (column < buckets)))
    grad_table[...] = cut[: grad_table.shape[0], :buckets]


def finish_inputs_kernel(steps, sums, count_ref, visual_ref, stats_ref, *refs):
    share_refs, refs = refs[:CHUNKS], refs[CHUNKS:]
    part_ref, refs = refs[0], refs[1:]
    sum_refs, refs = refs[:sums], refs[sums:]
    text_ref, grad_ref, gain_ref, shift_ref = refs
    head_rank = lax.axis_index("head")
    share = text_ref.shape[0]
    half = steps // 2
    text, visual = (
        functools.reduce(jnp.add, (part_ref[k].astype(F32) for k in range(start, start + half)))
        for start in (0, half)
    )
    text_ref[...] = functools.reduce(jnp.add, (ref[...] for ref in share_refs)) + text
    total = functools.reduce(jnp.add, (ref[...] for ref in sum_refs))
    mean, scale, gain, number = (stats_ref[i : i + 1, :] for i in range(4))
    start = pl.multiple_of(head_rank * share, share)
    keep = (iota((share, 1), 0) + start < count_ref[0]).astype(F32)
    hat = (visual_ref[pl.ds(start, share), :].astype(F32) - mean) * keep * scale
    dnormed = visual * keep
    shift_gradient, gain_gradient = total[0:1], total[1:2]
    shift_ref[...] = shift_gradient
    gain_ref[...] = gain_gradient
    grad_ref[...] = (
        keep
        * scale
        * gain
        * (dnormed - shift_gradient / number - hat * gain_gradient / number)
    )


def swap(value, axis, mask):
    size = lax.axis_size(axis)
    return lax.ppermute(value, axis, [(i, i ^ mask) for i in range(size)])


def after(value, *earlier):
    return lax.optimization_barrier((value, *earlier))[0]


def gather_heads(chunks):
    return [[piece] + [swap(piece, "head", k) for k in (1, 2, 3)] for piece in chunks]


def owned_blocks(mine, sib, name, earlier=()):
    shape = mine.shape[1:]
    own, *send = call(
        join_kernel,
        name,
        2,
        [(shape, F32)] + [(shape, BF16)] * 3,
        [mine, after(swap(sib, "dp", 1), *earlier)],
    )
    return [own] + [swap(b, "dp", (k + 1) << 1) for k, b in enumerate(send)], own


def per_device(
    text_in,
    visual_in,
    visual_count,
    line_index,
    box_index,
    qkv_weight,
    bias_table,
    out_weight,
    out_bias,
    norm1_gain,
    norm1_shift,
    ffn_weight_in,
    ffn_bias_in,
    ffn_weight_out,
    ffn_bias_out,
    norm2_gain,
    norm2_shift,
    batch_gain,
    batch_shift,
    cotangent,
):
    tokens, width = text_in.shape
    local_width = qkv_weight.shape[2]
    heads_local = local_width // HD
    head_count = lax.axis_size("head")
    dp_count = lax.axis_size("dp")
    head_rank = lax.axis_index("head")
    dp_rank = lax.axis_index("dp")
    fused = head_count == 4 and dp_count == 8
    share = tokens // head_count
    block = tokens // CHUNKS
    hidden_width = ffn_weight_in.shape[1]
    table_width = bias_table.shape[1]
    part_in = width // (dp_count * head_count)
    part_out = hidden_width // (dp_count * head_count)
    weight = jnp.transpose(qkv_weight, (1, 0, 2))
    row_vectors = [
        value.reshape(1, width)
        for value in (
            out_bias,
            norm1_gain,
            norm1_shift,
            ffn_bias_out,
            norm2_gain,
            norm2_shift,
            batch_gain,
            batch_shift,
        )
    ]

    packed_shape = ((8, width), F32)
    (packed,) = call(
        stats_kernel, "stats", 2, [packed_shape], [visual_in], visual_count
    )
    if fused:
        (packed,) = call(
            join_stats_kernel, "join_stats", 1, [packed_shape], [packed, swap(packed, "dp", 1)]
        )
        packed = [packed] + [swap(packed, "dp", k) for k in (2, 4, 6)]
    else:
        gathered = lax.all_gather(packed, "dp")
        packed = [gathered[i] for i in range(dp_count)]
    one, back, tab, small, bias_in = call(
        prep_kernel,
        "prep",
        2,
        [
            ((tokens, LEVELS), BF16),
            ((LEVELS, tokens), BF16),
            ((LEVELS, heads_local * LEVELS), BF16),
            ((8, width), F32),
            ((8, width), F32),
        ],
        [line_index, box_index, bias_table, ffn_bias_in.reshape(1, hidden_width)] + row_vectors,
        visual_count,
    )

    rows = ((tokens, local_width), BF16)
    turned = ((local_width, tokens), BF16)
    chunk_outs = [((local_width, block), BF16), ((heads_local, tokens, block), BF16)]
    stats, x, q, k, v, kt, vt, heads_one, prob_one = call(
        functools.partial(attend_first_kernel, len(packed)),
        "attend_first",
        6,
        [packed_shape, ((tokens, width), BF16), rows, rows, rows, turned, turned] + chunk_outs,
        [text_in, visual_in, small, weight, tab, one] + packed,
        visual_count,
        final=(1,),
    )
    heads_two, prob_two = call(
        functools.partial(attend_chunk, 1),
        "attend_second",
        3,
        chunk_outs,
        [q, k, vt, tab, one],
        visual_count,
    )
    heads = (heads_one, heads_two)
    if fused:
        pieces = gather_heads(heads)
    else:
        pieces = []
        for piece in heads:
            gathered = lax.all_gather(piece, "head")
            pieces.append([gathered[i] for i in range(head_count)])

    results = []
    for c in range(CHUNKS):
        text = after(text_in, results[-1][-1]) if results else text_in
        results.append(
            call(
                functools.partial(ffn_kernel, c, fused, len(pieces[c])),
                f"ffn_{c}",
                9,
                [
                    ((block, width), BF16),
                    ((share, width), F32),
                    ((block, hidden_width), BF16),
                    ((block, hidden_width), BF16),
                    ((block, width), BF16),
                    ((block, width), BF16),
                    ((block, width), BF16),
                    ((block, local_width), BF16),
                    ((local_width, block), BF16),
                    ((VEC_ROWS, width), F32),
                ],
                [text, cotangent, out_weight, ffn_weight_in, ffn_weight_out, small, bias_in]
                + list(pieces[c]),
                scratch=[pltpu.VMEM((block, hidden_width), F32)],
            )
        )
    out, dh_share, act, dpre, low, branch, mix, dheads, dheads_t, vec = zip(*results)
    if fused:
        block_rows = hidden_width // width * part_in + part_out + width // dp_count // 2 + VEC_ROWS
        layer_out, mine, sib = call(
            weight_grad_kernel,
            "weight_grad",
            5,
            [
                ((tokens, width), BF16),
                ((4, block_rows, width), F32),
                ((4, block_rows, width), BF16),
            ],
            [*out, *act, *dpre, *low, *branch, *mix, *heads, *vec],
            scratch=[
                pltpu.VMEM((4, block_rows, width), F32),
                pltpu.VMEM((width, local_width), F32),
            ],
            final=(0,),
        )
        ffn_blocks, ffn_joined = owned_blocks(mine, sib, "join_ffn")

    first_heads = min(2, heads_local - 1)
    last_heads = heads_local - first_heads
    inner = [q, k, v, kt, one, back, *heads, *dheads, *dheads_t, prob_one, prob_two]
    first, pairs_one = call(
        functools.partial(back_first_kernel, first_heads),
        "back_first",
        6,
        [((3, tokens, first_heads * HD), BF16), ((first_heads, LEVELS, LEVELS), F32)],
        inner,
        visual_count,
    )
    if fused:
        first = after(first, ffn_joined)
    second, pairs_two, sums, parts = call(
        functools.partial(back_second_kernel, last_heads, first_heads),
        "back_second",
        5,
        [
            ((3, tokens, last_heads * HD), BF16),
            ((last_heads, LEVELS, LEVELS), F32),
            packed_shape,
            ((head_count, share, width), BF16),
        ],
        [first, weight, visual_in, stats] + inner,
        visual_count,
    )
    received = lax.all_to_all(parts, "head", 0, 0, tiled=True)
    if fused:
        for axis, mask in (("dp", 1), ("dp", 2), ("dp", 4), ("head", 1)):
            sums = sums + swap(sums, axis, mask)
        sums = [sums, swap(sums, "head", 2)]
        block_rows = 3 * (width // dp_count) + 16
        mine, sib = call(
            functools.partial(qkv_grad_kernel, True),
            "qkv_grad",
            3,
            [((4, block_rows, local_width), F32), ((4, block_rows, local_width), BF16)],
            [x, first, second, pairs_one, pairs_two],
            scratch=[pltpu.VMEM((3, width, local_width), F32)],
        )
        qkv_blocks, unused_joined = owned_blocks(mine, sib, "join_qkv", ffn_blocks)
        one_row = ((1, part_in), F32)
        grad_in, grad_out, grad_ow, grad_bias_in, grad_qkv, grad_table, *own = call(
            functools.partial(finish_grads_kernel, hidden_width),
            "finish_grads",
            2,
            [
                ((part_in, hidden_width), F32),
                ((part_out, width), F32),
                ((local_width, width // dp_count), F32),
                ((1, part_out), F32),
                ((3, width // dp_count, local_width), F32),
                ((heads_local, table_width // dp_count), F32),
            ]
            + [one_row] * 6,
            ffn_blocks + qkv_blocks,
            final=range(12),
        )
        grad_bias_in = grad_bias_in.reshape(part_out)
        grad_qkv = jnp.transpose(grad_qkv, (1, 0, 2))
        own = [value.reshape(part_in) for value in own]
    else:
        layer_out = jnp.concatenate(out, axis=0)
        act, dpre, low, branch, mix = (
            jnp.concatenate(value, axis=0) for value in (act, dpre, low, branch, mix)
        )

        def scatter(value, dimension):
            return lax.psum_scatter(
                value.astype(BF16), "dp", scatter_dimension=dimension, tiled=True
            ).astype(F32)

        def own_columns(value, part):
            split = value.reshape(tokens, dp_count, head_count, part)
            return lax.dynamic_index_in_dim(split, head_rank, 2, keepdims=False).reshape(
                tokens, dp_count * part
            )

        grad_in = scatter(dot(own_columns(low, part_in), dpre, TN), 0)
        grad_out = scatter(dot(own_columns(act, part_out), branch, TN), 0)
        grad_ow = scatter(dot(jnp.concatenate(heads, axis=1), mix), 1)
        vec = lax.psum((vec[0] + vec[1]).astype(BF16), "dp").astype(F32)
        place = dp_rank * head_count + head_rank
        own = [
            lax.dynamic_slice_in_dim(vec[row], place * part_in, part_in, 0)
            for row in (0, 1, 2, 7, 8, 9)
        ]
        grad_bias_in = lax.dynamic_slice_in_dim(
            vec[3 : 3 + hidden_width // width].reshape(hidden_width), place * part_out, part_out, 0
        )
        sums = [lax.psum(sums, ("dp", "head"))]
        grad, table = call(
            functools.partial(qkv_grad_kernel, False),
            "qkv_grad",
            3,
            [((3, width, local_width), BF16), ((8, table_width), F32)],
            [x, first, second, pairs_one, pairs_two],
        )
        grad_qkv = jnp.transpose(scatter(grad, 1), (1, 0, 2))
        grad_table = scatter(table[:heads_local], 1)

    grad_text, grad_visual, gain_gradient, shift_gradient = call(
        functools.partial(finish_inputs_kernel, head_count, len(sums)),
        "finish_inputs",
        2,
        [((share, width), F32)] * 2 + [((1, width), F32)] * 2,
        [visual_in, stats, *dh_share, received, *sums],
        visual_count,
        final=range(4),
    )
    return (
        layer_out,
        grad_text,
        grad_visual,
        grad_qkv,
        grad_table,
        grad_ow,
        own[0],
        own[1],
        own[2],
        grad_in,
        grad_bias_in,
        grad_out,
        own[3],
        own[4],
        own[5],
        gain_gradient.reshape(width),
        shift_gradient.reshape(width),
    )


def solution(mesh):
    in_specs = (
        P("dp", None),
        P("dp", None),
        P("dp"),
        P(None, "dp"),
        P(None, None, "dp"),
        P(None, None, "head"),
        P("head", None),
        P(),
        P(),
        P(),
        P(),
        P(),
        P(),
        P(),
        P(),
        P(),
        P(),
        P(),
        P(),
        P("dp", None),
    )
    out_specs = (
        P("dp", None),
        P(("dp", "head"), None),
        P(("dp", "head"), None),
        P("dp", None, "head"),
        P("head", "dp"),
        P("head", "dp"),
        P(("dp", "head")),
        P(("dp", "head")),
        P(("dp", "head")),
        P(("dp", "head"), None),
        P(("dp", "head")),
        P(("dp", "head"), None),
        P(("dp", "head")),
        P(("dp", "head")),
        P(("dp", "head")),
        P(),
        P(),
    )
    return jax.shard_map(
        per_device, mesh=mesh, in_specs=in_specs, out_specs=out_specs, check_vma=False
    )
```

```python
import functools

import jax
import jax.numpy as jnp
from jax import lax
from jax.experimental import pallas as pl
from jax.experimental.pallas import tpu as pltpu
from jax.sharding import PartitionSpec as P

HD = 64
NB_REL = 32
NB_BOX = 16
LINES = 48
BOXES = 32

EPSILON = 1e-05
FLOOR_SCORE = -1000000000.0
SCALE = HD ** (-0.5)
LEVELS = 128
MASK_LANE = LINES + 2 * BOXES
VMEM_LIMIT = 12 * 1024 * 1024
VEC_ROWS = 16
CHUNKS = 2

F32 = jnp.float32
BF16 = jnp.bfloat16

NN = (((1,), (0,)), ((), ()))
NT = (((1,), (1,)), ((), ()))
TN = (((0,), (0,)), ((), ()))
TT = (((0,), (1,)), ((), ()))


def dot(left, right, dims=NN):
    return lax.dot_general(left, right, dims, preferred_element_type=F32)


def iota(shape, axis):
    return lax.broadcasted_iota(jnp.int32, shape, axis)


def one_hot(condition):
    return condition.astype(F32).astype(BF16)


def thirds(value):
    high = value.astype(BF16)
    rest = value - high.astype(F32)
    middle = rest.astype(BF16)
    return high, middle, (rest - middle.astype(F32)).astype(BF16)


def picked(value, selector, dims=NN):
    return functools.reduce(jnp.add, (dot(part, selector, dims) for part in thirds(value)))


def call(kernel, name, micros, outs, args, count=None, scratch=(), final=()):
    vmem = pl.BlockSpec(memory_space=pltpu.VMEM)
    scalars = [] if count is None else [count]
    return pl.pallas_call(
        kernel,
        out_shape=tuple(
            jax.ShapeDtypeStruct(*entry) if place in final else pltpu.VMEM(*entry)
            for place, entry in enumerate(outs)
        ),
        in_specs=[pl.BlockSpec(memory_space=pltpu.SMEM)] * len(scalars) + [vmem] * len(args),
        out_specs=tuple(vmem for entry in outs),
        scratch_shapes=list(scratch),
        compiler_params=pltpu.CompilerParams(vmem_limit_bytes=VMEM_LIMIT),
        cost_estimate=pl.CostEstimate(
            flops=int(micros * 1e9), bytes_accessed=int(micros * 3e6), transcendentals=0
        ),
        name=name,
    )(*scalars, *[pltpu.with_memory_space_constraint(a, pltpu.VMEM) for a in args])


def stream_is_visual():
    return lax.axis_index("head") >= lax.axis_size("head") // 2


def stats_kernel(count_ref, visual_ref, out_ref):
    tokens, width = visual_ref.shape
    number = count_ref[0].astype(F32)
    keep = (iota((tokens, 1), 0) < count_ref[0]).astype(F32)
    visual = visual_ref[...].astype(F32)
    total = jnp.sum(visual * keep, axis=0, keepdims=True)
    centred = (visual - total / number) * keep
    spread = jnp.sum(centred * centred, axis=0, keepdims=True)
    out_ref[...] = jnp.concatenate(
        [total, spread, jnp.full((1, width), number, F32), jnp.zeros((5, width), F32)], axis=0
    )


def joined_stats(blocks):
    total = functools.reduce(jnp.add, (b[0:1] for b in blocks))
    number = functools.reduce(jnp.add, (b[2:3] for b in blocks))
    mean = total / number
    spread = functools.reduce(
        jnp.add, (b[1:2] + b[2:3] * (b[0:1] / b[2:3] - mean) ** 2 for b in blocks)
    )
    return total, spread, number


def join_stats_kernel(*refs):
    total, spread, number = joined_stats([ref[...] for ref in refs[:-1]])
    refs[-1][...] = jnp.concatenate(
        [total, spread, number, jnp.zeros((5, total.shape[1]), F32)], axis=0
    )


GROUPS = (
    (0, LINES, NB_REL // 2, 0),
    (LINES, LINES + BOXES, NB_BOX // 2, NB_REL),
    (LINES + BOXES, LINES + 2 * BOXES, NB_BOX // 2, NB_REL + NB_BOX),
)


def bucket_map(level, half, offset, table_width):
    bucket = jnp.clip(level, -half, half - 1) + half + offset
    return one_hot(bucket == iota((table_width, LEVELS), 0))


def same_group(row, lane):
    inside = jnp.zeros(row.shape, jnp.bool_)
    for start, stop, unused_half, unused_offset in GROUPS:
        inside = inside | ((row >= start) & (row < stop) & (lane >= start) & (lane < stop))
    return inside


def by_level(level, line, across, down):
    wanted = jnp.where(level < LINES, line, jnp.where(level < LINES + BOXES, across, down))
    return wanted == level


def prep_kernel(count_ref, line_ref, box_ref, table_ref, bias_ref, *refs):
    oh_ref, back_ref, tab_ref, small_ref, b1_ref = refs[8:]
    width = small_ref.shape[1]
    small_ref[...] = jnp.concatenate([ref[...] for ref in refs[:8]], axis=0)
    for c in range(bias_ref.shape[1] // width):
        b1_ref[c : c + 1, :] = bias_ref[:, c * width : (c + 1) * width]
    visual = stream_is_visual()
    tokens = line_ref.shape[1]
    heads_local, table_width = table_ref.shape
    line = jnp.where(visual, line_ref[1:2, :], line_ref[0:1, :])
    across = jnp.where(visual, box_ref[1, 0:1, :], box_ref[0, 0:1, :]) + LINES
    down = jnp.where(visual, box_ref[1, 1:2, :], box_ref[0, 1:2, :]) + (LINES + BOXES)
    level = iota((LEVELS, tokens), 0)
    back_ref[...] = one_hot(by_level(LEVELS - 1 - level, line, across, down))
    closed = jnp.logical_and(visual, iota((LEVELS, tokens), 1) >= count_ref[0])
    mask = jnp.where(closed, FLOOR_SCORE, 0.0)
    flags = by_level(level, line, across, down).astype(F32)
    oh_ref[...] = jnp.transpose(jnp.where(level == MASK_LANE, mask, flags)).astype(BF16)
    row = iota((LEVELS, LEVELS), 0)
    lane = iota((LEVELS, LEVELS), 1)
    inside = same_group(row, lane)
    offsets = iota((table_width, LEVELS), 1) - LEVELS // 2
    table = table_ref[...]
    spread = [
        picked(table, bucket_map(offsets, half, offset, table_width))
        for unused_start, unused_stop, half, offset in GROUPS
    ]
    for head in range(heads_local):
        rows = [jnp.broadcast_to(s[head : head + 1, :], (LEVELS, LEVELS)) for s in spread]
        chosen = jnp.where(row < LINES, rows[0], jnp.where(row < LINES + BOXES, rows[1], rows[2]))
        turned = pltpu.roll(chosen, LEVELS // 2, 1, stride=1, stride_axis=0)
        pairs = jnp.where(inside, turned, 0.0)
        high = jnp.where((lane == MASK_LANE) & (row < LINES), 1.0, pairs)
        tab_ref[:, head * LEVELS : (head + 1) * LEVELS] = high.astype(BF16)


def attend_chunk(chunk, count_ref, q_ref, k_ref, vt_ref, tab_ref, oh_ref, heads_ref, prob_ref):
    visual = stream_is_visual()
    tokens, local_width = q_ref.shape
    heads_local = local_width // HD
    block = heads_ref.shape[1]
    span = slice(chunk * block, (chunk + 1) * block)
    place = iota((1, block), 1) + chunk * block
    allowed = jnp.logical_or(jnp.logical_not(visual), place < count_ref[0]).astype(F32)
    one = oh_ref[...]
    left = dot(oh_ref[span, :], tab_ref[...]).astype(BF16)
    ones = jnp.ones((16, tokens), F32).astype(BF16)

    def scores(head):
        own = slice(head * HD, (head + 1) * HD)
        query = q_ref[span, own] * jnp.asarray(SCALE, BF16)
        right = jnp.concatenate([left[:, head * LEVELS : (head + 1) * LEVELS], query], axis=1)
        return dot(jnp.concatenate([one, k_ref[:, own]], axis=1), right, NT)

    following = scores(0)
    for head in range(heads_local):
        own = slice(head * HD, (head + 1) * HD)
        current = following
        if head + 1 < heads_local:
            following = scores(head + 1)
        shifted = jnp.exp(current - jnp.max(current, axis=0, keepdims=True))
        mixed = dot(jnp.concatenate([vt_ref[own, :], ones], axis=0), shifted.astype(BF16))
        share = 1.0 / mixed[HD : HD + 1]
        prob_ref[head] = (shifted * share).astype(BF16)
        heads_ref[own, :] = (mixed[:HD] * (share * allowed)).astype(BF16)


def attend_first_kernel(pieces, count_ref, text_ref, visual_ref, small_ref, w_ref, tab_ref, oh_ref, *refs):
    piece_refs, refs = refs[:pieces], refs[pieces:]
    stats_ref, x_ref, q_ref, k_ref, v_ref, kt_ref, vt_ref, heads_ref, prob_ref = refs
    visual = stream_is_visual()
    tokens, width = text_ref.shape
    total, spread, number = joined_stats([ref[...] for ref in piece_refs])
    mean = total / number
    scale = lax.rsqrt(spread / number + EPSILON)
    gain, shift = small_ref[6:7, :], small_ref[7:8, :]
    stats_ref[...] = jnp.concatenate(
        [mean, scale, gain, number, jnp.zeros((4, width), F32)], axis=0
    )

    @pl.when(visual)
    def _():
        keep = (iota((tokens, 1), 0) < count_ref[0]).astype(F32)
        centred = (visual_ref[...].astype(F32) - mean) * keep
        x_ref[...] = ((centred * scale * gain + shift) * keep).astype(BF16)

    @pl.when(jnp.logical_not(visual))
    def _():
        x_ref[...] = text_ref[...]

    x = x_ref[...]
    q_ref[...] = dot(x, w_ref[0]).astype(BF16)
    k_ref[...] = dot(x, w_ref[1]).astype(BF16)
    v_ref[...] = dot(x, w_ref[2]).astype(BF16)
    kt_ref[...] = dot(w_ref[1], x, TT).astype(BF16)
    vt_ref[...] = dot(w_ref[2], x, TT).astype(BF16)
    attend_chunk(0, count_ref, q_ref, k_ref, vt_ref, tab_ref, oh_ref, heads_ref, prob_ref)


ERF_P = 0.3275911 * 0.7071067811865476
ERF_A = (0.254829592, -0.284496736, 1.421413741, -1.453152027, 1.061405429)


def gelu_parts(pre):
    t = 1.0 / (1.0 + ERF_P * jnp.abs(pre))
    bell = jnp.exp(-0.5 * pre * pre)
    poly = 0.5 * ERF_A[4]
    for coefficient in ERF_A[3::-1]:
        poly = poly * t + 0.5 * coefficient
    tail = poly * t * bell
    cdf = jnp.where(pre >= 0.0, 1.0 - tail, tail)
    return pre * cdf, cdf + pre * (bell * 0.3989422804014327)


def normed_rows(hidden):
    average = jnp.mean(hidden, axis=-1, keepdims=True)
    centred = hidden - average
    scale = lax.rsqrt(jnp.mean(centred * centred, axis=-1, keepdims=True) + EPSILON)
    return centred * scale, scale


def normed_back(upstream, hat, scale, gain):
    scaled = upstream * gain
    return scale * (
        scaled
        - jnp.mean(scaled, axis=-1, keepdims=True)
        - hat * jnp.mean(scaled * hat, axis=-1, keepdims=True)
    )


def ffn_kernel(chunk, relative, pieces, *refs):
    (text_ref, cot_ref, wo, w1, w2, small_ref, b1_ref), refs = refs[:7], refs[7:]
    piece_refs, refs = refs[:pieces], refs[pieces:]
    out_ref, share_ref, act_ref, dpre_ref, low_ref, branch_ref, mix_ref = refs[:7]
    dheads_ref, dheadst_ref, vec_ref, slope = refs[7:]
    local_width, block = piece_refs[0].shape
    width = text_ref.shape[1]
    hidden_width = w1.shape[1]
    head_rank = lax.axis_index("head")
    out_bias, gain1, shift1, b2, gain2, shift2 = (small_ref[i : i + 1, :] for i in range(6))
    parts = hidden_width // width
    share = share_ref.shape[0]
    rows = slice(chunk * block, (chunk + 1) * block)
    own_rows = pl.ds(pl.multiple_of(head_rank * local_width, 64), local_width)

    sources = [
        (ref[...], head_rank ^ index if relative else index)
        for index, ref in enumerate(piece_refs)
    ]
    mixed = text_ref[rows, :].astype(F32) + out_bias
    for piece, source in sources:
        wo_rows = pl.ds(pl.multiple_of(source * local_width, 64), local_width)
        mixed = mixed + dot(piece, wo[wo_rows, :], TN)
    hat1, scale1 = normed_rows(mixed)
    after = hat1 * gain1 + shift1
    after_low = after.astype(BF16)
    low_ref[...] = after_low
    branch = jnp.zeros((block, width), F32)
    for c in range(parts):
        cols = slice(c * width, (c + 1) * width)
        act, slope[:, cols] = gelu_parts(dot(after_low, w1[:, cols]) + b1_ref[c : c + 1, :])
        act = act.astype(BF16)
        act_ref[:, cols] = act
        branch = branch + dot(act, w2[cols, :])
    hat2, scale2 = normed_rows(after + (branch + b2))
    out_ref[...] = (hat2 * gain2 + shift2).astype(BF16)
    upstream = cot_ref[rows, :].astype(F32)
    dh_two = normed_back(upstream, hat2, scale2, gain2)
    dbranch = dh_two.astype(BF16)
    branch_ref[...] = dbranch
    vec = [None] * 3
    dy = dh_two
    for c in range(parts):
        cols = slice(c * width, (c + 1) * width)
        dpre = (dot(dbranch, w2[cols, :], NT) * slope[:, cols]).astype(BF16)
        dpre_ref[:, cols] = dpre
        vec.append(dpre.astype(F32))
        dy = dy + dot(dpre, w1[:, cols], NT)
    dh_one = normed_back(dy, hat1, scale1, gain1)
    vec[:3] = [dh_one, dy * hat1, dy]
    vec += [dbranch.astype(F32), upstream * hat2, upstream]
    sums = [jnp.sum(v, axis=0, keepdims=True) for v in vec]
    vec_ref[...] = jnp.concatenate(
        sums + [jnp.zeros((VEC_ROWS - len(sums), width), F32)], axis=0
    )
    share_ref[...] = jnp.zeros_like(share_ref)
    per_block = block // share
    for part in range(per_block):

        @pl.when(head_rank == chunk * per_block + part)
        def _():
            share_ref[...] = dh_one[part * share : (part + 1) * share]

    dmix = dh_one.astype(BF16)
    mix_ref[...] = dmix
    dheads_ref[...] = dot(dmix, wo[own_rows, :], NT).astype(BF16)
    dheadst_ref[...] = dot(wo[own_rows, :], dmix, NT).astype(BF16)


def owner_of(half, step):
    place = lax.axis_index("dp")
    core = place & 1
    return (((place >> 1) ^ step) << 1) | (core if half == 0 else 1 - core)


def own_order():
    return [owner_of(half, step) for half in range(2) for step in range(4)]


def weight_grad_in_kernel(*refs):
    head_rank = lax.axis_index("head")
    low_refs, dpre_refs, vec_refs = (refs[i * CHUNKS : (i + 1) * CHUNKS] for i in range(3))
    mine_ref, sib_ref = refs[3 * CHUNKS :]
    width = low_refs[0].shape[1]
    parts = dpre_refs[0].shape[1] // width
    width_own = width // 8
    part_in = width_own // 4
    lane = iota((part_in, width), 1)
    row = iota((part_in, width), 0)
    pick = jnp.concatenate(
        [
            (lane == owner * width_own + head_rank * part_in + row).astype(F32)
            for owner in own_order()
        ],
        axis=0,
    ).astype(BF16)
    low_t = [dot(pick, low[...], NT).astype(BF16) for low in low_refs]
    grads = []
    for p in range(parts):
        cols = slice(p * width, (p + 1) * width)
        grads.append(
            functools.reduce(
                jnp.add, (dot(low_t[c], dpre_refs[c][:, cols]) for c in range(CHUNKS))
            )
        )
    vec = functools.reduce(jnp.add, (v[...] for v in vec_refs))
    for n in range(8):
        rows = slice(n * part_in, (n + 1) * part_in)
        block = jnp.concatenate([grad[rows] for grad in grads] + [vec], axis=0)
        target = mine_ref if n < 4 else sib_ref
        target[n % 4] = block.astype(target.dtype)


def weight_grad_out_kernel(*refs):
    head_rank = lax.axis_index("head")
    names = ("out", "act", "branch", "mix", "heads")
    groups = {name: refs[i * CHUNKS : (i + 1) * CHUNKS] for i, name in enumerate(names)}
    layer_ref, mine_ref, sib_ref, whole = refs[len(names) * CHUNKS :]
    block, width = groups["out"][0].shape
    hidden_width = groups["act"][0].shape[1]
    owners = own_order()
    width_own = width // 8
    window = hidden_width // 8
    part_out = window // 4
    half_own = width_own // 2
    for c in range(CHUNKS):
        layer_ref[c * block : (c + 1) * block, :] = groups["out"][c][...]
    whole[...] = functools.reduce(
        jnp.add, (dot(groups["mix"][c][...], groups["heads"][c][...], TT) for c in range(CHUNKS))
    )
    pick = one_hot(
        iota((part_out, window), 1) == head_rank * part_out + iota((part_out, window), 0)
    )
    grad = jnp.zeros((8 * part_out, width), F32)
    for c in range(CHUNKS):
        stacked = []
        for owner in owners:
            cols = pl.ds(pl.multiple_of(owner * window, 128), window)
            stacked.append(dot(pick, groups["act"][c][:, cols], NT).astype(BF16))
        grad = grad + dot(jnp.concatenate(stacked, axis=0), groups["branch"][c][...])
    for n, owner in enumerate(owners):
        start = pl.multiple_of(owner * width_own, 8)
        packed = jnp.concatenate(
            [whole[pl.ds(start, half_own), :], whole[pl.ds(start + half_own, half_own), :]],
            axis=1,
        )
        target = mine_ref if n < 4 else sib_ref
        target[n % 4] = jnp.concatenate(
            [grad[n * part_out : (n + 1) * part_out], packed], axis=0
        ).astype(target.dtype)


X_FIRST = ((0, 2), (1, 3))
Y_FIRST = ((0, 1), (2, 3))


def join_cores_kernel(plans, *refs):
    mine_ref, other_ref, outs = refs[0], refs[1], refs[2:]
    start = 0
    for (keep, send), keep_ref, send_ref in zip(plans, outs[::2], outs[1::2]):
        rows = slice(start, start + keep_ref.shape[1])
        start = rows.stop
        for places, out in ((keep, keep_ref), (send, send_ref)):
            for n, place in enumerate(places):
                total = mine_ref[place, rows, :] + other_ref[place, rows, :].astype(F32)
                out[n] = total.astype(out.dtype)


def join_chips_kernel(*refs):
    count = len(refs) // 4
    ins, outs = refs[: 2 * count], refs[2 * count :]
    for n in range(count):
        keep, other = ins[2 * n : 2 * n + 2]
        for m, out in enumerate(outs[2 * n : 2 * n + 2]):
            out[...] = (keep[m] + other[m].astype(F32)).astype(out.dtype)


def attend_back_heads(heads, offset, count_ref, refs, dqkv_ref, pair_ref):
    q_ref, k_ref, v_ref, kt_ref, oh_ref, back_ref = refs[:6]
    groups = [refs[6 + i * CHUNKS : 6 + (i + 1) * CHUNKS] for i in range(4)]
    head_refs, dhead_refs, dheadt_refs, prob_refs = groups
    visual = stream_is_visual()
    tokens = q_ref.shape[0]
    block = tokens // CHUNKS
    count = count_ref[0]
    one = oh_ref[...]
    back = back_ref[...]
    inside = same_group(LEVELS - 1 - iota((LEVELS, LEVELS), 0), iota((LEVELS, LEVELS), 1))
    extra = one_hot(iota((tokens, 16), 1) < 2)
    sublane = iota((16, block), 0)
    turned = [[], [], []]
    for n in range(heads):
        head = offset + n
        own = slice(head * HD, (head + 1) * HD)
        left = jnp.concatenate([v_ref[:, own], extra], axis=1)
        below = jnp.concatenate([back, kt_ref[own, :]], axis=0)
        dquery_t = []
        dkey = jnp.zeros((tokens, HD), F32)
        dvalue = jnp.zeros((tokens, HD), F32)
        pairs = jnp.zeros((LEVELS, LEVELS), F32)
        for c in range(CHUNKS):
            span = slice(c * block, (c + 1) * block)
            free = jnp.logical_not(visual)
            row_open = jnp.logical_or(free, iota((block, 1), 0) + c * block < count)
            lane_open = jnp.logical_or(free, iota((1, block), 1) + c * block < count)
            dout = dhead_refs[c][:, own] * row_open.astype(BF16)
            dout_t = dheadt_refs[c][own, :] * lane_open.astype(BF16)
            inner = -jnp.sum(
                dout_t.astype(F32) * head_refs[c][own, :].astype(F32), axis=0, keepdims=True
            )
            high = inner.astype(BF16).astype(F32)
            tail = jnp.where(sublane == 0, high, jnp.where(sublane == 1, inner - high, 0.0))
            centred = dot(left, jnp.concatenate([dout_t, tail.astype(BF16)], axis=0))
            prob = prob_refs[c][head]
            dscore = (prob.astype(F32) * centred).astype(BF16)
            both = dot(below, dscore)
            level = both[:LEVELS]
            level_high = level.astype(BF16)
            level_low = (level - level_high.astype(F32)).astype(BF16)
            one_part = one[span, :]
            pairs = pairs + dot(level_high, one_part) + dot(level_low, one_part)
            dquery_t.append(both[LEVELS:] * SCALE)
            dkey = dkey + dot(dscore, q_ref[span, own])
            dvalue = dvalue + dot(prob, dout)
        pair_ref[n] = jnp.where(inside, pairs, 0.0)
        turned[0].append(jnp.concatenate(dquery_t, axis=1))
        turned[1].append(dkey * SCALE)
        turned[2].append(dvalue)
        if n % 2 == 1 or n == heads - 1:
            start = n - n % 2
            wide = HD * len(turned[0])
            for m in range(3):
                joined = jnp.concatenate(turned[m], axis=0 if m == 0 else 1)
                if m == 0:
                    joined = jnp.transpose(joined)
                dqkv_ref[m, :, start * HD : start * HD + wide] = joined.astype(BF16)
            turned = [[], [], []]


def back_kernel(
    relative, count_ref, w_ref, visual_ref, stats_ref, *refs
):
    steps = lax.axis_size("head")
    inner, refs = refs[: 6 + 4 * CHUNKS], refs[6 + 4 * CHUNKS :]
    dqkv_ref, pair_ref, sums_ref = refs[:3]
    heads = pair_ref.shape[0]
    attend_back_heads(heads, 0, count_ref, inner, dqkv_ref, pair_ref)
    visual = stream_is_visual()
    tokens = visual_ref.shape[0]
    share = tokens // steps
    mean, scale = stats_ref[0:1, :], stats_ref[1:2, :]
    shift_sum = jnp.zeros(mean.shape, F32)
    gain_sum = jnp.zeros(mean.shape, F32)
    for k in range(steps):
        if relative:
            start = pl.multiple_of((lax.axis_index("head") ^ k) * share, share)
            target = refs[3 + k % 2].at[k // 2]
        else:
            start = k * share
            target = refs[3].at[k]
        rows = pl.ds(start, share)
        part = functools.reduce(
            jnp.add, (dot(dqkv_ref[m, rows, :], w_ref[m], NT) for m in range(3))
        )
        target[...] = part.astype(target.dtype)
        keep = jnp.logical_and(visual, iota((share, 1), 0) + start < count_ref[0]).astype(F32)
        kept = part * keep
        shift_sum = shift_sum + jnp.sum(kept, axis=0, keepdims=True)
        hat = (visual_ref[rows, :].astype(F32) - mean) * scale
        gain_sum = gain_sum + jnp.sum(kept * hat, axis=0, keepdims=True)
    sums_ref[...] = jnp.concatenate(
        [shift_sum, gain_sum, jnp.zeros((6, mean.shape[1]), F32)], axis=0
    )


def join_pair_kernel(keep_ref, other_ref, own_ref, send_ref):
    own_ref[...] = keep_ref[0] + other_ref[0].astype(F32)
    send_ref[...] = (keep_ref[1] + other_ref[1].astype(F32)).astype(BF16)


def table_sums(pair_refs):
    table_width = NB_REL + 2 * NB_BOX
    sums = [[], [], []]
    for ref in pair_refs:
        for head in range(ref.shape[0]):
            turned = pltpu.roll(ref[head], LEVELS // 2 + 1, 1, stride=1, stride_axis=0)
            for n, (start, stop, unused_half, unused_offset) in enumerate(GROUPS):
                rows = turned[LEVELS - stop : LEVELS - start]
                sums[n].append(jnp.sum(rows, axis=0, keepdims=True))
    table = jnp.zeros((8, table_width), F32)
    offsets = LEVELS // 2 - iota((table_width, LEVELS), 1)
    for n, (unused_start, unused_stop, half, offset) in enumerate(GROUPS):
        missing = 8 - len(sums[n])
        stacked = jnp.concatenate(sums[n] + [jnp.zeros((missing, LEVELS), F32)], axis=0)
        table = table + picked(stacked, bucket_map(offsets, half, offset, table_width), NT)
    return table


def qkv_grad_kernel(fused, x_ref, dqkv_ref, pair_ref, *outs):
    tokens, width = x_ref.shape
    local_width = dqkv_ref.shape[2]
    table = table_sums((pair_ref,))
    x = x_ref[...]

    if not fused:
        grad_ref, table_ref = outs
        table_ref[...] = table
        for m in range(3):
            grad_ref[m] = dot(x, dqkv_ref[m], TN).astype(BF16)
        return
    mine_ref, sib_ref, whole = outs
    width_own = width // 8
    padded = jnp.concatenate(
        [
            jnp.concatenate([table, jnp.zeros((8, local_width - table.shape[1]), F32)], axis=1),
            jnp.zeros((8, local_width), F32),
        ],
        axis=0,
    )
    for m in range(3):
        whole[m] = dot(x, dqkv_ref[m], TN)
    for half, target in ((1, sib_ref), (0, mine_ref)):
        for k in range(4):
            rows = pl.ds(pl.multiple_of(owner_of(half, k) * width_own, 8), width_own)
            tall = jnp.concatenate([whole[m, rows, :] for m in range(3)] + [padded], axis=0)
            middle = tall.shape[0] // 2
            target[k] = jnp.concatenate([tall[:middle], tall[middle:]], axis=1).astype(
                target.dtype
            )


def finish_grads_kernel(hidden_width, *refs):
    block_refs, outs = refs[:8], refs[8:]
    grad_in, grad_out, grad_ow, bias_in, grad_qkv, grad_table = outs[:6]
    sums = [
        own[...] + other[...].astype(F32) for own, other in zip(block_refs[::2], block_refs[1::2])
    ]
    total = jnp.concatenate(sums, axis=0)
    width = total.shape[1]
    part_in = grad_in.shape[0]
    part_out = grad_out.shape[0]
    half_own = grad_ow.shape[1] // 2
    local_width = grad_ow.shape[0]
    parts = hidden_width // width
    place = lax.axis_index("dp") * lax.axis_size("head") + lax.axis_index("head")
    grad_in[...] = jnp.concatenate(
        [total[p * part_in : (p + 1) * part_in] for p in range(parts)], axis=1
    )
    base = parts * part_in
    vec = total[base : base + VEC_ROWS]
    base += VEC_ROWS
    grad_out[...] = total[base : base + part_out]
    base += part_out
    packed = total[base : base + half_own]
    grad_ow[...] = jnp.transpose(
        jnp.concatenate([packed[:, :local_width], packed[:, local_width:]], axis=0)
    )
    base += half_own
    lane = iota((width, 128), 0)
    column = iota((width, 128), 1)
    own = picked(vec, one_hot((lane == place * part_in + column) & (column < part_in)))
    for row, out in zip((0, 1, 2, 7, 8, 9), outs[6:]):
        out[...] = own[row : row + 1, :part_in]
    first = place * part_out
    wide = picked(
        vec, one_hot((lane == lax.rem(first, width) + column) & (column < part_out))
    )
    row = iota((VEC_ROWS, 128), 0)
    chosen = jnp.where(row == 3 + lax.div(first, width), wide, 0.0)
    bias_in[...] = jnp.sum(chosen, axis=0, keepdims=True)[:, :part_out]
    grads = jnp.concatenate([total[base:, :local_width], total[base:, local_width:]], axis=0)
    width_own = grad_qkv.shape[1]
    for m in range(3):
        grad_qkv[m] = grads[m * width_own : (m + 1) * width_own]
    table = grads[3 * width_own : 3 * width_own + 8]
    buckets = grad_table.shape[1]
    lane = iota((local_width, 128), 0)
    column = iota((local_width, 128), 1)
    start = lax.axis_index("dp") * buckets
    cut = picked(table, one_hot((lane == start + column) & (column < buckets)))
    grad_table[...] = cut[: grad_table.shape[0], :buckets]


def finish_inputs_kernel(steps, relative, sums, count_ref, visual_ref, stats_ref, *refs):
    share_refs, refs = refs[:CHUNKS], refs[CHUNKS:]
    part_refs, refs = refs[: 1 + relative], refs[1 + relative :]
    sum_refs, refs = refs[:sums], refs[sums:]
    text_ref, grad_ref, gain_ref, shift_ref = refs
    head_rank = lax.axis_index("head")
    share = text_ref.shape[0]
    half = steps // 2
    if relative:
        same, other = (ref[...].astype(F32) for ref in part_refs)
        text = jnp.where(stream_is_visual(), other, same)
        visual = jnp.where(stream_is_visual(), same, other)
    else:
        text, visual = (
            functools.reduce(
                jnp.add, (part_refs[0][k].astype(F32) for k in range(start, start + half))
            )
            for start in (0, half)
        )
    text_ref[...] = functools.reduce(jnp.add, (ref[...] for ref in share_refs)) + text
    total = functools.reduce(jnp.add, (ref[...] for ref in sum_refs))
    mean, scale, gain, number = (stats_ref[i : i + 1, :] for i in range(4))
    start = pl.multiple_of(head_rank * share, share)
    keep = (iota((share, 1), 0) + start < count_ref[0]).astype(F32)
    hat = (visual_ref[pl.ds(start, share), :].astype(F32) - mean) * keep * scale
    dnormed = visual * keep
    shift_gradient, gain_gradient = total[0:1], total[1:2]
    shift_ref[...] = shift_gradient
    gain_ref[...] = gain_gradient
    grad_ref[...] = (
        keep
        * scale
        * gain
        * (dnormed - shift_gradient / number - hat * gain_gradient / number)
    )


def swap(value, axis, mask):
    size = lax.axis_size(axis)
    return lax.ppermute(value, axis, [(i, i ^ mask) for i in range(size)])


def after(value, *earlier):
    return lax.optimization_barrier((value, *earlier))[0]


def gather_heads(chunks):
    return [[piece] + [swap(piece, "head", k) for k in (1, 2, 3)] for piece in chunks]


def across_chips(mine, other, plans, sizes, name):
    axes = {X_FIRST: (2, 4), Y_FIRST: (4, 2)}
    width = mine.shape[2]
    outs = []
    for size in sizes:
        outs += [((2, size, width), F32), ((2, size, width), BF16)]
    joined = call(functools.partial(join_cores_kernel, plans), name, 1, outs, [mine, other])
    return [
        (keep, swap(send, "dp", axes[plan][0]), axes[plan][1])
        for plan, keep, send in zip(plans, joined[::2], joined[1::2])
    ]


def second_exchange(stages, name, earlier=()):
    outs = []
    args = []
    for keep, other, mask in stages:
        outs += [(keep.shape[1:], F32), (keep.shape[1:], BF16)]
        args += [keep, other]
    args[1] = after(args[1], *earlier)
    joined = call(join_chips_kernel, name, 1, outs, args)
    blocks = []
    for n, stage in enumerate(stages):
        blocks += [joined[2 * n], swap(joined[2 * n + 1], "dp", stage[2])]
    return blocks, joined


def per_device(
    text_in,
    visual_in,
    visual_count,
    line_index,
    box_index,
    qkv_weight,
    bias_table,
    out_weight,
    out_bias,
    norm1_gain,
    norm1_shift,
    ffn_weight_in,
    ffn_bias_in,
    ffn_weight_out,
    ffn_bias_out,
    norm2_gain,
    norm2_shift,
    batch_gain,
    batch_shift,
    cotangent,
):
    tokens, width = text_in.shape
    local_width = qkv_weight.shape[2]
    heads_local = local_width // HD
    head_count = lax.axis_size("head")
    dp_count = lax.axis_size("dp")
    head_rank = lax.axis_index("head")
    dp_rank = lax.axis_index("dp")
    fused = head_count == 4 and dp_count == 8
    share = tokens // head_count
    block = tokens // CHUNKS
    hidden_width = ffn_weight_in.shape[1]
    table_width = bias_table.shape[1]
    part_in = width // (dp_count * head_count)
    part_out = hidden_width // (dp_count * head_count)
    weight = jnp.transpose(qkv_weight, (1, 0, 2))
    row_vectors = [
        value.reshape(1, width)
        for value in (
            out_bias,
            norm1_gain,
            norm1_shift,
            ffn_bias_out,
            norm2_gain,
            norm2_shift,
            batch_gain,
            batch_shift,
        )
    ]

    packed_shape = ((8, width), F32)
    (packed,) = call(
        stats_kernel, "stats", 2, [packed_shape], [visual_in], visual_count
    )
    if fused:
        (packed,) = call(
            join_stats_kernel, "join_stats", 1, [packed_shape], [packed, swap(packed, "dp", 1)]
        )
        packed = [packed] + [swap(packed, "dp", k) for k in (2, 4, 6)]
    else:
        gathered = lax.all_gather(packed, "dp")
        packed = [gathered[i] for i in range(dp_count)]
    one, back, tab, small, bias_in = call(
        prep_kernel,
        "prep",
        2,
        [
            ((tokens, LEVELS), BF16),
            ((LEVELS, tokens), BF16),
            ((LEVELS, heads_local * LEVELS), BF16),
            ((8, width), F32),
            ((8, width), F32),
        ],
        [line_index, box_index, bias_table, ffn_bias_in.reshape(1, hidden_width)] + row_vectors,
        visual_count,
    )

    rows = ((tokens, local_width), BF16)
    turned = ((local_width, tokens), BF16)
    chunk_outs = [((local_width, block), BF16), ((heads_local, tokens, block), BF16)]
    stats, x, q, k, v, kt, vt, heads_one, prob_one = call(
        functools.partial(attend_first_kernel, len(packed)),
        "attend_first",
        6,
        [packed_shape, ((tokens, width), BF16), rows, rows, rows, turned, turned] + chunk_outs,
        [text_in, visual_in, small, weight, tab, one] + packed,
        visual_count,
        final=(1,),
    )
    heads_two, prob_two = call(
        functools.partial(attend_chunk, 1),
        "attend_second",
        3,
        chunk_outs,
        [q, k, vt, tab, one],
        visual_count,
    )
    heads = (heads_one, heads_two)
    if fused:
        pieces = gather_heads(heads)
    else:
        pieces = []
        for piece in heads:
            gathered = lax.all_gather(piece, "head")
            pieces.append([gathered[i] for i in range(head_count)])

    results = []
    for c in range(CHUNKS):
        text = after(text_in, results[-1][-1]) if results else text_in
        results.append(
            call(
                functools.partial(ffn_kernel, c, fused, len(pieces[c])),
                f"ffn_{c}",
                9,
                [
                    ((block, width), BF16),
                    ((share, width), F32),
                    ((block, hidden_width), BF16),
                    ((block, hidden_width), BF16),
                    ((block, width), BF16),
                    ((block, width), BF16),
                    ((block, width), BF16),
                    ((block, local_width), BF16),
                    ((local_width, block), BF16),
                    ((VEC_ROWS, width), F32),
                ],
                [text, cotangent, out_weight, ffn_weight_in, ffn_weight_out, small, bias_in]
                + list(pieces[c]),
                scratch=[pltpu.VMEM((block, hidden_width), F32)],
            )
        )
    out, dh_share, act, dpre, low, branch, mix, dheads, dheads_t, vec = zip(*results)
    if fused:
        in_rows = hidden_width // width * part_in + VEC_ROWS
        out_rows = part_out + width // dp_count // 2
        mine, sib = call(
            weight_grad_in_kernel,
            "weight_grad_in",
            2,
            [((4, in_rows, width), F32), ((4, in_rows, width), BF16)],
            [*low, *dpre, *vec],
        )
        other = swap(sib, "dp", 1)
        layer_out, mine_out, sib_out = call(
            weight_grad_out_kernel,
            "weight_grad_out",
            3,
            [
                ((tokens, width), BF16),
                ((4, out_rows, width), F32),
                ((4, out_rows, width), BF16),
            ],
            [after(out[0], sib), *out[1:], *act, *branch, *mix, *heads],
            scratch=[pltpu.VMEM((width, local_width), F32)],
            final=(0,),
        )
        other_out = swap(sib_out, "dp", 1)
        ffn_stages = across_chips(mine, other, [X_FIRST], [in_rows], "join_cores_in")
        ffn_stages += across_chips(mine_out, other_out, [Y_FIRST], [out_rows], "join_cores_out")
    inner = [q, k, v, kt, one, back, *heads, *dheads, *dheads_t, prob_one, prob_two]
    if fused:
        inner[0] = after(q, *(stage[0] for stage in ffn_stages))
        part_outs = [((2, share, width), F32), ((2, share, width), BF16)]
    else:
        part_outs = [((head_count, share, width), BF16)]
    dqkv, pairs, sums, *parts = call(
        functools.partial(back_kernel, fused),
        "back",
        10,
        [
            ((3, tokens, local_width), BF16),
            ((heads_local, LEVELS, LEVELS), F32),
            packed_shape,
        ]
        + part_outs,
        [weight, visual_in, stats] + inner,
        visual_count,
    )
    if fused:
        keep, send = parts
        near = swap(send, "head", 1)
        sums = sums + swap(sums, "dp", 1)
        ffn_blocks, ffn_joined = second_exchange(ffn_stages, "join_chips_ffn", [sums])
        sums = sums + swap(sums, "dp", 2)
        block_rows = 3 * (width // dp_count) + 16
        mine, sib = call(
            functools.partial(qkv_grad_kernel, True),
            "qkv_grad",
            3,
            [
                ((4, block_rows // 2, 2 * local_width), F32),
                ((4, block_rows // 2, 2 * local_width), BF16),
            ],
            [after(x, ffn_joined[0]), dqkv, pairs],
            scratch=[pltpu.VMEM((3, width, local_width), F32)],
        )
        first_rows = block_rows // 4 // 8 * 8
        stages = across_chips(
            mine,
            after(swap(sib, "dp", 1), sums),
            [X_FIRST, Y_FIRST],
            [first_rows, block_rows // 2 - first_rows],
            "join_cores_qkv",
        )
        sums = sums + swap(sums, "dp", 4)
        qkv_blocks, unused_joined = second_exchange(stages, "join_chips_qkv", ffn_blocks)
        same, send = call(
            join_pair_kernel,
            "join_pair",
            1,
            [((share, width), F32), ((share, width), BF16)],
            [keep, after(near, sums)],
        )
        received = [same, swap(send, "head", 2)]
        sums = sums + swap(sums, "head", 1)
        sums = [sums, swap(sums, "head", 2)]
        blocks = ffn_blocks + qkv_blocks
        one_row = ((1, part_in), F32)
        grad_in, grad_out, grad_ow, grad_bias_in, grad_qkv, grad_table, *own = call(
            functools.partial(finish_grads_kernel, hidden_width),
            "finish_grads",
            2,
            [
                ((part_in, hidden_width), F32),
                ((part_out, width), F32),
                ((local_width, width // dp_count), F32),
                ((1, part_out), F32),
                ((3, width // dp_count, local_width), F32),
                ((heads_local, table_width // dp_count), F32),
            ]
            + [one_row] * 6,
            blocks,
            final=range(12),
        )
        grad_bias_in = grad_bias_in.reshape(part_out)
        grad_qkv = jnp.transpose(grad_qkv, (1, 0, 2))
        own = [value.reshape(part_in) for value in own]
    else:
        layer_out = jnp.concatenate(out, axis=0)
        act, dpre, low, branch, mix = (
            jnp.concatenate(value, axis=0) for value in (act, dpre, low, branch, mix)
        )

        def scatter(value, dimension):
            return lax.psum_scatter(
                value.astype(BF16), "dp", scatter_dimension=dimension, tiled=True
            ).astype(F32)

        def own_columns(value, part):
            split = value.reshape(tokens, dp_count, head_count, part)
            return lax.dynamic_index_in_dim(split, head_rank, 2, keepdims=False).reshape(
                tokens, dp_count * part
            )

        grad_in = scatter(dot(own_columns(low, part_in), dpre, TN), 0)
        grad_out = scatter(dot(own_columns(act, part_out), branch, TN), 0)
        grad_ow = scatter(dot(jnp.concatenate(heads, axis=1), mix), 1)
        vec = lax.psum((vec[0] + vec[1]).astype(BF16), "dp").astype(F32)
        place = dp_rank * head_count + head_rank
        own = [
            lax.dynamic_slice_in_dim(vec[row], place * part_in, part_in, 0)
            for row in (0, 1, 2, 7, 8, 9)
        ]
        grad_bias_in = lax.dynamic_slice_in_dim(
            vec[3 : 3 + hidden_width // width].reshape(hidden_width), place * part_out, part_out, 0
        )
        sums = [lax.psum(sums, ("dp", "head"))]
        grad, table = call(
            functools.partial(qkv_grad_kernel, False),
            "qkv_grad",
            3,
            [((3, width, local_width), BF16), ((8, table_width), F32)],
            [x, dqkv, pairs],
        )
        received = [lax.all_to_all(parts[0], "head", 0, 0, tiled=True)]
        grad_qkv = jnp.transpose(scatter(grad, 1), (1, 0, 2))
        grad_table = scatter(table[:heads_local], 1)

    grad_text, grad_visual, gain_gradient, shift_gradient = call(
        functools.partial(finish_inputs_kernel, head_count, fused, len(sums)),
        "finish_inputs",
        2,
        [((share, width), F32)] * 2 + [((1, width), F32)] * 2,
        [visual_in, stats, *dh_share, *received, *sums],
        visual_count,
        final=range(4),
    )
    return (
        layer_out,
        grad_text,
        grad_visual,
        grad_qkv,
        grad_table,
        grad_ow,
        own[0],
        own[1],
        own[2],
        grad_in,
        grad_bias_in,
        grad_out,
        own[3],
        own[4],
        own[5],
        gain_gradient.reshape(width),
        shift_gradient.reshape(width),
    )


def solution(mesh):
    in_specs = (
        P("dp", None),
        P("dp", None),
        P("dp"),
        P(None, "dp"),
        P(None, None, "dp"),
        P(None, None, "head"),
        P("head", None),
        P(),
        P(),
        P(),
        P(),
        P(),
        P(),
        P(),
        P(),
        P(),
        P(),
        P(),
        P(),
        P("dp", None),
    )
    out_specs = (
        P("dp", None),
        P(("dp", "head"), None),
        P(("dp", "head"), None),
        P("dp", None, "head"),
        P("head", "dp"),
        P("head", "dp"),
        P(("dp", "head")),
        P(("dp", "head")),
        P(("dp", "head")),
        P(("dp", "head"), None),
        P(("dp", "head")),
        P(("dp", "head"), None),
        P(("dp", "head")),
        P(("dp", "head")),
        P(("dp", "head")),
        P(),
        P(),
    )
    return jax.shard_map(
        per_device, mesh=mesh, in_specs=in_specs, out_specs=out_specs, check_vma=False
    )
```

```python
import functools

import jax
import jax.numpy as jnp
from jax import lax
from jax.experimental import pallas as pl
from jax.experimental.pallas import tpu as pltpu
from jax.sharding import PartitionSpec as P

HD = 64
NB_REL = 32
NB_BOX = 16
LINES = 48
BOXES = 32

EPSILON = 1e-05
FLOOR_SCORE = -1000000000.0
SCALE = HD ** (-0.5)
LEVELS = 128
MASK_LANE = LINES + 2 * BOXES
VMEM_LIMIT = 12 * 1024 * 1024
VEC_ROWS = 16
CHUNKS = 2

F32 = jnp.float32
BF16 = jnp.bfloat16

NN = (((1,), (0,)), ((), ()))
NT = (((1,), (1,)), ((), ()))
TN = (((0,), (0,)), ((), ()))
TT = (((0,), (1,)), ((), ()))


def dot(left, right, dims=NN):
    return lax.dot_general(left, right, dims, preferred_element_type=F32)


def iota(shape, axis):
    return lax.broadcasted_iota(jnp.int32, shape, axis)


def one_hot(condition):
    return condition.astype(F32).astype(BF16)


def thirds(value):
    high = value.astype(BF16)
    rest = value - high.astype(F32)
    middle = rest.astype(BF16)
    return high, middle, (rest - middle.astype(F32)).astype(BF16)


def picked(value, selector, dims=NN):
    return functools.reduce(jnp.add, (dot(part, selector, dims) for part in thirds(value)))


def call(kernel, name, micros, outs, args, count=None, scratch=(), final=()):
    vmem = pl.BlockSpec(memory_space=pltpu.VMEM)
    scalars = [] if count is None else [count]
    return pl.pallas_call(
        kernel,
        out_shape=tuple(
            jax.ShapeDtypeStruct(*entry) if place in final else pltpu.VMEM(*entry)
            for place, entry in enumerate(outs)
        ),
        in_specs=[pl.BlockSpec(memory_space=pltpu.SMEM)] * len(scalars) + [vmem] * len(args),
        out_specs=tuple(vmem for entry in outs),
        scratch_shapes=list(scratch),
        compiler_params=pltpu.CompilerParams(vmem_limit_bytes=VMEM_LIMIT),
        cost_estimate=pl.CostEstimate(
            flops=int(micros * 1e9), bytes_accessed=int(micros * 3e6), transcendentals=0
        ),
        name=name,
    )(*scalars, *[pltpu.with_memory_space_constraint(a, pltpu.VMEM) for a in args])


def head_groups(heads_local, body, loop=True):
    if heads_local % 2 or not loop:
        for first in range(0, heads_local, 2):
            body(first, min(2, heads_local - first))
        return

    def step(pair, carry):
        body(pair * 2, 2)
        return carry

    lax.fori_loop(0, heads_local // 2, step, 0)


def lanes(first, heads, offset=0):
    start = offset + first * HD
    if isinstance(first, int):
        return slice(start, start + heads * HD)
    return pl.ds(pl.multiple_of(start, 128), heads * HD)


def stream_is_visual():
    return lax.axis_index("head") >= lax.axis_size("head") // 2


def stats_kernel(count_ref, visual_ref, out_ref):
    tokens, width = visual_ref.shape
    number = count_ref[0].astype(F32)
    keep = (iota((tokens, 1), 0) < count_ref[0]).astype(F32)
    visual = visual_ref[...].astype(F32)
    total = jnp.sum(visual * keep, axis=0, keepdims=True)
    centred = (visual - total / number) * keep
    spread = jnp.sum(centred * centred, axis=0, keepdims=True)
    out_ref[...] = jnp.concatenate(
        [total, spread, jnp.full((1, width), number, F32), jnp.zeros((5, width), F32)], axis=0
    )


def joined_stats(blocks):
    total = functools.reduce(jnp.add, (b[0:1] for b in blocks))
    number = functools.reduce(jnp.add, (b[2:3] for b in blocks))
    mean = total / number
    spread = functools.reduce(
        jnp.add, (b[1:2] + b[2:3] * (b[0:1] / b[2:3] - mean) ** 2 for b in blocks)
    )
    return total, spread, number


def join_stats_kernel(*refs):
    total, spread, number = joined_stats([ref[...] for ref in refs[:-1]])
    refs[-1][...] = jnp.concatenate(
        [total, spread, number, jnp.zeros((5, total.shape[1]), F32)], axis=0
    )


GROUPS = (
    (0, LINES, NB_REL // 2, 0),
    (LINES, LINES + BOXES, NB_BOX // 2, NB_REL),
    (LINES + BOXES, LINES + 2 * BOXES, NB_BOX // 2, NB_REL + NB_BOX),
)


def bucket_map(level, half, offset, table_width):
    bucket = jnp.clip(level, -half, half - 1) + half + offset
    return one_hot(bucket == iota((table_width, LEVELS), 0))


def same_group(row, lane):
    inside = jnp.zeros(row.shape, jnp.bool_)
    for start, stop, unused_half, unused_offset in GROUPS:
        inside = inside | ((row >= start) & (row < stop) & (lane >= start) & (lane < stop))
    return inside


def by_level(level, line, across, down):
    wanted = jnp.where(level < LINES, line, jnp.where(level < LINES + BOXES, across, down))
    return wanted == level


def prep_kernel(count_ref, line_ref, box_ref, table_ref, bias_ref, *refs):
    oh_ref, back_ref, tab_ref, small_ref, b1_ref = refs[8:]
    width = small_ref.shape[1]
    small_ref[...] = jnp.concatenate([ref[...] for ref in refs[:8]], axis=0)
    for c in range(bias_ref.shape[1] // width):
        b1_ref[c : c + 1, :] = bias_ref[:, c * width : (c + 1) * width]
    visual = stream_is_visual()
    tokens = line_ref.shape[1]
    heads_local, table_width = table_ref.shape
    line = jnp.where(visual, line_ref[1:2, :], line_ref[0:1, :])
    across = jnp.where(visual, box_ref[1, 0:1, :], box_ref[0, 0:1, :]) + LINES
    down = jnp.where(visual, box_ref[1, 1:2, :], box_ref[0, 1:2, :]) + (LINES + BOXES)
    level = iota((LEVELS, tokens), 0)
    back_ref[...] = one_hot(by_level(LEVELS - 1 - level, line, across, down))
    closed = jnp.logical_and(visual, iota((LEVELS, tokens), 1) >= count_ref[0])
    mask = jnp.where(closed, FLOOR_SCORE, 0.0)
    flags = by_level(level, line, across, down).astype(F32)
    oh_ref[...] = jnp.transpose(jnp.where(level == MASK_LANE, mask, flags)).astype(BF16)
    row = iota((LEVELS, LEVELS), 0)
    lane = iota((LEVELS, LEVELS), 1)
    inside = same_group(row, lane)
    offsets = iota((table_width, LEVELS), 1) - LEVELS // 2
    table = table_ref[...]
    spread = [
        picked(table, bucket_map(offsets, half, offset, table_width))
        for unused_start, unused_stop, half, offset in GROUPS
    ]
    for head in range(heads_local):
        rows = [jnp.broadcast_to(s[head : head + 1, :], (LEVELS, LEVELS)) for s in spread]
        chosen = jnp.where(row < LINES, rows[0], jnp.where(row < LINES + BOXES, rows[1], rows[2]))
        turned = pltpu.roll(chosen, LEVELS // 2, 1, stride=1, stride_axis=0)
        pairs = jnp.where(inside, turned, 0.0)
        high = jnp.where((lane == MASK_LANE) & (row < LINES), 1.0, pairs)
        tab_ref[:, head * LEVELS : (head + 1) * LEVELS] = high.astype(BF16)


def attend_chunk(
    chunk, count_ref, q_ref, k_ref, vt_ref, tab_ref, oh_ref, heads_ref, prob_ref, left_ref
):
    visual = stream_is_visual()
    tokens, local_width = q_ref.shape
    heads_local = local_width // HD
    block = heads_ref.shape[1]
    span = slice(chunk * block, (chunk + 1) * block)
    place = iota((1, block), 1) + chunk * block
    allowed = jnp.logical_or(jnp.logical_not(visual), place < count_ref[0]).astype(F32)
    one = oh_ref[...]
    left_ref[...] = dot(oh_ref[span, :], tab_ref[...]).astype(BF16)
    ones = jnp.ones((16, tokens), F32).astype(BF16)

    def group(first, heads):
        span_lanes = lanes(first, heads)
        queries = q_ref[span, span_lanes] * jnp.asarray(SCALE, BF16)
        keys = k_ref[:, span_lanes]
        values = vt_ref[span_lanes, :]
        biases = left_ref[:, lanes(2 * first, 2 * heads)]

        def scores(n):
            own = slice(n * HD, (n + 1) * HD)
            right = jnp.concatenate(
                [biases[:, n * LEVELS : (n + 1) * LEVELS], queries[:, own]], axis=1
            )
            return dot(jnp.concatenate([one, keys[:, own]], axis=1), right, NT)

        results = []
        following = scores(0)
        for n in range(heads):
            own = slice(n * HD, (n + 1) * HD)
            current = following
            if n + 1 < heads:
                following = scores(n + 1)
            shifted = jnp.exp(current - jnp.max(current, axis=0, keepdims=True))
            mixed = dot(jnp.concatenate([values[own], ones], axis=0), shifted.astype(BF16))
            share = 1.0 / mixed[HD : HD + 1]
            prob_ref[first + n] = (shifted * share).astype(BF16)
            results.append((mixed[:HD] * (share * allowed)).astype(BF16))
        heads_ref[span_lanes, :] = jnp.concatenate(results, axis=0)

    head_groups(heads_local, group, loop=chunk > 0)


def attend_first_kernel(pieces, count_ref, text_ref, visual_ref, small_ref, w_ref, tab_ref, oh_ref, *refs):
    piece_refs, refs = refs[:pieces], refs[pieces:]
    stats_ref, x_ref, q_ref, k_ref, v_ref, kt_ref, vt_ref, heads_ref, prob_ref, left_ref = refs
    visual = stream_is_visual()
    tokens, width = text_ref.shape
    total, spread, number = joined_stats([ref[...] for ref in piece_refs])
    mean = total / number
    scale = lax.rsqrt(spread / number + EPSILON)
    gain, shift = small_ref[6:7, :], small_ref[7:8, :]
    stats_ref[...] = jnp.concatenate(
        [mean, scale, gain, number, jnp.zeros((4, width), F32)], axis=0
    )

    @pl.when(visual)
    def _():
        keep = (iota((tokens, 1), 0) < count_ref[0]).astype(F32)
        centred = (visual_ref[...].astype(F32) - mean) * keep
        x_ref[...] = ((centred * scale * gain + shift) * keep).astype(BF16)

    @pl.when(jnp.logical_not(visual))
    def _():
        x_ref[...] = text_ref[...]

    x = x_ref[...]
    q_ref[...] = dot(x, w_ref[0]).astype(BF16)
    k_ref[...] = dot(x, w_ref[1]).astype(BF16)
    v_ref[...] = dot(x, w_ref[2]).astype(BF16)
    kt_ref[...] = dot(w_ref[1], x, TT).astype(BF16)
    vt_ref[...] = dot(w_ref[2], x, TT).astype(BF16)
    attend_chunk(
        0, count_ref, q_ref, k_ref, vt_ref, tab_ref, oh_ref, heads_ref, prob_ref, left_ref
    )


ERF_P = 0.3275911 * 0.7071067811865476
ERF_A = (0.254829592, -0.284496736, 1.421413741, -1.453152027, 1.061405429)


def gelu_parts(pre):
    t = 1.0 / (1.0 + ERF_P * jnp.abs(pre))
    bell = jnp.exp(-0.5 * pre * pre)
    poly = 0.5 * ERF_A[4]
    for coefficient in ERF_A[3::-1]:
        poly = poly * t + 0.5 * coefficient
    tail = poly * t * bell
    cdf = jnp.where(pre >= 0.0, 1.0 - tail, tail)
    return pre * cdf, cdf + pre * (bell * 0.3989422804014327)


def normed_rows(hidden):
    average = jnp.mean(hidden, axis=-1, keepdims=True)
    centred = hidden - average
    scale = lax.rsqrt(jnp.mean(centred * centred, axis=-1, keepdims=True) + EPSILON)
    return centred * scale, scale


def normed_back(upstream, hat, scale, gain):
    scaled = upstream * gain
    return scale * (
        scaled
        - jnp.mean(scaled, axis=-1, keepdims=True)
        - hat * jnp.mean(scaled * hat, axis=-1, keepdims=True)
    )


def ffn_kernel(chunk, relative, pieces, *refs):
    (text_ref, cot_ref, wo, w1, w2, small_ref, b1_ref), refs = refs[:7], refs[7:]
    piece_refs, refs = refs[:pieces], refs[pieces:]
    out_ref, share_ref, act_ref, dpre_ref, low_ref, branch_ref, mix_ref = refs[:7]
    dheads_ref, dheadst_ref, vec_ref, slope = refs[7:]
    local_width, block = piece_refs[0].shape
    width = text_ref.shape[1]
    hidden_width = w1.shape[1]
    head_rank = lax.axis_index("head")
    out_bias, gain1, shift1, b2, gain2, shift2 = (small_ref[i : i + 1, :] for i in range(6))
    parts = hidden_width // width
    share = share_ref.shape[0]
    rows = slice(chunk * block, (chunk + 1) * block)
    own_rows = pl.ds(pl.multiple_of(head_rank * local_width, 64), local_width)

    sources = [
        (ref[...], head_rank ^ index if relative else index)
        for index, ref in enumerate(piece_refs)
    ]
    mixed = text_ref[rows, :].astype(F32) + out_bias
    for piece, source in sources:
        wo_rows = pl.ds(pl.multiple_of(source * local_width, 64), local_width)
        mixed = mixed + dot(piece, wo[wo_rows, :], TN)
    hat1, scale1 = normed_rows(mixed)
    after = hat1 * gain1 + shift1
    after_low = after.astype(BF16)
    low_ref[...] = after_low
    branch = jnp.zeros((block, width), F32)
    for c in range(parts):
        cols = slice(c * width, (c + 1) * width)
        act, slope[:, cols] = gelu_parts(dot(after_low, w1[:, cols]) + b1_ref[c : c + 1, :])
        act = act.astype(BF16)
        act_ref[:, cols] = act
        branch = branch + dot(act, w2[cols, :])
    hat2, scale2 = normed_rows(after + (branch + b2))
    out_ref[...] = (hat2 * gain2 + shift2).astype(BF16)
    upstream = cot_ref[rows, :].astype(F32)
    dh_two = normed_back(upstream, hat2, scale2, gain2)
    dbranch = dh_two.astype(BF16)
    branch_ref[...] = dbranch
    vec = [None] * 3
    dy = dh_two
    for c in range(parts):
        cols = slice(c * width, (c + 1) * width)
        dpre = (dot(dbranch, w2[cols, :], NT) * slope[:, cols]).astype(BF16)
        dpre_ref[:, cols] = dpre
        vec.append(dpre.astype(F32))
        dy = dy + dot(dpre, w1[:, cols], NT)
    dh_one = normed_back(dy, hat1, scale1, gain1)
    vec[:3] = [dh_one, dy * hat1, dy]
    vec += [dbranch.astype(F32), upstream * hat2, upstream]
    sums = [jnp.sum(v, axis=0, keepdims=True) for v in vec]
    vec_ref[...] = jnp.concatenate(
        sums + [jnp.zeros((VEC_ROWS - len(sums), width), F32)], axis=0
    )
    share_ref[...] = jnp.zeros_like(share_ref)
    per_block = block // share
    for part in range(per_block):

        @pl.when(head_rank == chunk * per_block + part)
        def _():
            share_ref[...] = dh_one[part * share : (part + 1) * share]

    dmix = dh_one.astype(BF16)
    mix_ref[...] = dmix
    dheads_ref[...] = dot(dmix, wo[own_rows, :], NT).astype(BF16)
    dheadst_ref[...] = dot(wo[own_rows, :], dmix, NT).astype(BF16)


def owner_of(half, step):
    place = lax.axis_index("dp")
    core = place & 1
    return (((place >> 1) ^ step) << 1) | (core if half == 0 else 1 - core)


def own_order():
    return [owner_of(half, step) for half in range(2) for step in range(4)]


def weight_grad_in_kernel(*refs):
    head_rank = lax.axis_index("head")
    low_refs, dpre_refs, vec_refs = (refs[i * CHUNKS : (i + 1) * CHUNKS] for i in range(3))
    mine_ref, sib_ref = refs[3 * CHUNKS :]
    width = low_refs[0].shape[1]
    parts = dpre_refs[0].shape[1] // width
    width_own = width // 8
    part_in = width_own // 4
    lane = iota((part_in, width), 1)
    row = iota((part_in, width), 0)
    pick = jnp.concatenate(
        [
            (lane == owner * width_own + head_rank * part_in + row).astype(F32)
            for owner in own_order()
        ],
        axis=0,
    ).astype(BF16)
    low_t = [dot(pick, low[...], NT).astype(BF16) for low in low_refs]
    grads = []
    for p in range(parts):
        cols = slice(p * width, (p + 1) * width)
        grads.append(
            functools.reduce(
                jnp.add, (dot(low_t[c], dpre_refs[c][:, cols]) for c in range(CHUNKS))
            )
        )
    vec = functools.reduce(jnp.add, (v[...] for v in vec_refs))
    for n in range(8):
        rows = slice(n * part_in, (n + 1) * part_in)
        block = jnp.concatenate([grad[rows] for grad in grads] + [vec], axis=0)
        target = mine_ref if n < 4 else sib_ref
        target[n % 4] = block.astype(target.dtype)


def weight_grad_out_kernel(*refs):
    head_rank = lax.axis_index("head")
    names = ("out", "act", "branch", "mix", "heads")
    groups = {name: refs[i * CHUNKS : (i + 1) * CHUNKS] for i, name in enumerate(names)}
    layer_ref, mine_ref, sib_ref, whole = refs[len(names) * CHUNKS :]
    block, width = groups["out"][0].shape
    hidden_width = groups["act"][0].shape[1]
    owners = own_order()
    width_own = width // 8
    window = hidden_width // 8
    part_out = window // 4
    half_own = width_own // 2
    for c in range(CHUNKS):
        layer_ref[c * block : (c + 1) * block, :] = groups["out"][c][...]
    whole[...] = functools.reduce(
        jnp.add, (dot(groups["mix"][c][...], groups["heads"][c][...], TT) for c in range(CHUNKS))
    )
    pick = one_hot(
        iota((part_out, window), 1) == head_rank * part_out + iota((part_out, window), 0)
    )
    grad = jnp.zeros((8 * part_out, width), F32)
    for c in range(CHUNKS):
        stacked = []
        for owner in owners:
            cols = pl.ds(pl.multiple_of(owner * window, 128), window)
            stacked.append(dot(pick, groups["act"][c][:, cols], NT).astype(BF16))
        grad = grad + dot(jnp.concatenate(stacked, axis=0), groups["branch"][c][...])
    for n, owner in enumerate(owners):
        start = pl.multiple_of(owner * width_own, 8)
        packed = jnp.concatenate(
            [whole[pl.ds(start, half_own), :], whole[pl.ds(start + half_own, half_own), :]],
            axis=1,
        )
        target = mine_ref if n < 4 else sib_ref
        target[n % 4] = jnp.concatenate(
            [grad[n * part_out : (n + 1) * part_out], packed], axis=0
        ).astype(target.dtype)


X_FIRST = ((0, 2), (1, 3))
Y_FIRST = ((0, 1), (2, 3))


def join_cores_kernel(plans, *refs):
    mine_ref, other_ref, outs = refs[0], refs[1], refs[2:]
    start = 0
    for (keep, send), keep_ref, send_ref in zip(plans, outs[::2], outs[1::2]):
        rows = slice(start, start + keep_ref.shape[1])
        start = rows.stop
        for places, out in ((keep, keep_ref), (send, send_ref)):
            for n, place in enumerate(places):
                total = mine_ref[place, rows, :] + other_ref[place, rows, :].astype(F32)
                out[n] = total.astype(out.dtype)


def join_chips_kernel(*refs):
    count = len(refs) // 4
    ins, outs = refs[: 2 * count], refs[2 * count :]
    for n in range(count):
        keep, other = ins[2 * n : 2 * n + 2]
        for m, out in enumerate(outs[2 * n : 2 * n + 2]):
            out[...] = (keep[m] + other[m].astype(F32)).astype(out.dtype)


def attend_back_heads(count_ref, refs, dqkv_ref, pair_ref):
    q_ref, k_ref, v_ref, kt_ref, oh_ref, back_ref = refs[:6]
    groups = [refs[6 + i * CHUNKS : 6 + (i + 1) * CHUNKS] for i in range(4)]
    head_refs, dhead_refs, dheadt_refs, prob_refs = groups
    visual = stream_is_visual()
    tokens = q_ref.shape[0]
    block = tokens // CHUNKS
    count = count_ref[0]
    one = oh_ref[...]
    back = back_ref[...]
    inside = same_group(LEVELS - 1 - iota((LEVELS, LEVELS), 0), iota((LEVELS, LEVELS), 1))
    extra = one_hot(iota((tokens, 16), 1) < 2)
    sublane = iota((16, block), 0)
    free = jnp.logical_not(visual)
    rows_open = []
    lanes_open = []
    for c in range(CHUNKS):
        rows_open.append(
            jnp.logical_or(free, iota((block, 1), 0) + c * block < count).astype(BF16)
        )
        lanes_open.append(
            jnp.logical_or(free, iota((1, block), 1) + c * block < count).astype(BF16)
        )

    def group(first, heads):
        span_lanes = lanes(first, heads)
        turned = [[], [], []]
        for n in range(heads):
            own = slice(n * HD, (n + 1) * HD)
            left = jnp.concatenate([v_ref[:, span_lanes][:, own], extra], axis=1)
            below = jnp.concatenate([back, kt_ref[span_lanes, :][own]], axis=0)
            dquery_t = []
            dkey = jnp.zeros((tokens, HD), F32)
            dvalue = jnp.zeros((tokens, HD), F32)
            pairs = jnp.zeros((LEVELS, LEVELS), F32)
            for c in range(CHUNKS):
                span = slice(c * block, (c + 1) * block)
                dout = dhead_refs[c][:, span_lanes][:, own] * rows_open[c]
                dout_t = dheadt_refs[c][span_lanes, :][own] * lanes_open[c]
                inner = -jnp.sum(
                    dout_t.astype(F32) * head_refs[c][span_lanes, :][own].astype(F32),
                    axis=0,
                    keepdims=True,
                )
                high = inner.astype(BF16).astype(F32)
                tail = jnp.where(sublane == 0, high, jnp.where(sublane == 1, inner - high, 0.0))
                centred = dot(left, jnp.concatenate([dout_t, tail.astype(BF16)], axis=0))
                prob = prob_refs[c][first + n]
                dscore = (prob.astype(F32) * centred).astype(BF16)
                both = dot(below, dscore)
                level = both[:LEVELS]
                level_high = level.astype(BF16)
                level_low = (level - level_high.astype(F32)).astype(BF16)
                one_part = one[span, :]
                pairs = pairs + dot(level_high, one_part) + dot(level_low, one_part)
                dquery_t.append(both[LEVELS:] * SCALE)
                dkey = dkey + dot(dscore, q_ref[span, span_lanes][:, own])
                dvalue = dvalue + dot(prob, dout)
            pair_ref[first + n] = jnp.where(inside, pairs, 0.0)
            turned[0].append(jnp.concatenate(dquery_t, axis=1))
            turned[1].append(dkey * SCALE)
            turned[2].append(dvalue)
        for m in range(3):
            joined = jnp.concatenate(turned[m], axis=0 if m == 0 else 1)
            if m == 0:
                joined = jnp.transpose(joined)
            dqkv_ref[m, :, span_lanes] = joined.astype(BF16)

    head_groups(q_ref.shape[1] // HD, group)


def back_kernel(
    relative, count_ref, w_ref, visual_ref, stats_ref, *refs
):
    steps = lax.axis_size("head")
    inner, refs = refs[: 6 + 4 * CHUNKS], refs[6 + 4 * CHUNKS :]
    dqkv_ref, pair_ref, sums_ref = refs[:3]
    attend_back_heads(count_ref, inner, dqkv_ref, pair_ref)
    visual = stream_is_visual()
    tokens = visual_ref.shape[0]
    share = tokens // steps
    mean, scale = stats_ref[0:1, :], stats_ref[1:2, :]
    shift_sum = jnp.zeros(mean.shape, F32)
    gain_sum = jnp.zeros(mean.shape, F32)
    for k in range(steps):
        if relative:
            start = pl.multiple_of((lax.axis_index("head") ^ k) * share, share)
            target = refs[3 + k % 2].at[k // 2]
        else:
            start = k * share
            target = refs[3].at[k]
        rows = pl.ds(start, share)
        part = functools.reduce(
            jnp.add, (dot(dqkv_ref[m, rows, :], w_ref[m], NT) for m in range(3))
        )
        target[...] = part.astype(target.dtype)
        keep = jnp.logical_and(visual, iota((share, 1), 0) + start < count_ref[0]).astype(F32)
        kept = part * keep
        shift_sum = shift_sum + jnp.sum(kept, axis=0, keepdims=True)
        hat = (visual_ref[rows, :].astype(F32) - mean) * scale
        gain_sum = gain_sum + jnp.sum(kept * hat, axis=0, keepdims=True)
    sums_ref[...] = jnp.concatenate(
        [shift_sum, gain_sum, jnp.zeros((6, mean.shape[1]), F32)], axis=0
    )


def join_pair_kernel(keep_ref, other_ref, own_ref, send_ref):
    own_ref[...] = keep_ref[0] + other_ref[0].astype(F32)
    send_ref[...] = (keep_ref[1] + other_ref[1].astype(F32)).astype(BF16)


def table_sums(pair_refs):
    table_width = NB_REL + 2 * NB_BOX
    sums = [[], [], []]
    for ref in pair_refs:
        for head in range(ref.shape[0]):
            turned = pltpu.roll(ref[head], LEVELS // 2 + 1, 1, stride=1, stride_axis=0)
            for n, (start, stop, unused_half, unused_offset) in enumerate(GROUPS):
                rows = turned[LEVELS - stop : LEVELS - start]
                sums[n].append(jnp.sum(rows, axis=0, keepdims=True))
    table = jnp.zeros((8, table_width), F32)
    offsets = LEVELS // 2 - iota((table_width, LEVELS), 1)
    for n, (unused_start, unused_stop, half, offset) in enumerate(GROUPS):
        missing = 8 - len(sums[n])
        stacked = jnp.concatenate(sums[n] + [jnp.zeros((missing, LEVELS), F32)], axis=0)
        table = table + picked(stacked, bucket_map(offsets, half, offset, table_width), NT)
    return table


def qkv_grad_kernel(fused, x_ref, dqkv_ref, pair_ref, *outs):
    tokens, width = x_ref.shape
    local_width = dqkv_ref.shape[2]
    table = table_sums((pair_ref,))
    x = x_ref[...]

    if not fused:
        grad_ref, table_ref = outs
        table_ref[...] = table
        for m in range(3):
            grad_ref[m] = dot(x, dqkv_ref[m], TN).astype(BF16)
        return
    mine_ref, sib_ref, whole = outs
    width_own = width // 8
    padded = jnp.concatenate(
        [
            jnp.concatenate([table, jnp.zeros((8, local_width - table.shape[1]), F32)], axis=1),
            jnp.zeros((8, local_width), F32),
        ],
        axis=0,
    )
    for m in range(3):
        whole[m] = dot(x, dqkv_ref[m], TN)
    for half, target in ((1, sib_ref), (0, mine_ref)):
        for k in range(4):
            rows = pl.ds(pl.multiple_of(owner_of(half, k) * width_own, 8), width_own)
            tall = jnp.concatenate([whole[m, rows, :] for m in range(3)] + [padded], axis=0)
            middle = tall.shape[0] // 2
            target[k] = jnp.concatenate([tall[:middle], tall[middle:]], axis=1).astype(
                target.dtype
            )


def finish_grads_kernel(hidden_width, *refs):
    block_refs, outs = refs[:8], refs[8:]
    grad_in, grad_out, grad_ow, bias_in, grad_qkv, grad_table = outs[:6]
    sums = [
        own[...] + other[...].astype(F32) for own, other in zip(block_refs[::2], block_refs[1::2])
    ]
    total = jnp.concatenate(sums, axis=0)
    width = total.shape[1]
    part_in = grad_in.shape[0]
    part_out = grad_out.shape[0]
    half_own = grad_ow.shape[1] // 2
    local_width = grad_ow.shape[0]
    parts = hidden_width // width
    place = lax.axis_index("dp") * lax.axis_size("head") + lax.axis_index("head")
    grad_in[...] = jnp.concatenate(
        [total[p * part_in : (p + 1) * part_in] for p in range(parts)], axis=1
    )
    base = parts * part_in
    vec = total[base : base + VEC_ROWS]
    base += VEC_ROWS
    grad_out[...] = total[base : base + part_out]
    base += part_out
    packed = total[base : base + half_own]
    grad_ow[...] = jnp.transpose(
        jnp.concatenate([packed[:, :local_width], packed[:, local_width:]], axis=0)
    )
    base += half_own
    lane = iota((width, 128), 0)
    column = iota((width, 128), 1)
    own = picked(vec, one_hot((lane == place * part_in + column) & (column < part_in)))
    for row, out in zip((0, 1, 2, 7, 8, 9), outs[6:]):
        out[...] = own[row : row + 1, :part_in]
    first = place * part_out
    wide = picked(
        vec, one_hot((lane == lax.rem(first, width) + column) & (column < part_out))
    )
    row = iota((VEC_ROWS, 128), 0)
    chosen = jnp.where(row == 3 + lax.div(first, width), wide, 0.0)
    bias_in[...] = jnp.sum(chosen, axis=0, keepdims=True)[:, :part_out]
    grads = jnp.concatenate([total[base:, :local_width], total[base:, local_width:]], axis=0)
    width_own = grad_qkv.shape[1]
    for m in range(3):
        grad_qkv[m] = grads[m * width_own : (m + 1) * width_own]
    table = grads[3 * width_own : 3 * width_own + 8]
    buckets = grad_table.shape[1]
    lane = iota((local_width, 128), 0)
    column = iota((local_width, 128), 1)
    start = lax.axis_index("dp") * buckets
    cut = picked(table, one_hot((lane == start + column) & (column < buckets)))
    grad_table[...] = cut[: grad_table.shape[0], :buckets]


def finish_inputs_kernel(steps, relative, sums, count_ref, visual_ref, stats_ref, *refs):
    share_refs, refs = refs[:CHUNKS], refs[CHUNKS:]
    part_refs, refs = refs[: 1 + relative], refs[1 + relative :]
    sum_refs, refs = refs[:sums], refs[sums:]
    text_ref, grad_ref, gain_ref, shift_ref = refs
    head_rank = lax.axis_index("head")
    share = text_ref.shape[0]
    half = steps // 2
    if relative:
        same, other = (ref[...].astype(F32) for ref in part_refs)
        text = jnp.where(stream_is_visual(), other, same)
        visual = jnp.where(stream_is_visual(), same, other)
    else:
        text, visual = (
            functools.reduce(
                jnp.add, (part_refs[0][k].astype(F32) for k in range(start, start + half))
            )
            for start in (0, half)
        )
    text_ref[...] = functools.reduce(jnp.add, (ref[...] for ref in share_refs)) + text
    total = functools.reduce(jnp.add, (ref[...] for ref in sum_refs))
    mean, scale, gain, number = (stats_ref[i : i + 1, :] for i in range(4))
    start = pl.multiple_of(head_rank * share, share)
    keep = (iota((share, 1), 0) + start < count_ref[0]).astype(F32)
    hat = (visual_ref[pl.ds(start, share), :].astype(F32) - mean) * keep * scale
    dnormed = visual * keep
    shift_gradient, gain_gradient = total[0:1], total[1:2]
    shift_ref[...] = shift_gradient
    gain_ref[...] = gain_gradient
    grad_ref[...] = (
        keep
        * scale
        * gain
        * (dnormed - shift_gradient / number - hat * gain_gradient / number)
    )


def swap(value, axis, mask):
    size = lax.axis_size(axis)
    return lax.ppermute(value, axis, [(i, i ^ mask) for i in range(size)])


def after(value, *earlier):
    return lax.optimization_barrier((value, *earlier))[0]


def gather_heads(chunks):
    return [[piece] + [swap(piece, "head", k) for k in (1, 2, 3)] for piece in chunks]


def across_chips(mine, other, plans, sizes, name):
    axes = {X_FIRST: (2, 4), Y_FIRST: (4, 2)}
    width = mine.shape[2]
    outs = []
    for size in sizes:
        outs += [((2, size, width), F32), ((2, size, width), BF16)]
    joined = call(functools.partial(join_cores_kernel, plans), name, 1, outs, [mine, other])
    return [
        (keep, swap(send, "dp", axes[plan][0]), axes[plan][1])
        for plan, keep, send in zip(plans, joined[::2], joined[1::2])
    ]


def second_exchange(stages, name, earlier=()):
    outs = []
    args = []
    for keep, other, mask in stages:
        outs += [(keep.shape[1:], F32), (keep.shape[1:], BF16)]
        args += [keep, other]
    args[1] = after(args[1], *earlier)
    joined = call(join_chips_kernel, name, 1, outs, args)
    blocks = []
    for n, stage in enumerate(stages):
        blocks += [joined[2 * n], swap(joined[2 * n + 1], "dp", stage[2])]
    return blocks, joined


def per_device(
    text_in,
    visual_in,
    visual_count,
    line_index,
    box_index,
    qkv_weight,
    bias_table,
    out_weight,
    out_bias,
    norm1_gain,
    norm1_shift,
    ffn_weight_in,
    ffn_bias_in,
    ffn_weight_out,
    ffn_bias_out,
    norm2_gain,
    norm2_shift,
    batch_gain,
    batch_shift,
    cotangent,
):
    tokens, width = text_in.shape
    local_width = qkv_weight.shape[2]
    heads_local = local_width // HD
    head_count = lax.axis_size("head")
    dp_count = lax.axis_size("dp")
    head_rank = lax.axis_index("head")
    dp_rank = lax.axis_index("dp")
    fused = head_count == 4 and dp_count == 8
    share = tokens // head_count
    block = tokens // CHUNKS
    hidden_width = ffn_weight_in.shape[1]
    table_width = bias_table.shape[1]
    part_in = width // (dp_count * head_count)
    part_out = hidden_width // (dp_count * head_count)
    weight = jnp.transpose(qkv_weight, (1, 0, 2))
    row_vectors = [
        value.reshape(1, width)
        for value in (
            out_bias,
            norm1_gain,
            norm1_shift,
            ffn_bias_out,
            norm2_gain,
            norm2_shift,
            batch_gain,
            batch_shift,
        )
    ]

    packed_shape = ((8, width), F32)
    (packed,) = call(
        stats_kernel, "stats", 2, [packed_shape], [visual_in], visual_count
    )
    if fused:
        (packed,) = call(
            join_stats_kernel, "join_stats", 1, [packed_shape], [packed, swap(packed, "dp", 1)]
        )
        packed = [packed] + [swap(packed, "dp", k) for k in (2, 4, 6)]
    else:
        gathered = lax.all_gather(packed, "dp")
        packed = [gathered[i] for i in range(dp_count)]
    one, back, tab, small, bias_in = call(
        prep_kernel,
        "prep",
        2,
        [
            ((tokens, LEVELS), BF16),
            ((LEVELS, tokens), BF16),
            ((LEVELS, heads_local * LEVELS), BF16),
            ((8, width), F32),
            ((8, width), F32),
        ],
        [line_index, box_index, bias_table, ffn_bias_in.reshape(1, hidden_width)] + row_vectors,
        visual_count,
    )

    rows = ((tokens, local_width), BF16)
    turned = ((local_width, tokens), BF16)
    left = [pltpu.VMEM((block, heads_local * LEVELS), BF16)]
    chunk_outs = [((local_width, block), BF16), ((heads_local, tokens, block), BF16)]
    stats, x, q, k, v, kt, vt, heads_one, prob_one = call(
        functools.partial(attend_first_kernel, len(packed)),
        "attend_first",
        6,
        [packed_shape, ((tokens, width), BF16), rows, rows, rows, turned, turned] + chunk_outs,
        [text_in, visual_in, small, weight, tab, one] + packed,
        visual_count,
        scratch=left,
        final=(1,),
    )
    heads_two, prob_two = call(
        functools.partial(attend_chunk, 1),
        "attend_second",
        3,
        chunk_outs,
        [q, k, vt, tab, one],
        visual_count,
        scratch=left,
    )
    heads = (heads_one, heads_two)
    if fused:
        pieces = gather_heads(heads)
    else:
        pieces = []
        for piece in heads:
            gathered = lax.all_gather(piece, "head")
            pieces.append([gathered[i] for i in range(head_count)])

    results = []
    for c in range(CHUNKS):
        text = after(text_in, results[-1][-1]) if results else text_in
        results.append(
            call(
                functools.partial(ffn_kernel, c, fused, len(pieces[c])),
                f"ffn_{c}",
                9,
                [
                    ((block, width), BF16),
                    ((share, width), F32),
                    ((block, hidden_width), BF16),
                    ((block, hidden_width), BF16),
                    ((block, width), BF16),
                    ((block, width), BF16),
                    ((block, width), BF16),
                    ((block, local_width), BF16),
                    ((local_width, block), BF16),
                    ((VEC_ROWS, width), F32),
                ],
                [text, cotangent, out_weight, ffn_weight_in, ffn_weight_out, small, bias_in]
                + list(pieces[c]),
                scratch=[pltpu.VMEM((block, hidden_width), F32)],
            )
        )
    out, dh_share, act, dpre, low, branch, mix, dheads, dheads_t, vec = zip(*results)
    if fused:
        in_rows = hidden_width // width * part_in + VEC_ROWS
        out_rows = part_out + width // dp_count // 2
        mine, sib = call(
            weight_grad_in_kernel,
            "weight_grad_in",
            2,
            [((4, in_rows, width), F32), ((4, in_rows, width), BF16)],
            [*low, *dpre, *vec],
        )
        other = swap(sib, "dp", 1)
        layer_out, mine_out, sib_out = call(
            weight_grad_out_kernel,
            "weight_grad_out",
            3,
            [
                ((tokens, width), BF16),
                ((4, out_rows, width), F32),
                ((4, out_rows, width), BF16),
            ],
            [after(out[0], sib), *out[1:], *act, *branch, *mix, *heads],
            scratch=[pltpu.VMEM((width, local_width), F32)],
            final=(0,),
        )
        other_out = swap(sib_out, "dp", 1)
        ffn_stages = across_chips(mine, other, [X_FIRST], [in_rows], "join_cores_in")
        ffn_stages += across_chips(mine_out, other_out, [Y_FIRST], [out_rows], "join_cores_out")
    inner = [q, k, v, kt, one, back, *heads, *dheads, *dheads_t, prob_one, prob_two]
    if fused:
        inner[0] = after(q, *(stage[0] for stage in ffn_stages))
        part_outs = [((2, share, width), F32), ((2, share, width), BF16)]
    else:
        part_outs = [((head_count, share, width), BF16)]
    dqkv, pairs, sums, *parts = call(
        functools.partial(back_kernel, fused),
        "back",
        10,
        [
            ((3, tokens, local_width), BF16),
            ((heads_local, LEVELS, LEVELS), F32),
            packed_shape,
        ]
        + part_outs,
        [weight, visual_in, stats] + inner,
        visual_count,
    )
    if fused:
        keep, send = parts
        near = swap(send, "head", 1)
        sums = sums + swap(sums, "dp", 1)
        ffn_blocks, ffn_joined = second_exchange(ffn_stages, "join_chips_ffn", [sums])
        sums = sums + swap(sums, "dp", 2)
        block_rows = 3 * (width // dp_count) + 16
        mine, sib = call(
            functools.partial(qkv_grad_kernel, True),
            "qkv_grad",
            3,
            [
                ((4, block_rows // 2, 2 * local_width), F32),
                ((4, block_rows // 2, 2 * local_width), BF16),
            ],
            [after(x, ffn_joined[0]), dqkv, pairs],
            scratch=[pltpu.VMEM((3, width, local_width), F32)],
        )
        first_rows = block_rows // 4 // 8 * 8
        stages = across_chips(
            mine,
            after(swap(sib, "dp", 1), sums),
            [X_FIRST, Y_FIRST],
            [first_rows, block_rows // 2 - first_rows],
            "join_cores_qkv",
        )
        sums = sums + swap(sums, "dp", 4)
        qkv_blocks, unused_joined = second_exchange(stages, "join_chips_qkv", ffn_blocks)
        same, send = call(
            join_pair_kernel,
            "join_pair",
            1,
            [((share, width), F32), ((share, width), BF16)],
            [keep, after(near, sums)],
        )
        received = [same, swap(send, "head", 2)]
        sums = sums + swap(sums, "head", 1)
        sums = [sums, swap(sums, "head", 2)]
        blocks = ffn_blocks + qkv_blocks
        one_row = ((1, part_in), F32)
        grad_in, grad_out, grad_ow, grad_bias_in, grad_qkv, grad_table, *own = call(
            functools.partial(finish_grads_kernel, hidden_width),
            "finish_grads",
            2,
            [
                ((part_in, hidden_width), F32),
                ((part_out, width), F32),
                ((local_width, width // dp_count), F32),
                ((1, part_out), F32),
                ((3, width // dp_count, local_width), F32),
                ((heads_local, table_width // dp_count), F32),
            ]
            + [one_row] * 6,
            blocks,
            final=range(12),
        )
        grad_bias_in = grad_bias_in.reshape(part_out)
        grad_qkv = jnp.transpose(grad_qkv, (1, 0, 2))
        own = [value.reshape(part_in) for value in own]
    else:
        layer_out = jnp.concatenate(out, axis=0)
        act, dpre, low, branch, mix = (
            jnp.concatenate(value, axis=0) for value in (act, dpre, low, branch, mix)
        )

        def scatter(value, dimension):
            return lax.psum_scatter(
                value.astype(BF16), "dp", scatter_dimension=dimension, tiled=True
            ).astype(F32)

        def own_columns(value, part):
            split = value.reshape(tokens, dp_count, head_count, part)
            return lax.dynamic_index_in_dim(split, head_rank, 2, keepdims=False).reshape(
                tokens, dp_count * part
            )

        grad_in = scatter(dot(own_columns(low, part_in), dpre, TN), 0)
        grad_out = scatter(dot(own_columns(act, part_out), branch, TN), 0)
        grad_ow = scatter(dot(jnp.concatenate(heads, axis=1), mix), 1)
        vec = lax.psum((vec[0] + vec[1]).astype(BF16), "dp").astype(F32)
        place = dp_rank * head_count + head_rank
        own = [
            lax.dynamic_slice_in_dim(vec[row], place * part_in, part_in, 0)
            for row in (0, 1, 2, 7, 8, 9)
        ]
        grad_bias_in = lax.dynamic_slice_in_dim(
            vec[3 : 3 + hidden_width // width].reshape(hidden_width), place * part_out, part_out, 0
        )
        sums = [lax.psum(sums, ("dp", "head"))]
        grad, table = call(
            functools.partial(qkv_grad_kernel, False),
            "qkv_grad",
            3,
            [((3, width, local_width), BF16), ((8, table_width), F32)],
            [x, dqkv, pairs],
        )
        received = [lax.all_to_all(parts[0], "head", 0, 0, tiled=True)]
        grad_qkv = jnp.transpose(scatter(grad, 1), (1, 0, 2))
        grad_table = scatter(table[:heads_local], 1)

    grad_text, grad_visual, gain_gradient, shift_gradient = call(
        functools.partial(finish_inputs_kernel, head_count, fused, len(sums)),
        "finish_inputs",
        2,
        [((share, width), F32)] * 2 + [((1, width), F32)] * 2,
        [visual_in, stats, *dh_share, *received, *sums],
        visual_count,
        final=range(4),
    )
    return (
        layer_out,
        grad_text,
        grad_visual,
        grad_qkv,
        grad_table,
        grad_ow,
        own[0],
        own[1],
        own[2],
        grad_in,
        grad_bias_in,
        grad_out,
        own[3],
        own[4],
        own[5],
        gain_gradient.reshape(width),
        shift_gradient.reshape(width),
    )


def solution(mesh):
    in_specs = (
        P("dp", None),
        P("dp", None),
        P("dp"),
        P(None, "dp"),
        P(None, None, "dp"),
        P(None, None, "head"),
        P("head", None),
        P(),
        P(),
        P(),
        P(),
        P(),
        P(),
        P(),
        P(),
        P(),
        P(),
        P(),
        P(),
        P("dp", None),
    )
    out_specs = (
        P("dp", None),
        P(("dp", "head"), None),
        P(("dp", "head"), None),
        P("dp", None, "head"),
        P("head", "dp"),
        P("head", "dp"),
        P(("dp", "head")),
        P(("dp", "head")),
        P(("dp", "head")),
        P(("dp", "head"), None),
        P(("dp", "head")),
        P(("dp", "head"), None),
        P(("dp", "head")),
        P(("dp", "head")),
        P(("dp", "head")),
        P(),
        P(),
    )
    return jax.shard_map(
        per_device, mesh=mesh, in_specs=in_specs, out_specs=out_specs, check_vma=False
    )
```

```python
import functools

import jax
import jax.numpy as jnp
from jax import lax
from jax.experimental import pallas as pl
from jax.experimental.pallas import tpu as pltpu
from jax.sharding import PartitionSpec as P

HD = 64
NB_REL = 32
NB_BOX = 16
LINES = 48
BOXES = 32

EPSILON = 1e-05
FLOOR_SCORE = -1000000000.0
SCALE = HD ** (-0.5)
LEVELS = 128
MASK_LANE = LINES + 2 * BOXES
VMEM_LIMIT = 12 * 1024 * 1024
VEC_ROWS = 16
CHUNKS = 2

F32 = jnp.float32
BF16 = jnp.bfloat16

NN = (((1,), (0,)), ((), ()))
NT = (((1,), (1,)), ((), ()))
TN = (((0,), (0,)), ((), ()))
TT = (((0,), (1,)), ((), ()))


def dot(left, right, dims=NN):
    return lax.dot_general(left, right, dims, preferred_element_type=F32)


def iota(shape, axis):
    return lax.broadcasted_iota(jnp.int32, shape, axis)


def one_hot(condition):
    return condition.astype(F32).astype(BF16)


def thirds(value):
    high = value.astype(BF16)
    rest = value - high.astype(F32)
    middle = rest.astype(BF16)
    return high, middle, (rest - middle.astype(F32)).astype(BF16)


def picked(value, selector, dims=NN):
    return functools.reduce(jnp.add, (dot(part, selector, dims) for part in thirds(value)))


def call(kernel, name, micros, outs, args, count=None, scratch=(), final=()):
    vmem = pl.BlockSpec(memory_space=pltpu.VMEM)
    scalars = [] if count is None else [count]
    return pl.pallas_call(
        kernel,
        out_shape=tuple(
            jax.ShapeDtypeStruct(*entry) if place in final else pltpu.VMEM(*entry)
            for place, entry in enumerate(outs)
        ),
        in_specs=[pl.BlockSpec(memory_space=pltpu.SMEM)] * len(scalars) + [vmem] * len(args),
        out_specs=tuple(vmem for entry in outs),
        scratch_shapes=list(scratch),
        compiler_params=pltpu.CompilerParams(vmem_limit_bytes=VMEM_LIMIT),
        cost_estimate=pl.CostEstimate(
            flops=int(micros * 1e9), bytes_accessed=int(micros * 3e6), transcendentals=0
        ),
        name=name,
    )(*scalars, *[pltpu.with_memory_space_constraint(a, pltpu.VMEM) for a in args])


def head_groups(heads_local, body, loop=True):
    if heads_local % 2 or not loop:
        for first in range(0, heads_local, 2):
            body(first, min(2, heads_local - first))
        return

    def step(pair, carry):
        body(pair * 2, 2)
        return carry

    lax.fori_loop(0, heads_local // 2, step, 0)


def lanes(first, heads, offset=0):
    start = offset + first * HD
    if isinstance(first, int):
        return slice(start, start + heads * HD)
    return pl.ds(pl.multiple_of(start, 128), heads * HD)


def stream_is_visual():
    return lax.axis_index("head") >= lax.axis_size("head") // 2


def stats_kernel(count_ref, visual_ref, out_ref):
    tokens, width = visual_ref.shape
    number = count_ref[0].astype(F32)
    keep = (iota((tokens, 1), 0) < count_ref[0]).astype(F32)
    visual = visual_ref[...].astype(F32)
    total = jnp.sum(visual * keep, axis=0, keepdims=True)
    centred = (visual - total / number) * keep
    spread = jnp.sum(centred * centred, axis=0, keepdims=True)
    out_ref[...] = jnp.concatenate(
        [total, spread, jnp.full((1, width), number, F32), jnp.zeros((5, width), F32)], axis=0
    )


def joined_stats(blocks):
    total = functools.reduce(jnp.add, (b[0:1] for b in blocks))
    number = functools.reduce(jnp.add, (b[2:3] for b in blocks))
    mean = total / number
    spread = functools.reduce(
        jnp.add, (b[1:2] + b[2:3] * (b[0:1] / b[2:3] - mean) ** 2 for b in blocks)
    )
    return total, spread, number


def join_stats_kernel(*refs):
    total, spread, number = joined_stats([ref[...] for ref in refs[:-1]])
    refs[-1][...] = jnp.concatenate(
        [total, spread, number, jnp.zeros((5, total.shape[1]), F32)], axis=0
    )


GROUPS = (
    (0, LINES, NB_REL // 2, 0),
    (LINES, LINES + BOXES, NB_BOX // 2, NB_REL),
    (LINES + BOXES, LINES + 2 * BOXES, NB_BOX // 2, NB_REL + NB_BOX),
)


def bucket_map(level, half, offset, table_width):
    bucket = jnp.clip(level, -half, half - 1) + half + offset
    return one_hot(bucket == iota((table_width, LEVELS), 0))


def same_group(row, lane):
    inside = jnp.zeros(row.shape, jnp.bool_)
    for start, stop, unused_half, unused_offset in GROUPS:
        inside = inside | ((row >= start) & (row < stop) & (lane >= start) & (lane < stop))
    return inside


def by_level(level, line, across, down):
    wanted = jnp.where(level < LINES, line, jnp.where(level < LINES + BOXES, across, down))
    return wanted == level


def prep_kernel(count_ref, line_ref, box_ref, table_ref, bias_ref, *refs):
    oh_ref, back_ref, tab_ref, small_ref, b1_ref = refs[8:]
    width = small_ref.shape[1]
    small_ref[...] = jnp.concatenate([ref[...] for ref in refs[:8]], axis=0)
    for c in range(bias_ref.shape[1] // width):
        b1_ref[c : c + 1, :] = bias_ref[:, c * width : (c + 1) * width]
    visual = stream_is_visual()
    tokens = line_ref.shape[1]
    heads_local, table_width = table_ref.shape
    line = jnp.where(visual, line_ref[1:2, :], line_ref[0:1, :])
    across = jnp.where(visual, box_ref[1, 0:1, :], box_ref[0, 0:1, :]) + LINES
    down = jnp.where(visual, box_ref[1, 1:2, :], box_ref[0, 1:2, :]) + (LINES + BOXES)
    level = iota((LEVELS, tokens), 0)
    back_ref[...] = one_hot(by_level(LEVELS - 1 - level, line, across, down))
    closed = jnp.logical_and(visual, iota((LEVELS, tokens), 1) >= count_ref[0])
    mask = jnp.where(closed, FLOOR_SCORE, 0.0)
    flags = by_level(level, line, across, down).astype(F32)
    oh_ref[...] = jnp.transpose(jnp.where(level == MASK_LANE, mask, flags)).astype(BF16)
    row = iota((LEVELS, LEVELS), 0)
    lane = iota((LEVELS, LEVELS), 1)
    inside = same_group(row, lane)
    offsets = iota((table_width, LEVELS), 1) - LEVELS // 2
    table = table_ref[...]
    spread = [
        picked(table, bucket_map(offsets, half, offset, table_width))
        for unused_start, unused_stop, half, offset in GROUPS
    ]
    for head in range(heads_local):
        rows = [jnp.broadcast_to(s[head : head + 1, :], (LEVELS, LEVELS)) for s in spread]
        chosen = jnp.where(row < LINES, rows[0], jnp.where(row < LINES + BOXES, rows[1], rows[2]))
        turned = pltpu.roll(chosen, LEVELS // 2, 1, stride=1, stride_axis=0)
        pairs = jnp.where(inside, turned, 0.0)
        high = jnp.where((lane == MASK_LANE) & (row < LINES), 1.0, pairs)
        tab_ref[:, head * LEVELS : (head + 1) * LEVELS] = high.astype(BF16)


def attend_chunk(
    chunk, count_ref, q_ref, k_ref, vt_ref, tab_ref, oh_ref, heads_ref, prob_ref, left_ref
):
    visual = stream_is_visual()
    tokens, local_width = q_ref.shape
    heads_local = local_width // HD
    block = heads_ref.shape[1]
    span = slice(chunk * block, (chunk + 1) * block)
    place = iota((1, block), 1) + chunk * block
    allowed = jnp.logical_or(jnp.logical_not(visual), place < count_ref[0]).astype(F32)
    one = oh_ref[...]
    left_ref[...] = dot(oh_ref[span, :], tab_ref[...]).astype(BF16)
    ones = jnp.ones((16, tokens), F32).astype(BF16)

    def group(first, heads):
        span_lanes = lanes(first, heads)
        queries = q_ref[span, span_lanes] * jnp.asarray(SCALE, BF16)
        keys = k_ref[:, span_lanes]
        values = vt_ref[span_lanes, :]
        biases = left_ref[:, lanes(2 * first, 2 * heads)]

        def scores(n):
            own = slice(n * HD, (n + 1) * HD)
            right = jnp.concatenate(
                [biases[:, n * LEVELS : (n + 1) * LEVELS], queries[:, own]], axis=1
            )
            return dot(jnp.concatenate([one, keys[:, own]], axis=1), right, NT)

        results = []
        following = scores(0)
        for n in range(heads):
            own = slice(n * HD, (n + 1) * HD)
            current = following
            if n + 1 < heads:
                following = scores(n + 1)
            shifted = jnp.exp(current - jnp.max(current, axis=0, keepdims=True))
            mixed = dot(jnp.concatenate([values[own], ones], axis=0), shifted.astype(BF16))
            share = 1.0 / mixed[HD : HD + 1]
            prob_ref[first + n] = (shifted * share).astype(BF16)
            results.append((mixed[:HD] * (share * allowed)).astype(BF16))
        heads_ref[span_lanes, :] = jnp.concatenate(results, axis=0)

    head_groups(heads_local, group, loop=chunk > 0)


def attend_first_kernel(pieces, count_ref, text_ref, visual_ref, small_ref, w_ref, tab_ref, oh_ref, *refs):
    piece_refs, refs = refs[:pieces], refs[pieces:]
    stats_ref, x_ref, q_ref, k_ref, v_ref, kt_ref, vt_ref, heads_ref, prob_ref, left_ref = refs
    visual = stream_is_visual()
    tokens, width = text_ref.shape
    total, spread, number = joined_stats([ref[...] for ref in piece_refs])
    mean = total / number
    scale = lax.rsqrt(spread / number + EPSILON)
    gain, shift = small_ref[6:7, :], small_ref[7:8, :]
    stats_ref[...] = jnp.concatenate(
        [mean, scale, gain, number, jnp.zeros((4, width), F32)], axis=0
    )

    @pl.when(visual)
    def _():
        keep = (iota((tokens, 1), 0) < count_ref[0]).astype(F32)
        centred = (visual_ref[...].astype(F32) - mean) * keep
        x_ref[...] = ((centred * scale * gain + shift) * keep).astype(BF16)

    @pl.when(jnp.logical_not(visual))
    def _():
        x_ref[...] = text_ref[...]

    x = x_ref[...]
    q_ref[...] = dot(x, w_ref[0]).astype(BF16)
    k_ref[...] = dot(x, w_ref[1]).astype(BF16)
    v_ref[...] = dot(x, w_ref[2]).astype(BF16)
    kt_ref[...] = dot(w_ref[1], x, TT).astype(BF16)
    vt_ref[...] = dot(w_ref[2], x, TT).astype(BF16)
    attend_chunk(
        0, count_ref, q_ref, k_ref, vt_ref, tab_ref, oh_ref, heads_ref, prob_ref, left_ref
    )


ERF_P = 0.3275911 * 0.7071067811865476
ERF_A = (0.254829592, -0.284496736, 1.421413741, -1.453152027, 1.061405429)


def gelu_parts(pre):
    t = 1.0 / (1.0 + ERF_P * jnp.abs(pre))
    bell = jnp.exp(-0.5 * pre * pre)
    poly = 0.5 * ERF_A[4]
    for coefficient in ERF_A[3::-1]:
        poly = poly * t + 0.5 * coefficient
    tail = poly * t * bell
    cdf = jnp.where(pre >= 0.0, 1.0 - tail, tail)
    return pre * cdf, cdf + pre * (bell * 0.3989422804014327)


def normed_rows(hidden):
    average = jnp.mean(hidden, axis=-1, keepdims=True)
    centred = hidden - average
    scale = lax.rsqrt(jnp.mean(centred * centred, axis=-1, keepdims=True) + EPSILON)
    return centred * scale, scale


def normed_back(upstream, hat, scale, gain):
    scaled = upstream * gain
    return scale * (
        scaled
        - jnp.mean(scaled, axis=-1, keepdims=True)
        - hat * jnp.mean(scaled * hat, axis=-1, keepdims=True)
    )


def ffn_kernel(chunk, relative, pieces, *refs):
    (text_ref, cot_ref, wo, w1, w2, small_ref, b1_ref), refs = refs[:7], refs[7:]
    piece_refs, refs = refs[:pieces], refs[pieces:]
    out_ref, share_ref, act_ref, dpre_ref, low_ref, branch_ref, mix_ref = refs[:7]
    dheads_ref, dheadst_ref, vec_ref, slope = refs[7:]
    local_width, block = piece_refs[0].shape
    width = text_ref.shape[1]
    hidden_width = w1.shape[1]
    head_rank = lax.axis_index("head")
    out_bias, gain1, shift1, b2, gain2, shift2 = (small_ref[i : i + 1, :] for i in range(6))
    parts = hidden_width // width
    share = share_ref.shape[0]
    rows = slice(chunk * block, (chunk + 1) * block)
    own_rows = pl.ds(pl.multiple_of(head_rank * local_width, 64), local_width)

    sources = [
        (ref[...], head_rank ^ index if relative else index)
        for index, ref in enumerate(piece_refs)
    ]
    mixed = text_ref[rows, :].astype(F32) + out_bias
    for piece, source in sources:
        wo_rows = pl.ds(pl.multiple_of(source * local_width, 64), local_width)
        mixed = mixed + dot(piece, wo[wo_rows, :], TN)
    hat1, scale1 = normed_rows(mixed)
    after = hat1 * gain1 + shift1
    after_low = after.astype(BF16)
    low_ref[...] = after_low
    branch = jnp.zeros((block, width), F32)
    for c in range(parts):
        cols = slice(c * width, (c + 1) * width)
        act, slope[:, cols] = gelu_parts(dot(after_low, w1[:, cols]) + b1_ref[c : c + 1, :])
        act = act.astype(BF16)
        act_ref[:, cols] = act
        branch = branch + dot(act, w2[cols, :])
    hat2, scale2 = normed_rows(after + (branch + b2))
    out_ref[...] = (hat2 * gain2 + shift2).astype(BF16)
    upstream = cot_ref[rows, :].astype(F32)
    dh_two = normed_back(upstream, hat2, scale2, gain2)
    dbranch = dh_two.astype(BF16)
    branch_ref[...] = dbranch
    vec = [None] * 3
    dy = dh_two
    for c in range(parts):
        cols = slice(c * width, (c + 1) * width)
        dpre = (dot(dbranch, w2[cols, :], NT) * slope[:, cols]).astype(BF16)
        dpre_ref[:, cols] = dpre
        vec.append(dpre.astype(F32))
        dy = dy + dot(dpre, w1[:, cols], NT)
    dh_one = normed_back(dy, hat1, scale1, gain1)
    vec[:3] = [dh_one, dy * hat1, dy]
    vec += [dbranch.astype(F32), upstream * hat2, upstream]
    sums = [jnp.sum(v, axis=0, keepdims=True) for v in vec]
    vec_ref[...] = jnp.concatenate(
        sums + [jnp.zeros((VEC_ROWS - len(sums), width), F32)], axis=0
    )
    share_ref[...] = jnp.zeros_like(share_ref)
    per_block = block // share
    for part in range(per_block):

        @pl.when(head_rank == chunk * per_block + part)
        def _():
            share_ref[...] = dh_one[part * share : (part + 1) * share]

    dmix = dh_one.astype(BF16)
    mix_ref[...] = dmix
    dheads_ref[...] = dot(dmix, wo[own_rows, :], NT).astype(BF16)
    dheadst_ref[...] = dot(wo[own_rows, :], dmix, NT).astype(BF16)


def owner_of(half, step):
    place = lax.axis_index("dp")
    core = place & 1
    return (((place >> 1) ^ step) << 1) | (core if half == 0 else 1 - core)


def own_order():
    return [owner_of(half, step) for half in range(2) for step in range(4)]


def weight_grad_in_kernel(*refs):
    head_rank = lax.axis_index("head")
    low_refs, dpre_refs, vec_refs = (refs[i * CHUNKS : (i + 1) * CHUNKS] for i in range(3))
    mine_ref, sib_ref = refs[3 * CHUNKS :]
    width = low_refs[0].shape[1]
    parts = dpre_refs[0].shape[1] // width
    width_own = width // 8
    part_in = width_own // 4
    lane = iota((part_in, width), 1)
    row = iota((part_in, width), 0)
    pick = jnp.concatenate(
        [
            (lane == owner * width_own + head_rank * part_in + row).astype(F32)
            for owner in own_order()
        ],
        axis=0,
    ).astype(BF16)
    low_t = [dot(pick, low[...], NT).astype(BF16) for low in low_refs]
    grads = []
    for p in range(parts):
        cols = slice(p * width, (p + 1) * width)
        grads.append(
            functools.reduce(
                jnp.add, (dot(low_t[c], dpre_refs[c][:, cols]) for c in range(CHUNKS))
            )
        )
    vec = functools.reduce(jnp.add, (v[...] for v in vec_refs))
    for n in range(8):
        rows = slice(n * part_in, (n + 1) * part_in)
        block = jnp.concatenate([grad[rows] for grad in grads] + [vec], axis=0)
        target = mine_ref if n < 4 else sib_ref
        target[n % 4] = block.astype(target.dtype)


def weight_grad_out_kernel(*refs):
    head_rank = lax.axis_index("head")
    names = ("out", "act", "branch", "mix", "heads")
    groups = {name: refs[i * CHUNKS : (i + 1) * CHUNKS] for i, name in enumerate(names)}
    layer_ref, mine_ref, sib_ref, whole = refs[len(names) * CHUNKS :]
    block, width = groups["out"][0].shape
    hidden_width = groups["act"][0].shape[1]
    owners = own_order()
    width_own = width // 8
    window = hidden_width // 8
    part_out = window // 4
    half_own = width_own // 2
    for c in range(CHUNKS):
        layer_ref[c * block : (c + 1) * block, :] = groups["out"][c][...]
    whole[...] = functools.reduce(
        jnp.add, (dot(groups["mix"][c][...], groups["heads"][c][...], TT) for c in range(CHUNKS))
    )
    pick = one_hot(
        iota((part_out, window), 1) == head_rank * part_out + iota((part_out, window), 0)
    )
    grad = jnp.zeros((8 * part_out, width), F32)
    for c in range(CHUNKS):
        stacked = []
        for owner in owners:
            cols = pl.ds(pl.multiple_of(owner * window, 128), window)
            stacked.append(dot(pick, groups["act"][c][:, cols], NT).astype(BF16))
        grad = grad + dot(jnp.concatenate(stacked, axis=0), groups["branch"][c][...])
    for n, owner in enumerate(owners):
        start = pl.multiple_of(owner * width_own, 8)
        packed = jnp.concatenate(
            [whole[pl.ds(start, half_own), :], whole[pl.ds(start + half_own, half_own), :]],
            axis=1,
        )
        target = mine_ref if n < 4 else sib_ref
        target[n % 4] = jnp.concatenate(
            [grad[n * part_out : (n + 1) * part_out], packed], axis=0
        ).astype(target.dtype)


X_FIRST = ((0, 2), (1, 3))
Y_FIRST = ((0, 1), (2, 3))


def join_cores_kernel(plans, *refs):
    mine_ref, other_ref, outs = refs[0], refs[1], refs[2:]
    start = 0
    for (keep, send), keep_ref, send_ref in zip(plans, outs[::2], outs[1::2]):
        rows = slice(start, start + keep_ref.shape[1])
        start = rows.stop
        for places, out in ((keep, keep_ref), (send, send_ref)):
            for n, place in enumerate(places):
                total = mine_ref[place, rows, :] + other_ref[place, rows, :].astype(F32)
                out[n] = total.astype(out.dtype)


def join_chips_kernel(*refs):
    count = len(refs) // 4
    ins, outs = refs[: 2 * count], refs[2 * count :]
    for n in range(count):
        keep, other = ins[2 * n : 2 * n + 2]
        for m, out in enumerate(outs[2 * n : 2 * n + 2]):
            out[...] = (keep[m] + other[m].astype(F32)).astype(out.dtype)


def attend_back_heads(count_ref, refs, dqkv_ref, pair_ref):
    q_ref, k_ref, v_ref, kt_ref, oh_ref, back_ref = refs[:6]
    groups = [refs[6 + i * CHUNKS : 6 + (i + 1) * CHUNKS] for i in range(4)]
    head_refs, dhead_refs, dheadt_refs, prob_refs = groups
    visual = stream_is_visual()
    tokens = q_ref.shape[0]
    block = tokens // CHUNKS
    count = count_ref[0]
    one = oh_ref[...]
    back = back_ref[...]
    inside = same_group(LEVELS - 1 - iota((LEVELS, LEVELS), 0), iota((LEVELS, LEVELS), 1))
    extra = one_hot(iota((tokens, 16), 1) < 2)
    sublane = iota((16, block), 0)
    free = jnp.logical_not(visual)
    rows_open = []
    lanes_open = []
    for c in range(CHUNKS):
        rows_open.append(
            jnp.logical_or(free, iota((block, 1), 0) + c * block < count).astype(BF16)
        )
        lanes_open.append(
            jnp.logical_or(free, iota((1, block), 1) + c * block < count).astype(BF16)
        )

    def group(first, heads):
        span_lanes = lanes(first, heads)
        turned = [[], [], []]
        for n in range(heads):
            own = slice(n * HD, (n + 1) * HD)
            left = jnp.concatenate([v_ref[:, span_lanes][:, own], extra], axis=1)
            below = jnp.concatenate([back, kt_ref[span_lanes, :][own]], axis=0)
            dquery_t = []
            dkey = jnp.zeros((tokens, HD), F32)
            dvalue = jnp.zeros((tokens, HD), F32)
            pairs = jnp.zeros((LEVELS, LEVELS), F32)
            for c in range(CHUNKS):
                span = slice(c * block, (c + 1) * block)
                dout = dhead_refs[c][:, span_lanes][:, own] * rows_open[c]
                dout_t = dheadt_refs[c][span_lanes, :][own] * lanes_open[c]
                inner = -jnp.sum(
                    dout_t.astype(F32) * head_refs[c][span_lanes, :][own].astype(F32),
                    axis=0,
                    keepdims=True,
                )
                high = inner.astype(BF16).astype(F32)
                tail = jnp.where(sublane == 0, high, jnp.where(sublane == 1, inner - high, 0.0))
                centred = dot(left, jnp.concatenate([dout_t, tail.astype(BF16)], axis=0))
                prob = prob_refs[c][first + n]
                dscore = (prob.astype(F32) * centred).astype(BF16)
                both = dot(below, dscore)
                level = both[:LEVELS]
                level_high = level.astype(BF16)
                level_low = (level - level_high.astype(F32)).astype(BF16)
                one_part = one[span, :]
                pairs = pairs + dot(level_high, one_part) + dot(level_low, one_part)
                dquery_t.append(both[LEVELS:] * SCALE)
                dkey = dkey + dot(dscore, q_ref[span, span_lanes][:, own])
                dvalue = dvalue + dot(prob, dout)
            pair_ref[first + n] = jnp.where(inside, pairs, 0.0)
            turned[0].append(jnp.concatenate(dquery_t, axis=1))
            turned[1].append(dkey * SCALE)
            turned[2].append(dvalue)
        for m in range(3):
            joined = jnp.concatenate(turned[m], axis=0 if m == 0 else 1)
            if m == 0:
                joined = jnp.transpose(joined)
            dqkv_ref[m, :, span_lanes] = joined.astype(BF16)

    head_groups(q_ref.shape[1] // HD, group)


def back_kernel(
    relative, count_ref, w_ref, visual_ref, stats_ref, *refs
):
    steps = lax.axis_size("head")
    inner, refs = refs[: 6 + 4 * CHUNKS], refs[6 + 4 * CHUNKS :]
    dqkv_ref, pair_ref, sums_ref = refs[:3]
    attend_back_heads(count_ref, inner, dqkv_ref, pair_ref)
    visual = stream_is_visual()
    tokens = visual_ref.shape[0]
    share = tokens // steps
    mean, scale = stats_ref[0:1, :], stats_ref[1:2, :]
    shift_sum = jnp.zeros(mean.shape, F32)
    gain_sum = jnp.zeros(mean.shape, F32)
    for k in range(steps):
        if relative:
            start = pl.multiple_of((lax.axis_index("head") ^ k) * share, share)
            target = refs[3 + k % 2].at[k // 2]
        else:
            start = k * share
            target = refs[3].at[k]
        rows = pl.ds(start, share)
        part = functools.reduce(
            jnp.add, (dot(dqkv_ref[m, rows, :], w_ref[m], NT) for m in range(3))
        )
        target[...] = part.astype(target.dtype)
        keep = jnp.logical_and(visual, iota((share, 1), 0) + start < count_ref[0]).astype(F32)
        kept = part * keep
        shift_sum = shift_sum + jnp.sum(kept, axis=0, keepdims=True)
        hat = (visual_ref[rows, :].astype(F32) - mean) * scale
        gain_sum = gain_sum + jnp.sum(kept * hat, axis=0, keepdims=True)
    sums_ref[...] = jnp.concatenate(
        [shift_sum, gain_sum, jnp.zeros((6, mean.shape[1]), F32)], axis=0
    )


def join_pair_kernel(keep_ref, other_ref, own_ref, send_ref):
    own_ref[...] = keep_ref[0] + other_ref[0].astype(F32)
    send_ref[...] = (keep_ref[1] + other_ref[1].astype(F32)).astype(BF16)


def table_sums(pair_refs):
    table_width = NB_REL + 2 * NB_BOX
    sums = [[], [], []]
    for ref in pair_refs:
        for head in range(ref.shape[0]):
            turned = pltpu.roll(ref[head], LEVELS // 2 + 1, 1, stride=1, stride_axis=0)
            for n, (start, stop, unused_half, unused_offset) in enumerate(GROUPS):
                rows = turned[LEVELS - stop : LEVELS - start]
                sums[n].append(jnp.sum(rows, axis=0, keepdims=True))
    table = jnp.zeros((8, table_width), F32)
    offsets = LEVELS // 2 - iota((table_width, LEVELS), 1)
    for n, (unused_start, unused_stop, half, offset) in enumerate(GROUPS):
        missing = 8 - len(sums[n])
        stacked = jnp.concatenate(sums[n] + [jnp.zeros((missing, LEVELS), F32)], axis=0)
        table = table + picked(stacked, bucket_map(offsets, half, offset, table_width), NT)
    return table


def qkv_grad_kernel(fused, x_ref, dqkv_ref, pair_ref, *outs):
    tokens, width = x_ref.shape
    local_width = dqkv_ref.shape[2]
    table = table_sums((pair_ref,))
    x = x_ref[...]

    if not fused:
        grad_ref, table_ref = outs
        table_ref[...] = table
        for m in range(3):
            grad_ref[m] = dot(x, dqkv_ref[m], TN).astype(BF16)
        return
    mine_ref, sib_ref, whole = outs
    width_own = width // 8
    padded = jnp.concatenate(
        [
            jnp.concatenate([table, jnp.zeros((8, local_width - table.shape[1]), F32)], axis=1),
            jnp.zeros((8, local_width), F32),
        ],
        axis=0,
    )
    for m in range(3):
        whole[m] = dot(x, dqkv_ref[m], TN)
    for half, target in ((1, sib_ref), (0, mine_ref)):
        for k in range(4):
            rows = pl.ds(pl.multiple_of(owner_of(half, k) * width_own, 8), width_own)
            tall = jnp.concatenate([whole[m, rows, :] for m in range(3)] + [padded], axis=0)
            middle = tall.shape[0] // 2
            target[k] = jnp.concatenate([tall[:middle], tall[middle:]], axis=1).astype(
                target.dtype
            )


def finish_grads_kernel(hidden_width, *refs):
    block_refs, outs = refs[:8], refs[8:]
    grad_in, grad_out, grad_ow, bias_in, grad_qkv, grad_table = outs[:6]
    sums = [
        own[...] + other[...].astype(F32) for own, other in zip(block_refs[::2], block_refs[1::2])
    ]
    total = jnp.concatenate(sums, axis=0)
    width = total.shape[1]
    part_in = grad_in.shape[0]
    part_out = grad_out.shape[0]
    half_own = grad_ow.shape[0] // 2
    local_width = grad_ow.shape[1]
    parts = hidden_width // width
    place = lax.axis_index("dp") * lax.axis_size("head") + lax.axis_index("head")
    grad_in[...] = jnp.concatenate(
        [total[p * part_in : (p + 1) * part_in] for p in range(parts)], axis=1
    )
    base = parts * part_in
    vec = total[base : base + VEC_ROWS]
    base += VEC_ROWS
    grad_out[...] = total[base : base + part_out]
    base += part_out
    packed = total[base : base + half_own]
    grad_ow[...] = jnp.concatenate([packed[:, :local_width], packed[:, local_width:]], axis=0)
    base += half_own
    lane = iota((width, 128), 0)
    column = iota((width, 128), 1)
    own = picked(vec, one_hot((lane == place * part_in + column) & (column < part_in)))
    for row, out in zip((0, 1, 2, 7, 8, 9), outs[6:]):
        out[...] = own[row : row + 1, :part_in]
    first = place * part_out
    wide = picked(
        vec, one_hot((lane == lax.rem(first, width) + column) & (column < part_out))
    )
    row = iota((VEC_ROWS, 128), 0)
    chosen = jnp.where(row == 3 + lax.div(first, width), wide, 0.0)
    bias_in[...] = jnp.sum(chosen, axis=0, keepdims=True)[:, :part_out]
    grads = jnp.concatenate([total[base:, :local_width], total[base:, local_width:]], axis=0)
    width_own = grad_qkv.shape[1]
    for m in range(3):
        grad_qkv[m] = grads[m * width_own : (m + 1) * width_own]
    table = grads[3 * width_own : 3 * width_own + 8]
    buckets = grad_table.shape[1]
    lane = iota((local_width, 128), 0)
    column = iota((local_width, 128), 1)
    start = lax.axis_index("dp") * buckets
    cut = picked(table, one_hot((lane == start + column) & (column < buckets)))
    grad_table[...] = cut[: grad_table.shape[0], :buckets]


def finish_inputs_kernel(steps, relative, sums, count_ref, visual_ref, stats_ref, *refs):
    share_refs, refs = refs[:CHUNKS], refs[CHUNKS:]
    part_refs, refs = refs[: 1 + relative], refs[1 + relative :]
    sum_refs, refs = refs[:sums], refs[sums:]
    text_ref, grad_ref, gain_ref, shift_ref = refs
    head_rank = lax.axis_index("head")
    share = text_ref.shape[0]
    half = steps // 2
    if relative:
        same, other = (ref[...].astype(F32) for ref in part_refs)
        text = jnp.where(stream_is_visual(), other, same)
        visual = jnp.where(stream_is_visual(), same, other)
    else:
        text, visual = (
            functools.reduce(
                jnp.add, (part_refs[0][k].astype(F32) for k in range(start, start + half))
            )
            for start in (0, half)
        )
    text_ref[...] = functools.reduce(jnp.add, (ref[...] for ref in share_refs)) + text
    total = functools.reduce(jnp.add, (ref[...] for ref in sum_refs))
    mean, scale, gain, number = (stats_ref[i : i + 1, :] for i in range(4))
    start = pl.multiple_of(head_rank * share, share)
    keep = (iota((share, 1), 0) + start < count_ref[0]).astype(F32)
    hat = (visual_ref[pl.ds(start, share), :].astype(F32) - mean) * keep * scale
    dnormed = visual * keep
    shift_gradient, gain_gradient = total[0:1], total[1:2]
    shift_ref[...] = shift_gradient.reshape(shift_ref.shape)
    gain_ref[...] = gain_gradient.reshape(gain_ref.shape)
    grad_ref[...] = (
        keep
        * scale
        * gain
        * (dnormed - shift_gradient / number - hat * gain_gradient / number)
    )


def swap(value, axis, mask):
    size = lax.axis_size(axis)
    return lax.ppermute(value, axis, [(i, i ^ mask) for i in range(size)])


def after(value, *earlier):
    return lax.optimization_barrier((value, *earlier))[0]


def gather_heads(chunks):
    first = [chunks[0]] + [swap(chunks[0], "head", k) for k in (1, 2, 3)]
    second = after(chunks[1], first[2])
    return [first, [chunks[1]] + [swap(second, "head", k) for k in (1, 2, 3)]]


def across_chips(mine, other, plans, sizes, name):
    axes = {X_FIRST: (2, 4), Y_FIRST: (4, 2)}
    width = mine.shape[2]
    outs = []
    for size in sizes:
        outs += [((2, size, width), F32), ((2, size, width), BF16)]
    joined = call(functools.partial(join_cores_kernel, plans), name, 1, outs, [mine, other])
    return [
        (keep, swap(send, "dp", axes[plan][0]), axes[plan][1])
        for plan, keep, send in zip(plans, joined[::2], joined[1::2])
    ]


def second_exchange(stages, name, earlier=()):
    outs = []
    args = []
    for keep, other, mask in stages:
        outs += [(keep.shape[1:], F32), (keep.shape[1:], BF16)]
        args += [keep, other]
    args[1] = after(args[1], *earlier)
    joined = call(join_chips_kernel, name, 1, outs, args)
    blocks = []
    for n, stage in enumerate(stages):
        blocks += [joined[2 * n], swap(joined[2 * n + 1], "dp", stage[2])]
    return blocks, joined


def per_device(
    text_in,
    visual_in,
    visual_count,
    line_index,
    box_index,
    qkv_weight,
    bias_table,
    out_weight,
    out_bias,
    norm1_gain,
    norm1_shift,
    ffn_weight_in,
    ffn_bias_in,
    ffn_weight_out,
    ffn_bias_out,
    norm2_gain,
    norm2_shift,
    batch_gain,
    batch_shift,
    cotangent,
):
    tokens, width = text_in.shape
    local_width = qkv_weight.shape[2]
    heads_local = local_width // HD
    head_count = lax.axis_size("head")
    dp_count = lax.axis_size("dp")
    head_rank = lax.axis_index("head")
    dp_rank = lax.axis_index("dp")
    fused = head_count == 4 and dp_count == 8
    share = tokens // head_count
    block = tokens // CHUNKS
    hidden_width = ffn_weight_in.shape[1]
    table_width = bias_table.shape[1]
    part_in = width // (dp_count * head_count)
    part_out = hidden_width // (dp_count * head_count)
    weight = jnp.transpose(qkv_weight, (1, 0, 2))
    row_vectors = [
        value.reshape(1, width)
        for value in (
            out_bias,
            norm1_gain,
            norm1_shift,
            ffn_bias_out,
            norm2_gain,
            norm2_shift,
            batch_gain,
            batch_shift,
        )
    ]

    packed_shape = ((8, width), F32)
    (packed,) = call(
        stats_kernel, "stats", 2, [packed_shape], [visual_in], visual_count
    )
    if fused:
        (packed,) = call(
            join_stats_kernel, "join_stats", 1, [packed_shape], [packed, swap(packed, "dp", 1)]
        )
        packed = [packed] + [swap(packed, "dp", k) for k in (2, 4, 6)]
    else:
        gathered = lax.all_gather(packed, "dp")
        packed = [gathered[i] for i in range(dp_count)]
    one, back, tab, small, bias_in = call(
        prep_kernel,
        "prep",
        2,
        [
            ((tokens, LEVELS), BF16),
            ((LEVELS, tokens), BF16),
            ((LEVELS, heads_local * LEVELS), BF16),
            ((8, width), F32),
            ((8, width), F32),
        ],
        [line_index, box_index, bias_table, ffn_bias_in.reshape(1, hidden_width)] + row_vectors,
        visual_count,
    )

    rows = ((tokens, local_width), BF16)
    turned = ((local_width, tokens), BF16)
    left = [pltpu.VMEM((block, heads_local * LEVELS), BF16)]
    chunk_outs = [((local_width, block), BF16), ((heads_local, tokens, block), BF16)]
    stats, x, q, k, v, kt, vt, heads_one, prob_one = call(
        functools.partial(attend_first_kernel, len(packed)),
        "attend_first",
        6,
        [packed_shape, ((tokens, width), BF16), rows, rows, rows, turned, turned] + chunk_outs,
        [text_in, visual_in, small, weight, tab, one] + packed,
        visual_count,
        scratch=left,
        final=(1,),
    )
    heads_two, prob_two = call(
        functools.partial(attend_chunk, 1),
        "attend_second",
        3,
        chunk_outs,
        [q, k, vt, tab, one],
        visual_count,
        scratch=left,
    )
    heads = (heads_one, heads_two)
    if fused:
        pieces = gather_heads(heads)
    else:
        pieces = []
        for piece in heads:
            gathered = lax.all_gather(piece, "head")
            pieces.append([gathered[i] for i in range(head_count)])

    results = []
    for c in range(CHUNKS):
        text = after(text_in, results[-1][-1]) if results else text_in
        results.append(
            call(
                functools.partial(ffn_kernel, c, fused, len(pieces[c])),
                f"ffn_{c}",
                9,
                [
                    ((block, width), BF16),
                    ((share, width), F32),
                    ((block, hidden_width), BF16),
                    ((block, hidden_width), BF16),
                    ((block, width), BF16),
                    ((block, width), BF16),
                    ((block, width), BF16),
                    ((block, local_width), BF16),
                    ((local_width, block), BF16),
                    ((VEC_ROWS, width), F32),
                ],
                [text, cotangent, out_weight, ffn_weight_in, ffn_weight_out, small, bias_in]
                + list(pieces[c]),
                scratch=[pltpu.VMEM((block, hidden_width), F32)],
            )
        )
    out, dh_share, act, dpre, low, branch, mix, dheads, dheads_t, vec = zip(*results)
    if fused:
        in_rows = hidden_width // width * part_in + VEC_ROWS
        out_rows = part_out + width // dp_count // 2
        mine, sib = call(
            weight_grad_in_kernel,
            "weight_grad_in",
            2,
            [((4, in_rows, width), F32), ((4, in_rows, width), BF16)],
            [*low, *dpre, *vec],
        )
        other = swap(sib, "dp", 1)
        layer_out, mine_out, sib_out = call(
            weight_grad_out_kernel,
            "weight_grad_out",
            3,
            [
                ((tokens, width), BF16),
                ((4, out_rows, width), F32),
                ((4, out_rows, width), BF16),
            ],
            [after(out[0], sib), *out[1:], *act, *branch, *mix, *heads],
            scratch=[pltpu.VMEM((width, local_width), F32)],
            final=(0,),
        )
        other_out = swap(sib_out, "dp", 1)
        ffn_stages = across_chips(mine, other, [X_FIRST], [in_rows], "join_cores_in")
        ffn_stages += across_chips(mine_out, other_out, [Y_FIRST], [out_rows], "join_cores_out")
    inner = [q, k, v, kt, one, back, *heads, *dheads, *dheads_t, prob_one, prob_two]
    if fused:
        inner[0] = after(q, *(stage[0] for stage in ffn_stages))
        part_outs = [((2, share, width), F32), ((2, share, width), BF16)]
    else:
        part_outs = [((head_count, share, width), BF16)]
    dqkv, pairs, sums, *parts = call(
        functools.partial(back_kernel, fused),
        "back",
        10,
        [
            ((3, tokens, local_width), BF16),
            ((heads_local, LEVELS, LEVELS), F32),
            packed_shape,
        ]
        + part_outs,
        [weight, visual_in, stats] + inner,
        visual_count,
    )
    if fused:
        keep, send = parts
        near = swap(send, "head", 1)
        sums = sums + swap(sums, "dp", 1)
        ffn_blocks, ffn_joined = second_exchange(ffn_stages, "join_chips_ffn", [sums])
        sums = sums + swap(sums, "dp", 2)
        block_rows = 3 * (width // dp_count) + 16
        mine, sib = call(
            functools.partial(qkv_grad_kernel, True),
            "qkv_grad",
            3,
            [
                ((4, block_rows // 2, 2 * local_width), F32),
                ((4, block_rows // 2, 2 * local_width), BF16),
            ],
            [after(x, ffn_joined[0]), dqkv, pairs],
            scratch=[pltpu.VMEM((3, width, local_width), F32)],
        )
        first_rows = block_rows // 4 // 8 * 8
        stages = across_chips(
            mine,
            after(swap(sib, "dp", 1), sums),
            [X_FIRST, Y_FIRST],
            [first_rows, block_rows // 2 - first_rows],
            "join_cores_qkv",
        )
        sums = sums + swap(sums, "dp", 4)
        qkv_blocks, unused_joined = second_exchange(stages, "join_chips_qkv", ffn_blocks)
        same, send = call(
            join_pair_kernel,
            "join_pair",
            1,
            [((share, width), F32), ((share, width), BF16)],
            [keep, after(near, sums)],
        )
        received = [same, swap(send, "head", 2)]
        sums = sums + swap(sums, "head", 1)
        sums = [sums, swap(sums, "head", 2)]
        blocks = ffn_blocks + qkv_blocks
        one_row = ((1, part_in), F32)
        grad_in, grad_out, grad_ow, grad_bias_in, grad_qkv, grad_table, *own = call(
            functools.partial(finish_grads_kernel, hidden_width),
            "finish_grads",
            2,
            [
                ((part_in, hidden_width), F32),
                ((part_out, width), F32),
                ((width // dp_count, local_width), F32),
                ((1, part_out), F32),
                ((3, width // dp_count, local_width), F32),
                ((heads_local, table_width // dp_count), F32),
            ]
            + [one_row] * 6,
            blocks,
            final=range(12),
        )
        grad_bias_in = grad_bias_in.reshape(part_out)
        grad_qkv = jnp.transpose(grad_qkv, (1, 0, 2))
        grad_ow = jnp.transpose(grad_ow)
        own = [value.reshape(part_in) for value in own]
    else:
        layer_out = jnp.concatenate(out, axis=0)
        act, dpre, low, branch, mix = (
            jnp.concatenate(value, axis=0) for value in (act, dpre, low, branch, mix)
        )

        def scatter(value, dimension):
            return lax.psum_scatter(
                value.astype(BF16), "dp", scatter_dimension=dimension, tiled=True
            ).astype(F32)

        def own_columns(value, part):
            split = value.reshape(tokens, dp_count, head_count, part)
            return lax.dynamic_index_in_dim(split, head_rank, 2, keepdims=False).reshape(
                tokens, dp_count * part
            )

        grad_in = scatter(dot(own_columns(low, part_in), dpre, TN), 0)
        grad_out = scatter(dot(own_columns(act, part_out), branch, TN), 0)
        grad_ow = scatter(dot(jnp.concatenate(heads, axis=1), mix), 1)
        vec = lax.psum((vec[0] + vec[1]).astype(BF16), "dp").astype(F32)
        place = dp_rank * head_count + head_rank
        own = [
            lax.dynamic_slice_in_dim(vec[row], place * part_in, part_in, 0)
            for row in (0, 1, 2, 7, 8, 9)
        ]
        grad_bias_in = lax.dynamic_slice_in_dim(
            vec[3 : 3 + hidden_width // width].reshape(hidden_width), place * part_out, part_out, 0
        )
        sums = [lax.psum(sums, ("dp", "head"))]
        grad, table = call(
            functools.partial(qkv_grad_kernel, False),
            "qkv_grad",
            3,
            [((3, width, local_width), BF16), ((8, table_width), F32)],
            [x, dqkv, pairs],
        )
        received = [lax.all_to_all(parts[0], "head", 0, 0, tiled=True)]
        grad_qkv = jnp.transpose(scatter(grad, 1), (1, 0, 2))
        grad_table = scatter(table[:heads_local], 1)

    grad_text, grad_visual, gain_gradient, shift_gradient = call(
        functools.partial(finish_inputs_kernel, head_count, fused, len(sums)),
        "finish_inputs",
        2,
        [((share, width), F32)] * 2 + [((width,), F32)] * 2,
        [visual_in, stats, *dh_share, *received, *sums],
        visual_count,
        final=range(4),
    )
    return (
        layer_out,
        grad_text,
        grad_visual,
        grad_qkv,
        grad_table,
        grad_ow,
        own[0],
        own[1],
        own[2],
        grad_in,
        grad_bias_in,
        grad_out,
        own[3],
        own[4],
        own[5],
        gain_gradient,
        shift_gradient,
    )


def solution(mesh):
    in_specs = (
        P("dp", None),
        P("dp", None),
        P("dp"),
        P(None, "dp"),
        P(None, None, "dp"),
        P(None, None, "head"),
        P("head", None),
        P(),
        P(),
        P(),
        P(),
        P(),
        P(),
        P(),
        P(),
        P(),
        P(),
        P(),
        P(),
        P("dp", None),
    )
    out_specs = (
        P("dp", None),
        P(("dp", "head"), None),
        P(("dp", "head"), None),
        P("dp", None, "head"),
        P("head", "dp"),
        P("head", "dp"),
        P(("dp", "head")),
        P(("dp", "head")),
        P(("dp", "head")),
        P(("dp", "head"), None),
        P(("dp", "head")),
        P(("dp", "head"), None),
        P(("dp", "head")),
        P(("dp", "head")),
        P(("dp", "head")),
        P(),
        P(),
    )
    return jax.shard_map(
        per_device, mesh=mesh, in_specs=in_specs, out_specs=out_specs, check_vma=False
    )
```

```python
import functools

import jax
import jax.numpy as jnp
from jax import lax
from jax.experimental import pallas as pl
from jax.experimental.pallas import tpu as pltpu
from jax.sharding import PartitionSpec as P

HD = 64
NB_REL = 32
NB_BOX = 16
LINES = 48
BOXES = 32

EPSILON = 1e-05
FLOOR_SCORE = -1000000000.0
SCALE = HD ** (-0.5)
LEVELS = 128
MASK_LANE = LINES + 2 * BOXES
VMEM_LIMIT = 12 * 1024 * 1024
VEC_ROWS = 16
CHUNKS = 2

F32 = jnp.float32
BF16 = jnp.bfloat16

NN = (((1,), (0,)), ((), ()))
NT = (((1,), (1,)), ((), ()))
TN = (((0,), (0,)), ((), ()))
TT = (((0,), (1,)), ((), ()))


def dot(left, right, dims=NN):
    return lax.dot_general(left, right, dims, preferred_element_type=F32)


def iota(shape, axis):
    return lax.broadcasted_iota(jnp.int32, shape, axis)


def one_hot(condition):
    return condition.astype(F32).astype(BF16)


def thirds(value):
    high = value.astype(BF16)
    rest = value - high.astype(F32)
    middle = rest.astype(BF16)
    return high, middle, (rest - middle.astype(F32)).astype(BF16)


def picked(value, selector, dims=NN):
    return functools.reduce(jnp.add, (dot(part, selector, dims) for part in thirds(value)))


def call(kernel, name, micros, outs, args, count=None, scratch=(), final=()):
    vmem = pl.BlockSpec(memory_space=pltpu.VMEM)
    scalars = [] if count is None else [count]
    return pl.pallas_call(
        kernel,
        out_shape=tuple(
            jax.ShapeDtypeStruct(*entry) if place in final else pltpu.VMEM(*entry)
            for place, entry in enumerate(outs)
        ),
        in_specs=[pl.BlockSpec(memory_space=pltpu.SMEM)] * len(scalars) + [vmem] * len(args),
        out_specs=tuple(vmem for entry in outs),
        scratch_shapes=list(scratch),
        compiler_params=pltpu.CompilerParams(vmem_limit_bytes=VMEM_LIMIT),
        cost_estimate=pl.CostEstimate(
            flops=int(micros * 1e9), bytes_accessed=int(micros * 3e6), transcendentals=0
        ),
        name=name,
    )(*scalars, *[pltpu.with_memory_space_constraint(a, pltpu.VMEM) for a in args])


def head_groups(heads_local, body, loop=True):
    if heads_local % 2 or not loop:
        for first in range(0, heads_local, 2):
            body(first, min(2, heads_local - first))
        return

    def step(pair, carry):
        body(pair * 2, 2)
        return carry

    lax.fori_loop(0, heads_local // 2, step, 0)


def lanes(first, heads, offset=0):
    start = offset + first * HD
    if isinstance(first, int):
        return slice(start, start + heads * HD)
    return pl.ds(pl.multiple_of(start, 128), heads * HD)


def stream_is_visual():
    return lax.axis_index("head") >= lax.axis_size("head") // 2


def stats_kernel(count_ref, visual_ref, out_ref):
    tokens, width = visual_ref.shape
    number = count_ref[0].astype(F32)
    keep = (iota((tokens, 1), 0) < count_ref[0]).astype(F32)
    visual = visual_ref[...].astype(F32)
    total = jnp.sum(visual * keep, axis=0, keepdims=True)
    centred = (visual - total / number) * keep
    spread = jnp.sum(centred * centred, axis=0, keepdims=True)
    out_ref[...] = jnp.concatenate(
        [total, spread, jnp.full((1, width), number, F32), jnp.zeros((5, width), F32)], axis=0
    )


def joined_stats(blocks):
    total = functools.reduce(jnp.add, (b[0:1] for b in blocks))
    number = functools.reduce(jnp.add, (b[2:3] for b in blocks))
    mean = total / number
    spread = functools.reduce(
        jnp.add, (b[1:2] + b[2:3] * (b[0:1] / b[2:3] - mean) ** 2 for b in blocks)
    )
    return total, spread, number


def join_stats_kernel(*refs):
    total, spread, number = joined_stats([ref[...] for ref in refs[:-1]])
    refs[-1][...] = jnp.concatenate(
        [total, spread, number, jnp.zeros((5, total.shape[1]), F32)], axis=0
    )


GROUPS = (
    (0, LINES, NB_REL // 2, 0),
    (LINES, LINES + BOXES, NB_BOX // 2, NB_REL),
    (LINES + BOXES, LINES + 2 * BOXES, NB_BOX // 2, NB_REL + NB_BOX),
)


def bucket_map(level, half, offset, table_width):
    bucket = jnp.clip(level, -half, half - 1) + half + offset
    return one_hot(bucket == iota((table_width, LEVELS), 0))


def same_group(row, lane):
    inside = jnp.zeros(row.shape, jnp.bool_)
    for start, stop, unused_half, unused_offset in GROUPS:
        inside = inside | ((row >= start) & (row < stop) & (lane >= start) & (lane < stop))
    return inside


def by_level(level, line, across, down):
    wanted = jnp.where(level < LINES, line, jnp.where(level < LINES + BOXES, across, down))
    return wanted == level


def prep_kernel(count_ref, line_ref, box_ref, table_ref, bias_ref, *refs):
    oh_ref, back_ref, tab_ref, small_ref, b1_ref = refs[8:]
    width = small_ref.shape[1]
    small_ref[...] = jnp.concatenate([ref[...] for ref in refs[:8]], axis=0)
    for c in range(bias_ref.shape[1] // width):
        b1_ref[c : c + 1, :] = bias_ref[:, c * width : (c + 1) * width]
    visual = stream_is_visual()
    tokens = line_ref.shape[1]
    heads_local, table_width = table_ref.shape
    line = jnp.where(visual, line_ref[1:2, :], line_ref[0:1, :])
    across = jnp.where(visual, box_ref[1, 0:1, :], box_ref[0, 0:1, :]) + LINES
    down = jnp.where(visual, box_ref[1, 1:2, :], box_ref[0, 1:2, :]) + (LINES + BOXES)
    level = iota((LEVELS, tokens), 0)
    back_ref[...] = one_hot(by_level(LEVELS - 1 - level, line, across, down))
    closed = jnp.logical_and(visual, iota((LEVELS, tokens), 1) >= count_ref[0])
    mask = jnp.where(closed, FLOOR_SCORE, 0.0)
    flags = by_level(level, line, across, down).astype(F32)
    oh_ref[...] = jnp.transpose(jnp.where(level == MASK_LANE, mask, flags)).astype(BF16)
    row = iota((LEVELS, LEVELS), 0)
    lane = iota((LEVELS, LEVELS), 1)
    inside = same_group(row, lane)
    offsets = iota((table_width, LEVELS), 1) - LEVELS // 2
    table = table_ref[...]
    spread = [
        picked(table, bucket_map(offsets, half, offset, table_width))
        for unused_start, unused_stop, half, offset in GROUPS
    ]
    for head in range(heads_local):
        rows = [jnp.broadcast_to(s[head : head + 1, :], (LEVELS, LEVELS)) for s in spread]
        chosen = jnp.where(row < LINES, rows[0], jnp.where(row < LINES + BOXES, rows[1], rows[2]))
        turned = pltpu.roll(chosen, LEVELS // 2, 1, stride=1, stride_axis=0)
        pairs = jnp.where(inside, turned, 0.0)
        high = jnp.where((lane == MASK_LANE) & (row < LINES), 1.0, pairs)
        tab_ref[:, head * LEVELS : (head + 1) * LEVELS] = high.astype(BF16)


def attend_chunk(
    chunk, count_ref, q_ref, k_ref, vt_ref, tab_ref, oh_ref, heads_ref, prob_ref, left_ref
):
    visual = stream_is_visual()
    tokens, local_width = q_ref.shape
    heads_local = local_width // HD
    block = heads_ref.shape[1]
    span = slice(chunk * block, (chunk + 1) * block)
    place = iota((1, block), 1) + chunk * block
    allowed = jnp.logical_or(jnp.logical_not(visual), place < count_ref[0]).astype(F32)
    one = oh_ref[...]
    left_ref[...] = dot(oh_ref[span, :], tab_ref[...]).astype(BF16)
    ones = jnp.ones((16, tokens), F32).astype(BF16)

    def group(first, heads):
        span_lanes = lanes(first, heads)
        queries = q_ref[span, span_lanes] * jnp.asarray(SCALE, BF16)
        keys = k_ref[:, span_lanes]
        values = vt_ref[span_lanes, :]
        biases = left_ref[:, lanes(2 * first, 2 * heads)]

        def scores(n):
            own = slice(n * HD, (n + 1) * HD)
            right = jnp.concatenate(
                [biases[:, n * LEVELS : (n + 1) * LEVELS], queries[:, own]], axis=1
            )
            return dot(jnp.concatenate([one, keys[:, own]], axis=1), right, NT)

        results = []
        following = scores(0)
        for n in range(heads):
            own = slice(n * HD, (n + 1) * HD)
            current = following
            if n + 1 < heads:
                following = scores(n + 1)
            shifted = jnp.exp(current - jnp.max(current, axis=0, keepdims=True))
            mixed = dot(jnp.concatenate([values[own], ones], axis=0), shifted.astype(BF16))
            share = 1.0 / mixed[HD : HD + 1]
            prob_ref[first + n] = (shifted * share).astype(BF16)
            results.append((mixed[:HD] * (share * allowed)).astype(BF16))
        heads_ref[span_lanes, :] = jnp.concatenate(results, axis=0)

    head_groups(heads_local, group, loop=chunk > 0)


def attend_first_kernel(pieces, count_ref, text_ref, visual_ref, small_ref, w_ref, tab_ref, oh_ref, *refs):
    piece_refs, refs = refs[:pieces], refs[pieces:]
    stats_ref, x_ref, q_ref, k_ref, v_ref, kt_ref, vt_ref, heads_ref, prob_ref, left_ref = refs
    visual = stream_is_visual()
    tokens, width = text_ref.shape
    total, spread, number = joined_stats([ref[...] for ref in piece_refs])
    mean = total / number
    scale = lax.rsqrt(spread / number + EPSILON)
    gain, shift = small_ref[6:7, :], small_ref[7:8, :]
    stats_ref[...] = jnp.concatenate(
        [mean, scale, gain, number, jnp.zeros((4, width), F32)], axis=0
    )

    @pl.when(visual)
    def _():
        keep = (iota((tokens, 1), 0) < count_ref[0]).astype(F32)
        centred = (visual_ref[...].astype(F32) - mean) * keep
        x_ref[...] = ((centred * scale * gain + shift) * keep).astype(BF16)

    @pl.when(jnp.logical_not(visual))
    def _():
        x_ref[...] = text_ref[...]

    x = x_ref[...]
    q_ref[...] = dot(x, w_ref[0]).astype(BF16)
    k_ref[...] = dot(x, w_ref[1]).astype(BF16)
    v_ref[...] = dot(x, w_ref[2]).astype(BF16)
    kt_ref[...] = dot(w_ref[1], x, TT).astype(BF16)
    vt_ref[...] = dot(w_ref[2], x, TT).astype(BF16)
    attend_chunk(
        0, count_ref, q_ref, k_ref, vt_ref, tab_ref, oh_ref, heads_ref, prob_ref, left_ref
    )


ERF_P = 0.3275911 * 0.7071067811865476
ERF_A = (0.254829592, -0.284496736, 1.421413741, -1.453152027, 1.061405429)


def gelu_parts(pre):
    t = 1.0 / (1.0 + ERF_P * jnp.abs(pre))
    bell = jnp.exp(-0.5 * pre * pre)
    poly = 0.5 * ERF_A[4]
    for coefficient in ERF_A[3::-1]:
        poly = poly * t + 0.5 * coefficient
    tail = poly * t * bell
    cdf = jnp.where(pre >= 0.0, 1.0 - tail, tail)
    return pre * cdf, cdf + pre * (bell * 0.3989422804014327)


def normed_rows(hidden):
    average = jnp.mean(hidden, axis=-1, keepdims=True)
    centred = hidden - average
    scale = lax.rsqrt(jnp.mean(centred * centred, axis=-1, keepdims=True) + EPSILON)
    return centred * scale, scale


def normed_back(upstream, hat, scale, gain):
    scaled = upstream * gain
    return scale * (
        scaled
        - jnp.mean(scaled, axis=-1, keepdims=True)
        - hat * jnp.mean(scaled * hat, axis=-1, keepdims=True)
    )


def ffn_kernel(chunk, relative, pieces, *refs):
    (text_ref, cot_ref, wo, w1, w2, small_ref, b1_ref), refs = refs[:7], refs[7:]
    piece_refs, refs = refs[:pieces], refs[pieces:]
    out_ref, share_ref, act_ref, dpre_ref, low_ref, branch_ref, mix_ref = refs[:7]
    dheads_ref, dheadst_ref, vec_ref, slope = refs[7:]
    local_width, block = piece_refs[0].shape
    width = text_ref.shape[1]
    hidden_width = w1.shape[1]
    head_rank = lax.axis_index("head")
    out_bias, gain1, shift1, b2, gain2, shift2 = (small_ref[i : i + 1, :] for i in range(6))
    parts = hidden_width // width
    share = share_ref.shape[0]
    rows = slice(chunk * block, (chunk + 1) * block)
    own_rows = pl.ds(pl.multiple_of(head_rank * local_width, 64), local_width)

    sources = [
        (ref[...], head_rank ^ index if relative else index)
        for index, ref in enumerate(piece_refs)
    ]
    mixed = text_ref[rows, :].astype(F32) + out_bias
    for piece, source in sources:
        wo_rows = pl.ds(pl.multiple_of(source * local_width, 64), local_width)
        mixed = mixed + dot(piece, wo[wo_rows, :], TN)
    hat1, scale1 = normed_rows(mixed)
    after = hat1 * gain1 + shift1
    after_low = after.astype(BF16)
    low_ref[...] = after_low
    branch = jnp.zeros((block, width), F32)
    for c in range(parts):
        cols = slice(c * width, (c + 1) * width)
        act, slope[:, cols] = gelu_parts(dot(after_low, w1[:, cols]) + b1_ref[c : c + 1, :])
        act = act.astype(BF16)
        act_ref[:, cols] = act
        branch = branch + dot(act, w2[cols, :])
    hat2, scale2 = normed_rows(after + (branch + b2))
    out_ref[...] = (hat2 * gain2 + shift2).astype(BF16)
    upstream = cot_ref[rows, :].astype(F32)
    dh_two = normed_back(upstream, hat2, scale2, gain2)
    dbranch = dh_two.astype(BF16)
    branch_ref[...] = dbranch
    vec = [None] * 3
    dy = dh_two
    for c in range(parts):
        cols = slice(c * width, (c + 1) * width)
        dpre = (dot(dbranch, w2[cols, :], NT) * slope[:, cols]).astype(BF16)
        dpre_ref[:, cols] = dpre
        vec.append(dpre.astype(F32))
        dy = dy + dot(dpre, w1[:, cols], NT)
    dh_one = normed_back(dy, hat1, scale1, gain1)
    vec[:3] = [dh_one, dy * hat1, dy]
    vec += [dbranch.astype(F32), upstream * hat2, upstream]
    sums = [jnp.sum(v, axis=0, keepdims=True) for v in vec]
    vec_ref[...] = jnp.concatenate(
        sums + [jnp.zeros((VEC_ROWS - len(sums), width), F32)], axis=0
    )
    share_ref[...] = jnp.zeros_like(share_ref)
    per_block = block // share
    for part in range(per_block):

        @pl.when(head_rank == chunk * per_block + part)
        def _():
            share_ref[...] = dh_one[part * share : (part + 1) * share]

    dmix = dh_one.astype(BF16)
    mix_ref[...] = dmix
    dheads_ref[...] = dot(dmix, wo[own_rows, :], NT).astype(BF16)
    dheadst_ref[...] = dot(wo[own_rows, :], dmix, NT).astype(BF16)


def owner_of(half, step):
    place = lax.axis_index("dp")
    core = place & 1
    return (((place >> 1) ^ step) << 1) | (core if half == 0 else 1 - core)


def own_order():
    return [owner_of(half, step) for half in range(2) for step in range(4)]


def weight_grad_in_kernel(*refs):
    head_rank = lax.axis_index("head")
    low_refs, dpre_refs, vec_refs = (refs[i * CHUNKS : (i + 1) * CHUNKS] for i in range(3))
    mine_ref, sib_ref = refs[3 * CHUNKS :]
    width = low_refs[0].shape[1]
    parts = dpre_refs[0].shape[1] // width
    width_own = width // 8
    part_in = width_own // 4
    lane = iota((part_in, width), 1)
    row = iota((part_in, width), 0)
    pick = jnp.concatenate(
        [
            (lane == owner * width_own + head_rank * part_in + row).astype(F32)
            for owner in own_order()
        ],
        axis=0,
    ).astype(BF16)
    low_t = [dot(pick, low[...], NT).astype(BF16) for low in low_refs]
    grads = []
    for p in range(parts):
        cols = slice(p * width, (p + 1) * width)
        grads.append(
            functools.reduce(
                jnp.add, (dot(low_t[c], dpre_refs[c][:, cols]) for c in range(CHUNKS))
            )
        )
    vec = functools.reduce(jnp.add, (v[...] for v in vec_refs))
    for n in range(8):
        rows = slice(n * part_in, (n + 1) * part_in)
        block = jnp.concatenate([grad[rows] for grad in grads] + [vec], axis=0)
        target = mine_ref if n < 4 else sib_ref
        target[n % 4] = block.astype(target.dtype)


def weight_grad_out_kernel(*refs):
    head_rank = lax.axis_index("head")
    names = ("out", "act", "branch", "mix", "heads")
    groups = {name: refs[i * CHUNKS : (i + 1) * CHUNKS] for i, name in enumerate(names)}
    layer_ref, mine_ref, sib_ref, whole = refs[len(names) * CHUNKS :]
    block, width = groups["out"][0].shape
    hidden_width = groups["act"][0].shape[1]
    owners = own_order()
    width_own = width // 8
    window = hidden_width // 8
    part_out = window // 4
    half_own = width_own // 2
    for c in range(CHUNKS):
        layer_ref[c * block : (c + 1) * block, :] = groups["out"][c][...]
    whole[...] = functools.reduce(
        jnp.add, (dot(groups["mix"][c][...], groups["heads"][c][...], TT) for c in range(CHUNKS))
    )
    pick = one_hot(
        iota((part_out, window), 1) == head_rank * part_out + iota((part_out, window), 0)
    )
    grad = jnp.zeros((8 * part_out, width), F32)
    for c in range(CHUNKS):
        stacked = []
        for owner in owners:
            cols = pl.ds(pl.multiple_of(owner * window, 128), window)
            stacked.append(dot(pick, groups["act"][c][:, cols], NT).astype(BF16))
        grad = grad + dot(jnp.concatenate(stacked, axis=0), groups["branch"][c][...])
    for n, owner in enumerate(owners):
        start = pl.multiple_of(owner * width_own, 8)
        packed = jnp.concatenate(
            [whole[pl.ds(start, half_own), :], whole[pl.ds(start + half_own, half_own), :]],
            axis=1,
        )
        target = mine_ref if n < 4 else sib_ref
        target[n % 4] = jnp.concatenate(
            [grad[n * part_out : (n + 1) * part_out], packed], axis=0
        ).astype(target.dtype)


X_FIRST = ((0, 2), (1, 3))
Y_FIRST = ((0, 1), (2, 3))


def join_cores_kernel(plans, *refs):
    mine_ref, other_ref, outs = refs[0], refs[1], refs[2:]
    start = 0
    for (keep, send), keep_ref, send_ref in zip(plans, outs[::2], outs[1::2]):
        rows = slice(start, start + keep_ref.shape[1])
        start = rows.stop
        for places, out in ((keep, keep_ref), (send, send_ref)):
            for n, place in enumerate(places):
                total = mine_ref[place, rows, :] + other_ref[place, rows, :].astype(F32)
                out[n] = total.astype(out.dtype)


def join_chips_kernel(*refs):
    count = len(refs) // 4
    ins, outs = refs[: 2 * count], refs[2 * count :]
    for n in range(count):
        keep, other = ins[2 * n : 2 * n + 2]
        for m, out in enumerate(outs[2 * n : 2 * n + 2]):
            out[...] = (keep[m] + other[m].astype(F32)).astype(out.dtype)


def attend_back_heads(count_ref, refs, dqkv_ref, pair_ref):
    q_ref, k_ref, v_ref, kt_ref, oh_ref, back_ref = refs[:6]
    groups = [refs[6 + i * CHUNKS : 6 + (i + 1) * CHUNKS] for i in range(4)]
    head_refs, dhead_refs, dheadt_refs, prob_refs = groups
    visual = stream_is_visual()
    tokens = q_ref.shape[0]
    block = tokens // CHUNKS
    count = count_ref[0]
    one = oh_ref[...]
    back = back_ref[...]
    inside = same_group(LEVELS - 1 - iota((LEVELS, LEVELS), 0), iota((LEVELS, LEVELS), 1))
    extra = one_hot(iota((tokens, 16), 1) < 2)
    sublane = iota((16, block), 0)
    free = jnp.logical_not(visual)
    rows_open = []
    lanes_open = []
    for c in range(CHUNKS):
        rows_open.append(
            jnp.logical_or(free, iota((block, 1), 0) + c * block < count).astype(BF16)
        )
        lanes_open.append(
            jnp.logical_or(free, iota((1, block), 1) + c * block < count).astype(BF16)
        )

    def group(first, heads):
        span_lanes = lanes(first, heads)
        turned = [[], [], []]
        for n in range(heads):
            own = slice(n * HD, (n + 1) * HD)
            left = jnp.concatenate([v_ref[:, span_lanes][:, own], extra], axis=1)
            below = jnp.concatenate([back, kt_ref[span_lanes, :][own]], axis=0)
            dquery_t = []
            dkey = jnp.zeros((tokens, HD), F32)
            dvalue = jnp.zeros((tokens, HD), F32)
            pairs = jnp.zeros((LEVELS, LEVELS), F32)
            for c in range(CHUNKS):
                span = slice(c * block, (c + 1) * block)
                dout = dhead_refs[c][:, span_lanes][:, own] * rows_open[c]
                dout_t = dheadt_refs[c][span_lanes, :][own] * lanes_open[c]
                inner = -jnp.sum(
                    dout_t.astype(F32) * head_refs[c][span_lanes, :][own].astype(F32),
                    axis=0,
                    keepdims=True,
                )
                high = inner.astype(BF16).astype(F32)
                tail = jnp.where(sublane == 0, high, jnp.where(sublane == 1, inner - high, 0.0))
                centred = dot(left, jnp.concatenate([dout_t, tail.astype(BF16)], axis=0))
                prob = prob_refs[c][first + n]
                dscore = (prob.astype(F32) * centred).astype(BF16)
                both = dot(below, dscore)
                level = both[:LEVELS]
                level_high = level.astype(BF16)
                level_low = (level - level_high.astype(F32)).astype(BF16)
                one_part = one[span, :]
                pairs = pairs + dot(level_high, one_part) + dot(level_low, one_part)
                dquery_t.append(both[LEVELS:] * SCALE)
                dkey = dkey + dot(dscore, q_ref[span, span_lanes][:, own])
                dvalue = dvalue + dot(prob, dout)
            pair_ref[first + n] = jnp.where(inside, pairs, 0.0)
            turned[0].append(jnp.concatenate(dquery_t, axis=1))
            turned[1].append(dkey * SCALE)
            turned[2].append(dvalue)
        for m in range(3):
            joined = jnp.concatenate(turned[m], axis=0 if m == 0 else 1)
            if m == 0:
                joined = jnp.transpose(joined)
            dqkv_ref[m, :, span_lanes] = joined.astype(BF16)

    head_groups(q_ref.shape[1] // HD, group)


def back_kernel(relative, count_ref, w_ref, visual_ref, stats_ref, x_ref, *refs):
    steps = lax.axis_size("head")
    inner, refs = refs[: 6 + 4 * CHUNKS], refs[6 + 4 * CHUNKS :]
    sums_ref, refs = refs[0], refs[1:]
    part_refs, refs = refs[: 1 + relative], refs[1 + relative :]
    grad_refs, (dqkv_ref, pair_ref), whole = refs[:2], refs[2:4], refs[4:]
    attend_back_heads(count_ref, inner, dqkv_ref, pair_ref)
    visual = stream_is_visual()
    tokens = visual_ref.shape[0]
    share = tokens // steps
    mean, scale = stats_ref[0:1, :], stats_ref[1:2, :]
    shift_sum = jnp.zeros(mean.shape, F32)
    gain_sum = jnp.zeros(mean.shape, F32)
    for k in range(steps):
        if relative:
            start = pl.multiple_of((lax.axis_index("head") ^ k) * share, share)
            target = part_refs[k % 2].at[k // 2]
        else:
            start = k * share
            target = part_refs[0].at[k]
        rows = pl.ds(start, share)
        part = functools.reduce(
            jnp.add, (dot(dqkv_ref[m, rows, :], w_ref[m], NT) for m in range(3))
        )
        target[...] = part.astype(target.dtype)
        keep = jnp.logical_and(visual, iota((share, 1), 0) + start < count_ref[0]).astype(F32)
        kept = part * keep
        shift_sum = shift_sum + jnp.sum(kept, axis=0, keepdims=True)
        hat = (visual_ref[rows, :].astype(F32) - mean) * scale
        gain_sum = gain_sum + jnp.sum(kept * hat, axis=0, keepdims=True)
    sums_ref[...] = jnp.concatenate(
        [shift_sum, gain_sum, jnp.zeros((6, mean.shape[1]), F32)], axis=0
    )
    qkv_grads(relative, x_ref, dqkv_ref, pair_ref, *grad_refs, *whole)


def join_pair_kernel(keep_ref, other_ref, own_ref, send_ref):
    own_ref[...] = keep_ref[0] + other_ref[0].astype(F32)
    send_ref[...] = (keep_ref[1] + other_ref[1].astype(F32)).astype(BF16)


def table_sums(pair_refs):
    table_width = NB_REL + 2 * NB_BOX
    sums = [[], [], []]
    for ref in pair_refs:
        for head in range(ref.shape[0]):
            turned = pltpu.roll(ref[head], LEVELS // 2 + 1, 1, stride=1, stride_axis=0)
            for n, (start, stop, unused_half, unused_offset) in enumerate(GROUPS):
                rows = turned[LEVELS - stop : LEVELS - start]
                sums[n].append(jnp.sum(rows, axis=0, keepdims=True))
    table = jnp.zeros((8, table_width), F32)
    offsets = LEVELS // 2 - iota((table_width, LEVELS), 1)
    for n, (unused_start, unused_stop, half, offset) in enumerate(GROUPS):
        missing = 8 - len(sums[n])
        stacked = jnp.concatenate(sums[n] + [jnp.zeros((missing, LEVELS), F32)], axis=0)
        table = table + picked(stacked, bucket_map(offsets, half, offset, table_width), NT)
    return table


def qkv_grads(fused, x_ref, dqkv_ref, pair_ref, *outs):
    tokens, width = x_ref.shape
    local_width = dqkv_ref.shape[2]
    table = table_sums((pair_ref,))
    x = x_ref[...]

    if not fused:
        grad_ref, table_ref = outs
        table_ref[...] = table
        for m in range(3):
            grad_ref[m] = dot(x, dqkv_ref[m], TN).astype(BF16)
        return
    mine_ref, sib_ref, whole = outs
    width_own = width // 8
    padded = jnp.concatenate(
        [
            jnp.concatenate([table, jnp.zeros((8, local_width - table.shape[1]), F32)], axis=1),
            jnp.zeros((8, local_width), F32),
        ],
        axis=0,
    )
    for m in range(3):
        whole[m] = dot(x, dqkv_ref[m], TN)
    for half, target in ((1, sib_ref), (0, mine_ref)):
        for k in range(4):
            rows = pl.ds(pl.multiple_of(owner_of(half, k) * width_own, 8), width_own)
            tall = jnp.concatenate([whole[m, rows, :] for m in range(3)] + [padded], axis=0)
            middle = tall.shape[0] // 2
            target[k] = jnp.concatenate([tall[:middle], tall[middle:]], axis=1).astype(
                target.dtype
            )


def finish_grads_kernel(hidden_width, *refs):
    block_refs, outs = refs[:8], refs[8:]
    grad_in, grad_out, grad_ow, bias_in, grad_qkv, grad_table = outs[:6]
    sums = [
        own[...] + other[...].astype(F32) for own, other in zip(block_refs[::2], block_refs[1::2])
    ]
    total = jnp.concatenate(sums, axis=0)
    width = total.shape[1]
    part_in = grad_in.shape[0]
    part_out = grad_out.shape[0]
    half_own = grad_ow.shape[0] // 2
    local_width = grad_ow.shape[1]
    parts = hidden_width // width
    place = lax.axis_index("dp") * lax.axis_size("head") + lax.axis_index("head")
    grad_in[...] = jnp.concatenate(
        [total[p * part_in : (p + 1) * part_in] for p in range(parts)], axis=1
    )
    base = parts * part_in
    vec = total[base : base + VEC_ROWS]
    base += VEC_ROWS
    grad_out[...] = total[base : base + part_out]
    base += part_out
    packed = total[base : base + half_own]
    grad_ow[...] = jnp.concatenate([packed[:, :local_width], packed[:, local_width:]], axis=0)
    base += half_own
    lane = iota((width, 128), 0)
    column = iota((width, 128), 1)
    own = picked(vec, one_hot((lane == place * part_in + column) & (column < part_in)))
    for row, out in zip((0, 1, 2, 7, 8, 9), outs[6:]):
        out[...] = own[row : row + 1, :part_in]
    first = place * part_out
    wide = picked(
        vec, one_hot((lane == lax.rem(first, width) + column) & (column < part_out))
    )
    row = iota((VEC_ROWS, 128), 0)
    chosen = jnp.where(row == 3 + lax.div(first, width), wide, 0.0)
    bias_in[...] = jnp.sum(chosen, axis=0, keepdims=True)[:, :part_out]
    grads = jnp.concatenate([total[base:, :local_width], total[base:, local_width:]], axis=0)
    width_own = grad_qkv.shape[1]
    for m in range(3):
        grad_qkv[m] = grads[m * width_own : (m + 1) * width_own]
    table = grads[3 * width_own : 3 * width_own + 8]
    buckets = grad_table.shape[1]
    lane = iota((local_width, 128), 0)
    column = iota((local_width, 128), 1)
    start = lax.axis_index("dp") * buckets
    cut = picked(table, one_hot((lane == start + column) & (column < buckets)))
    grad_table[...] = cut[: grad_table.shape[0], :buckets]


def finish_inputs_kernel(steps, relative, sums, count_ref, visual_ref, stats_ref, *refs):
    share_refs, refs = refs[:CHUNKS], refs[CHUNKS:]
    part_refs, refs = refs[: 1 + relative], refs[1 + relative :]
    sum_refs, refs = refs[:sums], refs[sums:]
    text_ref, grad_ref, gain_ref, shift_ref = refs
    head_rank = lax.axis_index("head")
    share = text_ref.shape[0]
    half = steps // 2
    if relative:
        same, other = (ref[...].astype(F32) for ref in part_refs)
        text = jnp.where(stream_is_visual(), other, same)
        visual = jnp.where(stream_is_visual(), same, other)
    else:
        text, visual = (
            functools.reduce(
                jnp.add, (part_refs[0][k].astype(F32) for k in range(start, start + half))
            )
            for start in (0, half)
        )
    text_ref[...] = functools.reduce(jnp.add, (ref[...] for ref in share_refs)) + text
    total = functools.reduce(jnp.add, (ref[...] for ref in sum_refs))
    mean, scale, gain, number = (stats_ref[i : i + 1, :] for i in range(4))
    start = pl.multiple_of(head_rank * share, share)
    keep = (iota((share, 1), 0) + start < count_ref[0]).astype(F32)
    hat = (visual_ref[pl.ds(start, share), :].astype(F32) - mean) * keep * scale
    dnormed = visual * keep
    shift_gradient, gain_gradient = total[0:1], total[1:2]
    shift_ref[...] = shift_gradient.reshape(shift_ref.shape)
    gain_ref[...] = gain_gradient.reshape(gain_ref.shape)
    grad_ref[...] = (
        keep
        * scale
        * gain
        * (dnormed - shift_gradient / number - hat * gain_gradient / number)
    )


def swap(value, axis, mask):
    size = lax.axis_size(axis)
    return lax.ppermute(value, axis, [(i, i ^ mask) for i in range(size)])


def after(value, *earlier):
    return lax.optimization_barrier((value, *earlier))[0]


def gather_heads(chunks):
    first = [chunks[0]] + [swap(chunks[0], "head", k) for k in (1, 2, 3)]
    second = after(chunks[1], first[2])
    return [first, [chunks[1]] + [swap(second, "head", k) for k in (1, 2, 3)]]


def across_chips(mine, other, plans, sizes, name):
    axes = {X_FIRST: (2, 4), Y_FIRST: (4, 2)}
    width = mine.shape[2]
    outs = []
    for size in sizes:
        outs += [((2, size, width), F32), ((2, size, width), BF16)]
    joined = call(functools.partial(join_cores_kernel, plans), name, 1, outs, [mine, other])
    return [
        (keep, swap(send, "dp", axes[plan][0]), axes[plan][1])
        for plan, keep, send in zip(plans, joined[::2], joined[1::2])
    ]


def second_exchange(stages, name, earlier=()):
    outs = []
    args = []
    for keep, other, mask in stages:
        outs += [(keep.shape[1:], F32), (keep.shape[1:], BF16)]
        args += [keep, other]
    args[1] = after(args[1], *earlier)
    joined = call(join_chips_kernel, name, 1, outs, args)
    blocks = []
    for n, stage in enumerate(stages):
        blocks += [joined[2 * n], swap(joined[2 * n + 1], "dp", stage[2])]
    return blocks, joined


def per_device(
    text_in,
    visual_in,
    visual_count,
    line_index,
    box_index,
    qkv_weight,
    bias_table,
    out_weight,
    out_bias,
    norm1_gain,
    norm1_shift,
    ffn_weight_in,
    ffn_bias_in,
    ffn_weight_out,
    ffn_bias_out,
    norm2_gain,
    norm2_shift,
    batch_gain,
    batch_shift,
    cotangent,
):
    tokens, width = text_in.shape
    local_width = qkv_weight.shape[2]
    heads_local = local_width // HD
    head_count = lax.axis_size("head")
    dp_count = lax.axis_size("dp")
    head_rank = lax.axis_index("head")
    dp_rank = lax.axis_index("dp")
    fused = head_count == 4 and dp_count == 8
    share = tokens // head_count
    block = tokens // CHUNKS
    hidden_width = ffn_weight_in.shape[1]
    table_width = bias_table.shape[1]
    part_in = width // (dp_count * head_count)
    part_out = hidden_width // (dp_count * head_count)
    weight = jnp.transpose(qkv_weight, (1, 0, 2))
    row_vectors = [
        value.reshape(1, width)
        for value in (
            out_bias,
            norm1_gain,
            norm1_shift,
            ffn_bias_out,
            norm2_gain,
            norm2_shift,
            batch_gain,
            batch_shift,
        )
    ]

    packed_shape = ((8, width), F32)
    (packed,) = call(
        stats_kernel, "stats", 2, [packed_shape], [visual_in], visual_count
    )
    if fused:
        (packed,) = call(
            join_stats_kernel, "join_stats", 1, [packed_shape], [packed, swap(packed, "dp", 1)]
        )
        packed = [packed] + [swap(packed, "dp", k) for k in (2, 4, 6)]
    else:
        gathered = lax.all_gather(packed, "dp")
        packed = [gathered[i] for i in range(dp_count)]
    one, back, tab, small, bias_in = call(
        prep_kernel,
        "prep",
        2,
        [
            ((tokens, LEVELS), BF16),
            ((LEVELS, tokens), BF16),
            ((LEVELS, heads_local * LEVELS), BF16),
            ((8, width), F32),
            ((8, width), F32),
        ],
        [line_index, box_index, bias_table, ffn_bias_in.reshape(1, hidden_width)] + row_vectors,
        visual_count,
    )

    rows = ((tokens, local_width), BF16)
    turned = ((local_width, tokens), BF16)
    left = [pltpu.VMEM((block, heads_local * LEVELS), BF16)]
    chunk_outs = [((local_width, block), BF16), ((heads_local, tokens, block), BF16)]
    stats, x, q, k, v, kt, vt, heads_one, prob_one = call(
        functools.partial(attend_first_kernel, len(packed)),
        "attend_first",
        6,
        [packed_shape, ((tokens, width), BF16), rows, rows, rows, turned, turned] + chunk_outs,
        [text_in, visual_in, small, weight, tab, one] + packed,
        visual_count,
        scratch=left,
        final=(1,),
    )
    heads_two, prob_two = call(
        functools.partial(attend_chunk, 1),
        "attend_second",
        3,
        chunk_outs,
        [q, k, vt, tab, one],
        visual_count,
        scratch=left,
    )
    heads = (heads_one, heads_two)
    if fused:
        pieces = gather_heads(heads)
    else:
        pieces = []
        for piece in heads:
            gathered = lax.all_gather(piece, "head")
            pieces.append([gathered[i] for i in range(head_count)])

    results = []
    for c in range(CHUNKS):
        text = after(text_in, results[-1][-1]) if results else text_in
        results.append(
            call(
                functools.partial(ffn_kernel, c, fused, len(pieces[c])),
                f"ffn_{c}",
                9,
                [
                    ((block, width), BF16),
                    ((share, width), F32),
                    ((block, hidden_width), BF16),
                    ((block, hidden_width), BF16),
                    ((block, width), BF16),
                    ((block, width), BF16),
                    ((block, width), BF16),
                    ((block, local_width), BF16),
                    ((local_width, block), BF16),
                    ((VEC_ROWS, width), F32),
                ],
                [text, cotangent, out_weight, ffn_weight_in, ffn_weight_out, small, bias_in]
                + list(pieces[c]),
                scratch=[pltpu.VMEM((block, hidden_width), F32)],
            )
        )
    out, dh_share, act, dpre, low, branch, mix, dheads, dheads_t, vec = zip(*results)
    if fused:
        in_rows = hidden_width // width * part_in + VEC_ROWS
        out_rows = part_out + width // dp_count // 2
        mine, sib = call(
            weight_grad_in_kernel,
            "weight_grad_in",
            2,
            [((4, in_rows, width), F32), ((4, in_rows, width), BF16)],
            [*low, *dpre, *vec],
        )
        other = swap(sib, "dp", 1)
        layer_out, mine_out, sib_out = call(
            weight_grad_out_kernel,
            "weight_grad_out",
            3,
            [
                ((tokens, width), BF16),
                ((4, out_rows, width), F32),
                ((4, out_rows, width), BF16),
            ],
            [after(out[0], sib), *out[1:], *act, *branch, *mix, *heads],
            scratch=[pltpu.VMEM((width, local_width), F32)],
            final=(0,),
        )
        other_out = swap(sib_out, "dp", 1)
        ffn_stages = across_chips(mine, other, [X_FIRST], [in_rows], "join_cores_in")
        ffn_stages += across_chips(mine_out, other_out, [Y_FIRST], [out_rows], "join_cores_out")
    inner = [q, k, v, kt, one, back, *heads, *dheads, *dheads_t, prob_one, prob_two]
    packed_qkv = 3 * (width // dp_count) // 2 + 8
    scratch = [
        pltpu.VMEM((3, tokens, local_width), BF16),
        pltpu.VMEM((heads_local, LEVELS, LEVELS), F32),
    ]
    if fused:
        inner[0] = after(q, *(stage[0] for stage in ffn_stages))
        part_outs = [((2, share, width), F32), ((2, share, width), BF16)]
        grad_outs = [((4, packed_qkv, width), F32), ((4, packed_qkv, width), BF16)]
        scratch.append(pltpu.VMEM((3, width, local_width), F32))
    else:
        part_outs = [((head_count, share, width), BF16)]
        grad_outs = [((3, width, local_width), BF16), ((8, table_width), F32)]
    sums, *rest = call(
        functools.partial(back_kernel, fused),
        "back",
        12,
        [packed_shape] + part_outs + grad_outs,
        [weight, visual_in, stats, x] + inner,
        visual_count,
        scratch=scratch,
    )
    parts, grads = rest[: len(part_outs)], rest[len(part_outs) :]
    if fused:
        mine, sib = grads
        keep, send = parts
        arrived = [stage[1] for stage in ffn_stages]
        send, sib, sums, *arrived = lax.optimization_barrier((send, sib, sums, *arrived))
        ffn_stages = [(stage[0], other, stage[2]) for stage, other in zip(ffn_stages, arrived)]
        near = swap(send, "head", 1)
        sums = sums + swap(sums, "dp", 1)
        ffn_blocks, ffn_joined = second_exchange(ffn_stages, "join_chips_ffn", [sums])
        sums = sums + swap(sums, "dp", 2)
        first_rows = packed_qkv // 2 // 8 * 8
        stages = across_chips(
            mine,
            after(swap(sib, "dp", 1), ffn_joined[0]),
            [X_FIRST, Y_FIRST],
            [first_rows, packed_qkv - first_rows],
            "join_cores_qkv",
        )
        sums = sums + swap(sums, "dp", 4)
        qkv_blocks, unused_joined = second_exchange(stages, "join_chips_qkv", ffn_blocks[::2])
        same, send = call(
            join_pair_kernel,
            "join_pair",
            1,
            [((share, width), F32), ((share, width), BF16)],
            [keep, near],
        )
        received = [same, swap(send, "head", 2)]
        sums = after(sums, same)
        sums = sums + swap(sums, "head", 1)
        sums = after(sums, *ffn_blocks)
        sums = [sums, swap(sums, "head", 2)]
        blocks = ffn_blocks + qkv_blocks
        one_row = ((1, part_in), F32)
        grad_in, grad_out, grad_ow, grad_bias_in, grad_qkv, grad_table, *own = call(
            functools.partial(finish_grads_kernel, hidden_width),
            "finish_grads",
            2,
            [
                ((part_in, hidden_width), F32),
                ((part_out, width), F32),
                ((width // dp_count, local_width), F32),
                ((1, part_out), F32),
                ((3, width // dp_count, local_width), F32),
                ((heads_local, table_width // dp_count), F32),
            ]
            + [one_row] * 6,
            blocks,
            final=range(12),
        )
        grad_bias_in = grad_bias_in.reshape(part_out)
        grad_qkv = jnp.transpose(grad_qkv, (1, 0, 2))
        grad_ow = jnp.transpose(grad_ow)
        own = [value.reshape(part_in) for value in own]
    else:
        layer_out = jnp.concatenate(out, axis=0)
        act, dpre, low, branch, mix = (
            jnp.concatenate(value, axis=0) for value in (act, dpre, low, branch, mix)
        )

        def scatter(value, dimension):
            return lax.psum_scatter(
                value.astype(BF16), "dp", scatter_dimension=dimension, tiled=True
            ).astype(F32)

        def own_columns(value, part):
            split = value.reshape(tokens, dp_count, head_count, part)
            return lax.dynamic_index_in_dim(split, head_rank, 2, keepdims=False).reshape(
                tokens, dp_count * part
            )

        grad_in = scatter(dot(own_columns(low, part_in), dpre, TN), 0)
        grad_out = scatter(dot(own_columns(act, part_out), branch, TN), 0)
        grad_ow = scatter(dot(jnp.concatenate(heads, axis=1), mix), 1)
        vec = lax.psum((vec[0] + vec[1]).astype(BF16), "dp").astype(F32)
        place = dp_rank * head_count + head_rank
        own = [
            lax.dynamic_slice_in_dim(vec[row], place * part_in, part_in, 0)
            for row in (0, 1, 2, 7, 8, 9)
        ]
        grad_bias_in = lax.dynamic_slice_in_dim(
            vec[3 : 3 + hidden_width // width].reshape(hidden_width), place * part_out, part_out, 0
        )
        sums = [lax.psum(sums, ("dp", "head"))]
        grad, table = grads
        received = [lax.all_to_all(parts[0], "head", 0, 0, tiled=True)]
        grad_qkv = jnp.transpose(scatter(grad, 1), (1, 0, 2))
        grad_table = scatter(table[:heads_local], 1)

    grad_text, grad_visual, gain_gradient, shift_gradient = call(
        functools.partial(finish_inputs_kernel, head_count, fused, len(sums)),
        "finish_inputs",
        2,
        [((share, width), F32)] * 2 + [((width,), F32)] * 2,
        [visual_in, stats, *dh_share, *received, *sums],
        visual_count,
        final=range(4),
    )
    return (
        layer_out,
        grad_text,
        grad_visual,
        grad_qkv,
        grad_table,
        grad_ow,
        own[0],
        own[1],
        own[2],
        grad_in,
        grad_bias_in,
        grad_out,
        own[3],
        own[4],
        own[5],
        gain_gradient,
        shift_gradient,
    )


def solution(mesh):
    in_specs = (
        P("dp", None),
        P("dp", None),
        P("dp"),
        P(None, "dp"),
        P(None, None, "dp"),
        P(None, None, "head"),
        P("head", None),
        P(),
        P(),
        P(),
        P(),
        P(),
        P(),
        P(),
        P(),
        P(),
        P(),
        P(),
        P(),
        P("dp", None),
    )
    out_specs = (
        P("dp", None),
        P(("dp", "head"), None),
        P(("dp", "head"), None),
        P("dp", None, "head"),
        P("head", "dp"),
        P("head", "dp"),
        P(("dp", "head")),
        P(("dp", "head")),
        P(("dp", "head")),
        P(("dp", "head"), None),
        P(("dp", "head")),
        P(("dp", "head"), None),
        P(("dp", "head")),
        P(("dp", "head")),
        P(("dp", "head")),
        P(),
        P(),
    )
    return jax.shard_map(
        per_device, mesh=mesh, in_specs=in_specs, out_specs=out_specs, check_vma=False
    )
```

```python
import functools

import jax
import jax.numpy as jnp
from jax import lax
from jax.experimental import pallas as pl
from jax.experimental.pallas import tpu as pltpu
from jax.sharding import PartitionSpec as P

HD = 64
NB_REL = 32
NB_BOX = 16
LINES = 48
BOXES = 32

EPSILON = 1e-05
FLOOR_SCORE = -1000000000.0
SCALE = HD ** (-0.5)
LEVELS = 128
MASK_LANE = LINES + 2 * BOXES
VMEM_LIMIT = 12 * 1024 * 1024
VEC_ROWS = 16
CHUNKS = 2

F32 = jnp.float32
BF16 = jnp.bfloat16

NN = (((1,), (0,)), ((), ()))
NT = (((1,), (1,)), ((), ()))
TN = (((0,), (0,)), ((), ()))
TT = (((0,), (1,)), ((), ()))


def dot(left, right, dims=NN):
    return lax.dot_general(left, right, dims, preferred_element_type=F32)


def iota(shape, axis):
    return lax.broadcasted_iota(jnp.int32, shape, axis)


def one_hot(condition):
    return condition.astype(F32).astype(BF16)


def thirds(value):
    high = value.astype(BF16)
    rest = value - high.astype(F32)
    middle = rest.astype(BF16)
    return high, middle, (rest - middle.astype(F32)).astype(BF16)


def picked(value, selector, dims=NN):
    return functools.reduce(jnp.add, (dot(part, selector, dims) for part in thirds(value)))


def call(kernel, name, micros, outs, args, count=None, scratch=(), final=()):
    vmem = pl.BlockSpec(memory_space=pltpu.VMEM)
    scalars = [] if count is None else [count]
    return pl.pallas_call(
        kernel,
        out_shape=tuple(
            jax.ShapeDtypeStruct(*entry) if place in final else pltpu.VMEM(*entry)
            for place, entry in enumerate(outs)
        ),
        in_specs=[pl.BlockSpec(memory_space=pltpu.SMEM)] * len(scalars) + [vmem] * len(args),
        out_specs=tuple(vmem for entry in outs),
        scratch_shapes=list(scratch),
        compiler_params=pltpu.CompilerParams(vmem_limit_bytes=VMEM_LIMIT),
        cost_estimate=pl.CostEstimate(
            flops=int(micros * 1e9), bytes_accessed=int(micros * 3e6), transcendentals=0
        ),
        name=name,
    )(*scalars, *[pltpu.with_memory_space_constraint(a, pltpu.VMEM) for a in args])


def head_groups(heads_local, body, loop=True):
    if heads_local % 2 or not loop:
        for first in range(0, heads_local, 2):
            body(first, min(2, heads_local - first))
        return

    def step(pair, carry):
        body(pair * 2, 2)
        return carry

    lax.fori_loop(0, heads_local // 2, step, 0)


def lanes(first, heads, offset=0):
    start = offset + first * HD
    if isinstance(first, int):
        return slice(start, start + heads * HD)
    return pl.ds(pl.multiple_of(start, 128), heads * HD)


def stream_is_visual():
    return lax.axis_index("head") >= lax.axis_size("head") // 2


def stats_kernel(count_ref, visual_ref, out_ref):
    tokens, width = visual_ref.shape
    number = count_ref[0].astype(F32)
    keep = (iota((tokens, 1), 0) < count_ref[0]).astype(F32)
    visual = visual_ref[...].astype(F32)
    total = jnp.sum(visual * keep, axis=0, keepdims=True)
    centred = (visual - total / number) * keep
    spread = jnp.sum(centred * centred, axis=0, keepdims=True)
    out_ref[...] = jnp.concatenate(
        [total, spread, jnp.full((1, width), number, F32), jnp.zeros((5, width), F32)], axis=0
    )


def joined_stats(blocks):
    total = functools.reduce(jnp.add, (b[0:1] for b in blocks))
    number = functools.reduce(jnp.add, (b[2:3] for b in blocks))
    mean = total / number
    spread = functools.reduce(
        jnp.add, (b[1:2] + b[2:3] * (b[0:1] / b[2:3] - mean) ** 2 for b in blocks)
    )
    return total, spread, number


def join_stats_kernel(*refs):
    total, spread, number = joined_stats([ref[...] for ref in refs[:-1]])
    refs[-1][...] = jnp.concatenate(
        [total, spread, number, jnp.zeros((5, total.shape[1]), F32)], axis=0
    )


GROUPS = (
    (0, LINES, NB_REL // 2, 0),
    (LINES, LINES + BOXES, NB_BOX // 2, NB_REL),
    (LINES + BOXES, LINES + 2 * BOXES, NB_BOX // 2, NB_REL + NB_BOX),
)


def bucket_map(level, half, offset, table_width):
    bucket = jnp.clip(level, -half, half - 1) + half + offset
    return one_hot(bucket == iota((table_width, LEVELS), 0))


def same_group(row, lane):
    inside = jnp.zeros(row.shape, jnp.bool_)
    for start, stop, unused_half, unused_offset in GROUPS:
        inside = inside | ((row >= start) & (row < stop) & (lane >= start) & (lane < stop))
    return inside


def by_level(level, line, across, down):
    wanted = jnp.where(level < LINES, line, jnp.where(level < LINES + BOXES, across, down))
    return wanted == level


def prep_kernel(count_ref, line_ref, box_ref, table_ref, bias_ref, *refs):
    oh_ref, back_ref, tab_ref, small_ref, b1_ref = refs[8:]
    width = small_ref.shape[1]
    small_ref[...] = jnp.concatenate([ref[...] for ref in refs[:8]], axis=0)
    for c in range(bias_ref.shape[1] // width):
        b1_ref[c : c + 1, :] = bias_ref[:, c * width : (c + 1) * width]
    visual = stream_is_visual()
    tokens = line_ref.shape[1]
    heads_local, table_width = table_ref.shape
    line = jnp.where(visual, line_ref[1:2, :], line_ref[0:1, :])
    across = jnp.where(visual, box_ref[1, 0:1, :], box_ref[0, 0:1, :]) + LINES
    down = jnp.where(visual, box_ref[1, 1:2, :], box_ref[0, 1:2, :]) + (LINES + BOXES)
    level = iota((LEVELS, tokens), 0)
    back_ref[...] = one_hot(by_level(LEVELS - 1 - level, line, across, down))
    closed = jnp.logical_and(visual, iota((LEVELS, tokens), 1) >= count_ref[0])
    mask = jnp.where(closed, FLOOR_SCORE, 0.0)
    flags = by_level(level, line, across, down).astype(F32)
    oh_ref[...] = jnp.transpose(jnp.where(level == MASK_LANE, mask, flags)).astype(BF16)
    row = iota((LEVELS, LEVELS), 0)
    lane = iota((LEVELS, LEVELS), 1)
    inside = same_group(row, lane)
    offsets = iota((table_width, LEVELS), 1) - LEVELS // 2
    table = table_ref[...]
    spread = [
        picked(table, bucket_map(offsets, half, offset, table_width))
        for unused_start, unused_stop, half, offset in GROUPS
    ]
    for head in range(heads_local):
        rows = [jnp.broadcast_to(s[head : head + 1, :], (LEVELS, LEVELS)) for s in spread]
        chosen = jnp.where(row < LINES, rows[0], jnp.where(row < LINES + BOXES, rows[1], rows[2]))
        turned = pltpu.roll(chosen, LEVELS // 2, 1, stride=1, stride_axis=0)
        pairs = jnp.where(inside, turned, 0.0)
        high = jnp.where((lane == MASK_LANE) & (row < LINES), 1.0, pairs)
        tab_ref[:, head * LEVELS : (head + 1) * LEVELS] = high.astype(BF16)


def attend_chunk(
    chunk, count_ref, q_ref, k_ref, vt_ref, tab_ref, oh_ref, heads_ref, prob_ref, left_ref
):
    visual = stream_is_visual()
    tokens, local_width = q_ref.shape
    heads_local = local_width // HD
    block = heads_ref.shape[1]
    span = slice(chunk * block, (chunk + 1) * block)
    place = iota((1, block), 1) + chunk * block
    allowed = jnp.logical_or(jnp.logical_not(visual), place < count_ref[0]).astype(F32)
    one = oh_ref[...]
    left_ref[...] = dot(oh_ref[span, :], tab_ref[...]).astype(BF16)
    ones = jnp.ones((16, tokens), F32).astype(BF16)

    def group(first, heads):
        span_lanes = lanes(first, heads)
        queries = q_ref[span, span_lanes] * jnp.asarray(SCALE, BF16)
        keys = k_ref[:, span_lanes]
        values = vt_ref[span_lanes, :]
        biases = left_ref[:, lanes(2 * first, 2 * heads)]

        def scores(n):
            own = slice(n * HD, (n + 1) * HD)
            right = jnp.concatenate(
                [biases[:, n * LEVELS : (n + 1) * LEVELS], queries[:, own]], axis=1
            )
            return dot(jnp.concatenate([one, keys[:, own]], axis=1), right, NT)

        results = []
        following = scores(0)
        for n in range(heads):
            own = slice(n * HD, (n + 1) * HD)
            current = following
            if n + 1 < heads:
                following = scores(n + 1)
            shifted = jnp.exp(current - jnp.max(current, axis=0, keepdims=True))
            mixed = dot(jnp.concatenate([values[own], ones], axis=0), shifted.astype(BF16))
            share = 1.0 / mixed[HD : HD + 1]
            prob_ref[first + n] = (shifted * share).astype(BF16)
            results.append((mixed[:HD] * (share * allowed)).astype(BF16))
        heads_ref[span_lanes, :] = jnp.concatenate(results, axis=0)

    head_groups(heads_local, group, loop=chunk > 0)


def attend_first_kernel(pieces, count_ref, text_ref, visual_ref, small_ref, w_ref, tab_ref, oh_ref, *refs):
    piece_refs, refs = refs[:pieces], refs[pieces:]
    stats_ref, x_ref, q_ref, k_ref, v_ref, kt_ref, vt_ref, heads_ref, prob_ref, left_ref = refs
    visual = stream_is_visual()
    tokens, width = text_ref.shape
    total, spread, number = joined_stats([ref[...] for ref in piece_refs])
    mean = total / number
    scale = lax.rsqrt(spread / number + EPSILON)
    gain, shift = small_ref[6:7, :], small_ref[7:8, :]
    stats_ref[...] = jnp.concatenate(
        [mean, scale, gain, number, jnp.zeros((4, width), F32)], axis=0
    )

    @pl.when(visual)
    def _():
        keep = (iota((tokens, 1), 0) < count_ref[0]).astype(F32)
        centred = (visual_ref[...].astype(F32) - mean) * keep
        x_ref[...] = ((centred * scale * gain + shift) * keep).astype(BF16)

    @pl.when(jnp.logical_not(visual))
    def _():
        x_ref[...] = text_ref[...]

    x = x_ref[...]
    q_ref[...] = dot(x, w_ref[0]).astype(BF16)
    k_ref[...] = dot(x, w_ref[1]).astype(BF16)
    v_ref[...] = dot(x, w_ref[2]).astype(BF16)
    kt_ref[...] = dot(w_ref[1], x, TT).astype(BF16)
    vt_ref[...] = dot(w_ref[2], x, TT).astype(BF16)
    attend_chunk(
        0, count_ref, q_ref, k_ref, vt_ref, tab_ref, oh_ref, heads_ref, prob_ref, left_ref
    )


ERF_P = 0.3275911 * 0.7071067811865476
ERF_A = (0.254829592, -0.284496736, 1.421413741, -1.453152027, 1.061405429)


def gelu_parts(pre):
    t = 1.0 / (1.0 + ERF_P * jnp.abs(pre))
    bell = jnp.exp(-0.5 * pre * pre)
    poly = 0.5 * ERF_A[4]
    for coefficient in ERF_A[3::-1]:
        poly = poly * t + 0.5 * coefficient
    tail = poly * t * bell
    cdf = jnp.where(pre >= 0.0, 1.0 - tail, tail)
    return pre * cdf, cdf + pre * (bell * 0.3989422804014327)


def normed_rows(hidden):
    average = jnp.mean(hidden, axis=-1, keepdims=True)
    centred = hidden - average
    scale = lax.rsqrt(jnp.mean(centred * centred, axis=-1, keepdims=True) + EPSILON)
    return centred * scale, scale


def normed_back(upstream, hat, scale, gain):
    scaled = upstream * gain
    return scale * (
        scaled
        - jnp.mean(scaled, axis=-1, keepdims=True)
        - hat * jnp.mean(scaled * hat, axis=-1, keepdims=True)
    )


def ffn_kernel(chunk, relative, pieces, *refs):
    (text_ref, cot_ref, wo, w1, w2, small_ref, b1_ref), refs = refs[:7], refs[7:]
    piece_refs, refs = refs[:pieces], refs[pieces:]
    out_ref, share_ref, act_ref, dpre_ref, low_ref, branch_ref, mix_ref = refs[:7]
    dheads_ref, dheadst_ref, vec_ref, slope = refs[7:]
    local_width, block = piece_refs[0].shape
    width = text_ref.shape[1]
    hidden_width = w1.shape[1]
    head_rank = lax.axis_index("head")
    out_bias, gain1, shift1, b2, gain2, shift2 = (small_ref[i : i + 1, :] for i in range(6))
    parts = hidden_width // width
    share = share_ref.shape[0]
    rows = slice(chunk * block, (chunk + 1) * block)
    own_rows = pl.ds(pl.multiple_of(head_rank * local_width, 64), local_width)

    sources = [
        (ref[...], head_rank ^ index if relative else index)
        for index, ref in enumerate(piece_refs)
    ]
    mixed = text_ref[rows, :].astype(F32) + out_bias
    for piece, source in sources:
        wo_rows = pl.ds(pl.multiple_of(source * local_width, 64), local_width)
        mixed = mixed + dot(piece, wo[wo_rows, :], TN)
    hat1, scale1 = normed_rows(mixed)
    after = hat1 * gain1 + shift1
    after_low = after.astype(BF16)
    low_ref[...] = after_low
    branch = jnp.zeros((block, width), F32)
    for c in range(parts):
        cols = slice(c * width, (c + 1) * width)
        act, slope[:, cols] = gelu_parts(dot(after_low, w1[:, cols]) + b1_ref[c : c + 1, :])
        act = act.astype(BF16)
        act_ref[:, cols] = act
        branch = branch + dot(act, w2[cols, :])
    hat2, scale2 = normed_rows(after + (branch + b2))
    out_ref[...] = (hat2 * gain2 + shift2).astype(BF16)
    upstream = cot_ref[rows, :].astype(F32)
    dh_two = normed_back(upstream, hat2, scale2, gain2)
    dbranch = dh_two.astype(BF16)
    branch_ref[...] = dbranch
    vec = [None] * 3
    dy = dh_two
    for c in range(parts):
        cols = slice(c * width, (c + 1) * width)
        dpre = (dot(dbranch, w2[cols, :], NT) * slope[:, cols]).astype(BF16)
        dpre_ref[:, cols] = dpre
        vec.append(dpre.astype(F32))
        dy = dy + dot(dpre, w1[:, cols], NT)
    dh_one = normed_back(dy, hat1, scale1, gain1)
    vec[:3] = [dh_one, dy * hat1, dy]
    vec += [dbranch.astype(F32), upstream * hat2, upstream]
    sums = [jnp.sum(v, axis=0, keepdims=True) for v in vec]
    vec_ref[...] = jnp.concatenate(
        sums + [jnp.zeros((VEC_ROWS - len(sums), width), F32)], axis=0
    )
    share_ref[...] = jnp.zeros_like(share_ref)
    per_block = block // share
    for part in range(per_block):

        @pl.when(head_rank == chunk * per_block + part)
        def _():
            share_ref[...] = dh_one[part * share : (part + 1) * share]

    dmix = dh_one.astype(BF16)
    mix_ref[...] = dmix
    dheads_ref[...] = dot(dmix, wo[own_rows, :], NT).astype(BF16)
    dheadst_ref[...] = dot(wo[own_rows, :], dmix, NT).astype(BF16)


def owner_of(half, step):
    place = lax.axis_index("dp")
    core = place & 1
    return (((place >> 1) ^ step) << 1) | (core if half == 0 else 1 - core)


def own_order():
    return [owner_of(half, step) for half in range(2) for step in range(4)]


def weight_grad_in_kernel(*refs):
    head_rank = lax.axis_index("head")
    low_refs, dpre_refs, vec_refs = (refs[i * CHUNKS : (i + 1) * CHUNKS] for i in range(3))
    mine_ref, sib_ref = refs[3 * CHUNKS :]
    width = low_refs[0].shape[1]
    parts = dpre_refs[0].shape[1] // width
    width_own = width // 8
    part_in = width_own // 4
    lane = iota((part_in, width), 1)
    row = iota((part_in, width), 0)
    pick = jnp.concatenate(
        [
            (lane == owner * width_own + head_rank * part_in + row).astype(F32)
            for owner in own_order()
        ],
        axis=0,
    ).astype(BF16)
    low_t = [dot(pick, low[...], NT).astype(BF16) for low in low_refs]
    grads = []
    for p in range(parts):
        cols = slice(p * width, (p + 1) * width)
        grads.append(
            functools.reduce(
                jnp.add, (dot(low_t[c], dpre_refs[c][:, cols]) for c in range(CHUNKS))
            )
        )
    vec = functools.reduce(jnp.add, (v[...] for v in vec_refs))
    for n in range(8):
        rows = slice(n * part_in, (n + 1) * part_in)
        block = jnp.concatenate([grad[rows] for grad in grads] + [vec], axis=0)
        target = mine_ref if n < 4 else sib_ref
        target[n % 4] = block.astype(target.dtype)


def weight_grad_out_kernel(*refs):
    head_rank = lax.axis_index("head")
    names = ("out", "act", "branch", "mix", "heads")
    groups = {name: refs[i * CHUNKS : (i + 1) * CHUNKS] for i, name in enumerate(names)}
    layer_ref, mine_ref, sib_ref, whole = refs[len(names) * CHUNKS :]
    block, width = groups["out"][0].shape
    hidden_width = groups["act"][0].shape[1]
    owners = own_order()
    width_own = width // 8
    window = hidden_width // 8
    part_out = window // 4
    half_own = width_own // 2
    for c in range(CHUNKS):
        layer_ref[c * block : (c + 1) * block, :] = groups["out"][c][...]
    whole[...] = functools.reduce(
        jnp.add, (dot(groups["mix"][c][...], groups["heads"][c][...], TT) for c in range(CHUNKS))
    )
    pick = one_hot(
        iota((part_out, window), 1) == head_rank * part_out + iota((part_out, window), 0)
    )
    grad = jnp.zeros((8 * part_out, width), F32)
    for c in range(CHUNKS):
        stacked = []
        for owner in owners:
            cols = pl.ds(pl.multiple_of(owner * window, 128), window)
            stacked.append(dot(pick, groups["act"][c][:, cols], NT).astype(BF16))
        grad = grad + dot(jnp.concatenate(stacked, axis=0), groups["branch"][c][...])
    for n, owner in enumerate(owners):
        start = pl.multiple_of(owner * width_own, 8)
        packed = jnp.concatenate(
            [whole[pl.ds(start, half_own), :], whole[pl.ds(start + half_own, half_own), :]],
            axis=1,
        )
        target = mine_ref if n < 4 else sib_ref
        target[n % 4] = jnp.concatenate(
            [grad[n * part_out : (n + 1) * part_out], packed], axis=0
        ).astype(target.dtype)


X_FIRST = ((0, 2), (1, 3))
Y_FIRST = ((0, 1), (2, 3))


def join_cores_kernel(plans, *refs):
    mine_ref, other_ref, outs = refs[0], refs[1], refs[2:]
    start = 0
    for (keep, send), keep_ref, send_ref in zip(plans, outs[::2], outs[1::2]):
        rows = slice(start, start + keep_ref.shape[1])
        start = rows.stop
        for places, out in ((keep, keep_ref), (send, send_ref)):
            for n, place in enumerate(places):
                total = mine_ref[place, rows, :] + other_ref[place, rows, :].astype(F32)
                out[n] = total.astype(out.dtype)


def join_chips_kernel(*refs):
    count = len(refs) // 4
    ins, outs = refs[: 2 * count], refs[2 * count :]
    for n in range(count):
        keep, other = ins[2 * n : 2 * n + 2]
        for m, out in enumerate(outs[2 * n : 2 * n + 2]):
            out[...] = (keep[m] + other[m].astype(F32)).astype(out.dtype)


def attend_back_heads(count_ref, refs, dqkv_ref, pair_ref):
    q_ref, k_ref, v_ref, kt_ref, oh_ref, back_ref = refs[:6]
    groups = [refs[6 + i * CHUNKS : 6 + (i + 1) * CHUNKS] for i in range(4)]
    head_refs, dhead_refs, dheadt_refs, prob_refs = groups
    visual = stream_is_visual()
    tokens = q_ref.shape[0]
    block = tokens // CHUNKS
    count = count_ref[0]
    one = oh_ref[...]
    back = back_ref[...]
    inside = same_group(LEVELS - 1 - iota((LEVELS, LEVELS), 0), iota((LEVELS, LEVELS), 1))
    extra = one_hot(iota((tokens, 16), 1) < 2)
    sublane = iota((16, block), 0)
    free = jnp.logical_not(visual)
    rows_open = []
    lanes_open = []
    for c in range(CHUNKS):
        rows_open.append(
            jnp.logical_or(free, iota((block, 1), 0) + c * block < count).astype(BF16)
        )
        lanes_open.append(
            jnp.logical_or(free, iota((1, block), 1) + c * block < count).astype(BF16)
        )

    def group(first, heads):
        span_lanes = lanes(first, heads)
        turned = [[], [], []]
        for n in range(heads):
            own = slice(n * HD, (n + 1) * HD)
            left = jnp.concatenate([v_ref[:, span_lanes][:, own], extra], axis=1)
            below = jnp.concatenate([back, kt_ref[span_lanes, :][own]], axis=0)
            dquery_t = []
            dkey = jnp.zeros((tokens, HD), F32)
            dvalue = jnp.zeros((tokens, HD), F32)
            pairs = jnp.zeros((LEVELS, LEVELS), F32)
            for c in range(CHUNKS):
                span = slice(c * block, (c + 1) * block)
                dout = dhead_refs[c][:, span_lanes][:, own] * rows_open[c]
                dout_t = dheadt_refs[c][span_lanes, :][own] * lanes_open[c]
                inner = -jnp.sum(
                    dout_t.astype(F32) * head_refs[c][span_lanes, :][own].astype(F32),
                    axis=0,
                    keepdims=True,
                )
                high = inner.astype(BF16).astype(F32)
                tail = jnp.where(sublane == 0, high, jnp.where(sublane == 1, inner - high, 0.0))
                centred = dot(left, jnp.concatenate([dout_t, tail.astype(BF16)], axis=0))
                prob = prob_refs[c][first + n]
                dscore = (prob.astype(F32) * centred).astype(BF16)
                both = dot(below, dscore)
                level = both[:LEVELS]
                level_high = level.astype(BF16)
                level_low = (level - level_high.astype(F32)).astype(BF16)
                one_part = one[span, :]
                pairs = pairs + dot(level_high, one_part) + dot(level_low, one_part)
                dquery_t.append(both[LEVELS:] * SCALE)
                dkey = dkey + dot(dscore, q_ref[span, span_lanes][:, own])
                dvalue = dvalue + dot(prob, dout)
            pair_ref[first + n] = jnp.where(inside, pairs, 0.0)
            turned[0].append(jnp.concatenate(dquery_t, axis=1))
            turned[1].append(dkey * SCALE)
            turned[2].append(dvalue)
        for m in range(3):
            joined = jnp.concatenate(turned[m], axis=0 if m == 0 else 1)
            if m == 0:
                joined = jnp.transpose(joined)
            dqkv_ref[m, :, span_lanes] = joined.astype(BF16)

    head_groups(q_ref.shape[1] // HD, group)


def back_kernel(relative, count_ref, w_ref, visual_ref, stats_ref, x_ref, *refs):
    steps = lax.axis_size("head")
    inner, refs = refs[: 6 + 4 * CHUNKS], refs[6 + 4 * CHUNKS :]
    sums_ref, refs = refs[0], refs[1:]
    part_refs, refs = refs[: 1 + relative], refs[1 + relative :]
    grad_refs, (dqkv_ref, pair_ref), whole = refs[:2], refs[2:4], refs[4:]
    attend_back_heads(count_ref, inner, dqkv_ref, pair_ref)
    visual = stream_is_visual()
    tokens = visual_ref.shape[0]
    share = tokens // steps
    mean, scale = stats_ref[0:1, :], stats_ref[1:2, :]
    shift_sum = jnp.zeros(mean.shape, F32)
    gain_sum = jnp.zeros(mean.shape, F32)
    for k in range(steps):
        if relative:
            start = pl.multiple_of((lax.axis_index("head") ^ k) * share, share)
            target = part_refs[k % 2].at[k // 2]
        else:
            start = k * share
            target = part_refs[0].at[k]
        rows = pl.ds(start, share)
        part = functools.reduce(
            jnp.add, (dot(dqkv_ref[m, rows, :], w_ref[m], NT) for m in range(3))
        )
        target[...] = part.astype(target.dtype)
        keep = jnp.logical_and(visual, iota((share, 1), 0) + start < count_ref[0]).astype(F32)
        kept = part * keep
        shift_sum = shift_sum + jnp.sum(kept, axis=0, keepdims=True)
        hat = (visual_ref[rows, :].astype(F32) - mean) * scale
        gain_sum = gain_sum + jnp.sum(kept * hat, axis=0, keepdims=True)
    sums_ref[...] = jnp.concatenate(
        [shift_sum, gain_sum, jnp.zeros((6, mean.shape[1]), F32)], axis=0
    )
    qkv_grads(relative, x_ref, dqkv_ref, pair_ref, *grad_refs, *whole)


def join_pair_kernel(keep_ref, other_ref, own_ref, send_ref):
    own_ref[...] = keep_ref[0] + other_ref[0].astype(F32)
    send_ref[...] = (keep_ref[1] + other_ref[1].astype(F32)).astype(BF16)


def table_sums(pair_refs):
    table_width = NB_REL + 2 * NB_BOX
    sums = [[], [], []]
    for ref in pair_refs:
        for head in range(ref.shape[0]):
            turned = pltpu.roll(ref[head], LEVELS // 2 + 1, 1, stride=1, stride_axis=0)
            for n, (start, stop, unused_half, unused_offset) in enumerate(GROUPS):
                rows = turned[LEVELS - stop : LEVELS - start]
                sums[n].append(jnp.sum(rows, axis=0, keepdims=True))
    table = jnp.zeros((8, table_width), F32)
    offsets = LEVELS // 2 - iota((table_width, LEVELS), 1)
    for n, (unused_start, unused_stop, half, offset) in enumerate(GROUPS):
        missing = 8 - len(sums[n])
        stacked = jnp.concatenate(sums[n] + [jnp.zeros((missing, LEVELS), F32)], axis=0)
        table = table + picked(stacked, bucket_map(offsets, half, offset, table_width), NT)
    return table


def qkv_grads(fused, x_ref, dqkv_ref, pair_ref, *outs):
    tokens, width = x_ref.shape
    local_width = dqkv_ref.shape[2]
    table = table_sums((pair_ref,))
    x = x_ref[...]

    if not fused:
        grad_ref, table_ref = outs
        table_ref[...] = table
        for m in range(3):
            grad_ref[m] = dot(x, dqkv_ref[m], TN).astype(BF16)
        return
    mine_ref, sib_ref, whole = outs
    width_own = width // 8
    padded = jnp.concatenate(
        [
            jnp.concatenate([table, jnp.zeros((8, local_width - table.shape[1]), F32)], axis=1),
            jnp.zeros((8, local_width), F32),
        ],
        axis=0,
    )
    for m in range(3):
        whole[m] = dot(x, dqkv_ref[m], TN)
    for half, target in ((1, sib_ref), (0, mine_ref)):
        for k in range(4):
            rows = pl.ds(pl.multiple_of(owner_of(half, k) * width_own, 8), width_own)
            tall = jnp.concatenate([whole[m, rows, :] for m in range(3)] + [padded], axis=0)
            middle = tall.shape[0] // 2
            target[k] = jnp.concatenate([tall[:middle], tall[middle:]], axis=1).astype(
                target.dtype
            )


def finish_grads_kernel(hidden_width, *refs):
    block_refs, outs = refs[:8], refs[8:]
    grad_in, grad_out, grad_ow, bias_in, grad_qkv, grad_table = outs[:6]
    sums = [
        own[...] + other[...].astype(F32) for own, other in zip(block_refs[::2], block_refs[1::2])
    ]
    total = jnp.concatenate(sums, axis=0)
    width = total.shape[1]
    part_in = grad_in.shape[0]
    part_out = grad_out.shape[0]
    half_own = grad_ow.shape[0] // 2
    local_width = grad_ow.shape[1]
    parts = hidden_width // width
    place = lax.axis_index("dp") * lax.axis_size("head") + lax.axis_index("head")
    grad_in[...] = jnp.concatenate(
        [total[p * part_in : (p + 1) * part_in] for p in range(parts)], axis=1
    )
    base = parts * part_in
    vec = total[base : base + VEC_ROWS]
    base += VEC_ROWS
    grad_out[...] = total[base : base + part_out]
    base += part_out
    packed = total[base : base + half_own]
    grad_ow[...] = jnp.concatenate([packed[:, :local_width], packed[:, local_width:]], axis=0)
    base += half_own
    lane = iota((width, 128), 0)
    column = iota((width, 128), 1)
    own = picked(vec, one_hot((lane == place * part_in + column) & (column < part_in)))
    for row, out in zip((0, 1, 2, 7, 8, 9), outs[6:]):
        out[...] = own[row : row + 1, :part_in]
    first = place * part_out
    wide = picked(
        vec, one_hot((lane == lax.rem(first, width) + column) & (column < part_out))
    )
    row = iota((VEC_ROWS, 128), 0)
    chosen = jnp.where(row == 3 + lax.div(first, width), wide, 0.0)
    bias_in[...] = jnp.sum(chosen, axis=0, keepdims=True)[:, :part_out]
    grads = jnp.concatenate([total[base:, :local_width], total[base:, local_width:]], axis=0)
    width_own = grad_qkv.shape[1]
    for m in range(3):
        grad_qkv[m] = grads[m * width_own : (m + 1) * width_own]
    table = grads[3 * width_own : 3 * width_own + 8]
    buckets = grad_table.shape[1]
    lane = iota((local_width, 128), 0)
    column = iota((local_width, 128), 1)
    start = lax.axis_index("dp") * buckets
    cut = picked(table, one_hot((lane == start + column) & (column < buckets)))
    grad_table[...] = cut[: grad_table.shape[0], :buckets]


def finish_inputs_kernel(steps, relative, sums, count_ref, visual_ref, stats_ref, *refs):
    share_refs, refs = refs[:CHUNKS], refs[CHUNKS:]
    part_refs, refs = refs[: 1 + relative], refs[1 + relative :]
    sum_refs, refs = refs[:sums], refs[sums:]
    text_ref, grad_ref, gain_ref, shift_ref = refs
    head_rank = lax.axis_index("head")
    share = text_ref.shape[0]
    half = steps // 2
    if relative:
        same, other = (ref[...].astype(F32) for ref in part_refs)
        text = jnp.where(stream_is_visual(), other, same)
        visual = jnp.where(stream_is_visual(), same, other)
    else:
        text, visual = (
            functools.reduce(
                jnp.add, (part_refs[0][k].astype(F32) for k in range(start, start + half))
            )
            for start in (0, half)
        )
    text_ref[...] = functools.reduce(jnp.add, (ref[...] for ref in share_refs)) + text
    total = functools.reduce(jnp.add, (ref[...] for ref in sum_refs))
    mean, scale, gain, number = (stats_ref[i : i + 1, :] for i in range(4))
    start = pl.multiple_of(head_rank * share, share)
    keep = (iota((share, 1), 0) + start < count_ref[0]).astype(F32)
    hat = (visual_ref[pl.ds(start, share), :].astype(F32) - mean) * keep * scale
    dnormed = visual * keep
    shift_gradient, gain_gradient = total[0:1], total[1:2]
    shift_ref[...] = shift_gradient.reshape(shift_ref.shape)
    gain_ref[...] = gain_gradient.reshape(gain_ref.shape)
    grad_ref[...] = (
        keep
        * scale
        * gain
        * (dnormed - shift_gradient / number - hat * gain_gradient / number)
    )


def swap(value, axis, mask):
    size = lax.axis_size(axis)
    return lax.ppermute(value, axis, [(i, i ^ mask) for i in range(size)])


def after(value, *earlier):
    return lax.optimization_barrier((value, *earlier))[0]


def gather_heads(chunks):
    first = [chunks[0]] + [swap(chunks[0], "head", k) for k in (1, 2, 3)]
    second = after(chunks[1], first[2])
    return [first, [chunks[1]] + [swap(second, "head", k) for k in (1, 2, 3)]]


def across_chips(mine, other, plans, sizes, name):
    axes = {X_FIRST: (2, 4), Y_FIRST: (4, 2)}
    width = mine.shape[2]
    outs = []
    for size in sizes:
        outs += [((2, size, width), F32), ((2, size, width), BF16)]
    joined = call(functools.partial(join_cores_kernel, plans), name, 1, outs, [mine, other])
    return [
        (keep, swap(send, "dp", axes[plan][0]), axes[plan][1])
        for plan, keep, send in zip(plans, joined[::2], joined[1::2])
    ]


def second_exchange(stages, name, earlier=()):
    outs = []
    args = []
    for keep, other, mask in stages:
        outs += [(keep.shape[1:], F32), (keep.shape[1:], BF16)]
        args += [keep, other]
    args[1] = after(args[1], *earlier)
    joined = call(join_chips_kernel, name, 1, outs, args)
    blocks = []
    for n, stage in enumerate(stages):
        blocks += [joined[2 * n], swap(joined[2 * n + 1], "dp", stage[2])]
    return blocks, joined


def per_device(
    text_in,
    visual_in,
    visual_count,
    line_index,
    box_index,
    qkv_weight,
    bias_table,
    out_weight,
    out_bias,
    norm1_gain,
    norm1_shift,
    ffn_weight_in,
    ffn_bias_in,
    ffn_weight_out,
    ffn_bias_out,
    norm2_gain,
    norm2_shift,
    batch_gain,
    batch_shift,
    cotangent,
):
    tokens, width = text_in.shape
    local_width = qkv_weight.shape[2]
    heads_local = local_width // HD
    head_count = lax.axis_size("head")
    dp_count = lax.axis_size("dp")
    head_rank = lax.axis_index("head")
    dp_rank = lax.axis_index("dp")
    fused = head_count == 4 and dp_count == 8
    share = tokens // head_count
    block = tokens // CHUNKS
    hidden_width = ffn_weight_in.shape[1]
    table_width = bias_table.shape[1]
    part_in = width // (dp_count * head_count)
    part_out = hidden_width // (dp_count * head_count)
    weight = jnp.transpose(qkv_weight, (1, 0, 2))
    row_vectors = [
        value.reshape(1, width)
        for value in (
            out_bias,
            norm1_gain,
            norm1_shift,
            ffn_bias_out,
            norm2_gain,
            norm2_shift,
            batch_gain,
            batch_shift,
        )
    ]

    packed_shape = ((8, width), F32)
    (packed,) = call(
        stats_kernel, "stats", 2, [packed_shape], [visual_in], visual_count
    )
    if fused:
        (packed,) = call(
            join_stats_kernel, "join_stats", 1, [packed_shape], [packed, swap(packed, "dp", 1)]
        )
        packed = [packed] + [swap(packed, "dp", k) for k in (2, 4, 6)]
    else:
        gathered = lax.all_gather(packed, "dp")
        packed = [gathered[i] for i in range(dp_count)]
    one, back, tab, small, bias_in = call(
        prep_kernel,
        "prep",
        2,
        [
            ((tokens, LEVELS), BF16),
            ((LEVELS, tokens), BF16),
            ((LEVELS, heads_local * LEVELS), BF16),
            ((8, width), F32),
            ((8, width), F32),
        ],
        [line_index, box_index, bias_table, ffn_bias_in.reshape(1, hidden_width)] + row_vectors,
        visual_count,
    )

    rows = ((tokens, local_width), BF16)
    turned = ((local_width, tokens), BF16)
    left = [pltpu.VMEM((block, heads_local * LEVELS), BF16)]
    chunk_outs = [((local_width, block), BF16), ((heads_local, tokens, block), BF16)]
    stats, x, q, k, v, kt, vt, heads_one, prob_one = call(
        functools.partial(attend_first_kernel, len(packed)),
        "attend_first",
        6,
        [packed_shape, ((tokens, width), BF16), rows, rows, rows, turned, turned] + chunk_outs,
        [text_in, visual_in, small, weight, tab, one] + packed,
        visual_count,
        scratch=left,
        final=(1,),
    )
    heads_two, prob_two = call(
        functools.partial(attend_chunk, 1),
        "attend_second",
        3,
        chunk_outs,
        [q, k, vt, tab, one],
        visual_count,
        scratch=left,
    )
    heads = (heads_one, heads_two)
    if fused:
        pieces = gather_heads(heads)
    else:
        pieces = []
        for piece in heads:
            gathered = lax.all_gather(piece, "head")
            pieces.append([gathered[i] for i in range(head_count)])

    results = []
    for c in range(CHUNKS):
        text = after(text_in, results[-1][-1]) if results else text_in
        results.append(
            call(
                functools.partial(ffn_kernel, c, fused, len(pieces[c])),
                f"ffn_{c}",
                9,
                [
                    ((block, width), BF16),
                    ((share, width), F32),
                    ((block, hidden_width), BF16),
                    ((block, hidden_width), BF16),
                    ((block, width), BF16),
                    ((block, width), BF16),
                    ((block, width), BF16),
                    ((block, local_width), BF16),
                    ((local_width, block), BF16),
                    ((VEC_ROWS, width), F32),
                ],
                [text, cotangent, out_weight, ffn_weight_in, ffn_weight_out, small, bias_in]
                + list(pieces[c]),
                scratch=[pltpu.VMEM((block, hidden_width), F32)],
            )
        )
    out, dh_share, act, dpre, low, branch, mix, dheads, dheads_t, vec = zip(*results)
    if fused:
        in_rows = hidden_width // width * part_in + VEC_ROWS
        out_rows = part_out + width // dp_count // 2
        mine, sib = call(
            weight_grad_in_kernel,
            "weight_grad_in",
            2,
            [((4, in_rows, width), F32), ((4, in_rows, width), BF16)],
            [*low, *dpre, *vec],
        )
        other = swap(sib, "dp", 1)
        layer_out, mine_out, sib_out = call(
            weight_grad_out_kernel,
            "weight_grad_out",
            3,
            [
                ((tokens, width), BF16),
                ((4, out_rows, width), F32),
                ((4, out_rows, width), BF16),
            ],
            [after(out[0], sib), *out[1:], *act, *branch, *mix, *heads],
            scratch=[pltpu.VMEM((width, local_width), F32)],
            final=(0,),
        )
        other_out = swap(after(sib_out, other), "dp", 1)
        ffn_stages = across_chips(mine, other, [X_FIRST], [in_rows], "join_cores_in")
        ffn_stages += across_chips(mine_out, other_out, [Y_FIRST], [out_rows], "join_cores_out")
    inner = [q, k, v, kt, one, back, *heads, *dheads, *dheads_t, prob_one, prob_two]
    packed_qkv = 3 * (width // dp_count) // 2 + 8
    scratch = [
        pltpu.VMEM((3, tokens, local_width), BF16),
        pltpu.VMEM((heads_local, LEVELS, LEVELS), F32),
    ]
    if fused:
        inner[0] = after(q, *(stage[0] for stage in ffn_stages))
        part_outs = [((2, share, width), F32), ((2, share, width), BF16)]
        grad_outs = [((4, packed_qkv, width), F32), ((4, packed_qkv, width), BF16)]
        scratch.append(pltpu.VMEM((3, width, local_width), F32))
    else:
        part_outs = [((head_count, share, width), BF16)]
        grad_outs = [((3, width, local_width), BF16), ((8, table_width), F32)]
    sums, *rest = call(
        functools.partial(back_kernel, fused),
        "back",
        12,
        [packed_shape] + part_outs + grad_outs,
        [weight, visual_in, stats, x] + inner,
        visual_count,
        scratch=scratch,
    )
    parts, grads = rest[: len(part_outs)], rest[len(part_outs) :]
    if fused:
        mine, sib = grads
        keep, send = parts
        arrived = [stage[1] for stage in ffn_stages]
        send, sib, sums, *arrived = lax.optimization_barrier((send, sib, sums, *arrived))
        ffn_stages = [(stage[0], other, stage[2]) for stage, other in zip(ffn_stages, arrived)]
        near = swap(send, "head", 1)
        sums = sums + swap(sums, "dp", 1)
        ffn_blocks, ffn_joined = second_exchange(ffn_stages, "join_chips_ffn", [sums])
        sums = sums + swap(sums, "dp", 2)
        first_rows = packed_qkv // 2 // 8 * 8
        stages = across_chips(
            mine,
            after(swap(sib, "dp", 1), ffn_joined[0]),
            [X_FIRST, Y_FIRST],
            [first_rows, packed_qkv - first_rows],
            "join_cores_qkv",
        )
        sums = sums + swap(sums, "dp", 4)
        qkv_blocks, unused_joined = second_exchange(stages, "join_chips_qkv", ffn_blocks[::2])
        same, send = call(
            join_pair_kernel,
            "join_pair",
            1,
            [((share, width), F32), ((share, width), BF16)],
            [keep, near],
        )
        received = [same, swap(send, "head", 2)]
        sums = after(sums, same)
        sums = sums + swap(sums, "head", 1)
        sums = after(sums, *ffn_blocks)
        sums = [sums, swap(sums, "head", 2)]
        blocks = ffn_blocks + qkv_blocks
        one_row = ((1, part_in), F32)
        grad_in, grad_out, grad_ow, grad_bias_in, grad_qkv, grad_table, *own = call(
            functools.partial(finish_grads_kernel, hidden_width),
            "finish_grads",
            2,
            [
                ((part_in, hidden_width), F32),
                ((part_out, width), F32),
                ((width // dp_count, local_width), F32),
                ((1, part_out), F32),
                ((3, width // dp_count, local_width), F32),
                ((heads_local, table_width // dp_count), F32),
            ]
            + [one_row] * 6,
            blocks,
            final=range(12),
        )
        grad_bias_in = grad_bias_in.reshape(part_out)
        grad_qkv = jnp.transpose(grad_qkv, (1, 0, 2))
        grad_ow = jnp.transpose(grad_ow)
        own = [value.reshape(part_in) for value in own]
    else:
        layer_out = jnp.concatenate(out, axis=0)
        act, dpre, low, branch, mix = (
            jnp.concatenate(value, axis=0) for value in (act, dpre, low, branch, mix)
        )

        def scatter(value, dimension):
            return lax.psum_scatter(
                value.astype(BF16), "dp", scatter_dimension=dimension, tiled=True
            ).astype(F32)

        def own_columns(value, part):
            split = value.reshape(tokens, dp_count, head_count, part)
            return lax.dynamic_index_in_dim(split, head_rank, 2, keepdims=False).reshape(
                tokens, dp_count * part
            )

        grad_in = scatter(dot(own_columns(low, part_in), dpre, TN), 0)
        grad_out = scatter(dot(own_columns(act, part_out), branch, TN), 0)
        grad_ow = scatter(dot(jnp.concatenate(heads, axis=1), mix), 1)
        vec = lax.psum((vec[0] + vec[1]).astype(BF16), "dp").astype(F32)
        place = dp_rank * head_count + head_rank
        own = [
            lax.dynamic_slice_in_dim(vec[row], place * part_in, part_in, 0)
            for row in (0, 1, 2, 7, 8, 9)
        ]
        grad_bias_in = lax.dynamic_slice_in_dim(
            vec[3 : 3 + hidden_width // width].reshape(hidden_width), place * part_out, part_out, 0
        )
        sums = [lax.psum(sums, ("dp", "head"))]
        grad, table = grads
        received = [lax.all_to_all(parts[0], "head", 0, 0, tiled=True)]
        grad_qkv = jnp.transpose(scatter(grad, 1), (1, 0, 2))
        grad_table = scatter(table[:heads_local], 1)

    grad_text, grad_visual, gain_gradient, shift_gradient = call(
        functools.partial(finish_inputs_kernel, head_count, fused, len(sums)),
        "finish_inputs",
        2,
        [((share, width), F32)] * 2 + [((width,), F32)] * 2,
        [visual_in, stats, *dh_share, *received, *sums],
        visual_count,
        final=range(4),
    )
    return (
        layer_out,
        grad_text,
        grad_visual,
        grad_qkv,
        grad_table,
        grad_ow,
        own[0],
        own[1],
        own[2],
        grad_in,
        grad_bias_in,
        grad_out,
        own[3],
        own[4],
        own[5],
        gain_gradient,
        shift_gradient,
    )


def solution(mesh):
    in_specs = (
        P("dp", None),
        P("dp", None),
        P("dp"),
        P(None, "dp"),
        P(None, None, "dp"),
        P(None, None, "head"),
        P("head", None),
        P(),
        P(),
        P(),
        P(),
        P(),
        P(),
        P(),
        P(),
        P(),
        P(),
        P(),
        P(),
        P("dp", None),
    )
    out_specs = (
        P("dp", None),
        P(("dp", "head"), None),
        P(("dp", "head"), None),
        P("dp", None, "head"),
        P("head", "dp"),
        P("head", "dp"),
        P(("dp", "head")),
        P(("dp", "head")),
        P(("dp", "head")),
        P(("dp", "head"), None),
        P(("dp", "head")),
        P(("dp", "head"), None),
        P(("dp", "head")),
        P(("dp", "head")),
        P(("dp", "head")),
        P(),
        P(),
    )
    return jax.shard_map(
        per_device, mesh=mesh, in_specs=in_specs, out_specs=out_specs, check_vma=False
    )
```
